128 devices in a mesh: src: 64 (over y, z_hi, x, core), hi: 2 (over z_lo).
Axes of the slice: x: 4, y: 4, z: 4 (z_hi: 2, z_lo: 2; z = z_hi * 2 + z_lo), core: 2. Of those that a mesh axis runs over, the one named last changes fastest.
Arguments:
- traces: bfloat16 [64, 64, 2, 64, 128], P(None, None, 'hi', 'src'), may hold values from -6 to 6
- observed: bfloat16 [64, 2, 64, 64, 128], P(None, 'hi', 'src'), may hold values from -6 to 6
- leaf_maps: bfloat16 [64, 2, 64, 64, 128], P(None, 'hi', 'src'), may hold values from -0.5 to 0.5
- level_maps: bfloat16 [13, 64, 2, 64, 64, 128], P(None, None, 'hi', 'src'), may hold values from -0.5 to 0.5
- final_maps: bfloat16 [2, 64, 64, 64, 128], P('hi', 'src'), may hold values from -0.75 to 0.75
Outputs:
- residual: bfloat16 [64, 2, 64, 64, 128], P(None, 'hi', 'src')
- gradient: bfloat16 [64, 64, 2, 64, 128], P(None, None, 'hi', 'src')
The draws below stay inside these ranges and needn't reach their ends.
All inputs are finite; a program needn't handle non-finite values.
Results may differ from the reference program's by a relative error of at most 0.035.
Values may be sent and summed in bfloat16 or wider, within the bound.
No kernel may reach another device: no remote copies, remote signals or barrier semaphores. Data moves between devices by JAX's collectives and lax.ppermute only.
A program may use at most 128 MiB of HBM per device.

```python
import jax
import jax.numpy as jnp

TRACES = 64
RANK = 64
POINTS = 128
BOXES = 64
LEVELS = 13
N_SRC = 64
N_HI = 2


def steps_of(own_key, shape, shards, smallest, top_value):
    def one(dim, shards_of):
        steps = jax.random.uniform(jax.random.fold_in(jax.random.fold_in(own_key, 6), dim), (shards_of,), jnp.float32, smallest / len(shards), top_value / len(shards))
        return jnp.repeat(jnp.exp(steps), shape[dim] // shards_of).reshape((-1,) + (1,) * (len(shape) - dim - 1))

    gain = one(*shards[0])
    for cut in shards[1:]:
        gain = gain * one(*cut)
    return gain


def bell_draw(key, dims, width, bound, cuts=(), held_as=jnp.bfloat16):
    result = jax.random.normal(key, dims, jnp.float32) * width
    if len(cuts) > 0:
        result = steps_of(key, dims, cuts, -0.22, 0.18) * result
    return jnp.clip(result, min=-bound, max=bound).astype(held_as)


def setup_inputs(seed: int = 0) -> dict:
    streams_of = jax.random.split(jax.random.key(seed), 6)
    return {
        "traces": bell_draw(streams_of[0], (TRACES, BOXES, N_HI, N_SRC, POINTS), 1.0, 6.0, ((2, 2), (3, 64))),
        "observed": bell_draw(streams_of[1], (TRACES, N_HI, N_SRC, BOXES, POINTS), 1.0, 6.0, ((1, 2), (2, 64))),
        "leaf_maps": bell_draw(streams_of[2], (BOXES, N_HI, N_SRC, RANK, POINTS), POINTS ** -0.5, 0.5, ((1, 2), (2, 64))),
        "level_maps": bell_draw(streams_of[3], (LEVELS, BOXES, N_HI, N_SRC, RANK, 2 * RANK), (2 * RANK) ** -0.5, 0.5, ((2, 2), (3, 64))),
        "final_maps": bell_draw(streams_of[4], (N_HI, N_SRC, BOXES, RANK, POINTS), RANK ** -0.5, 0.75, ((0, 2), (1, 64))),
    }


def flip_order(array_in, bit_count):
    tail_shape = array_in.shape[1:]
    opened = array_in.reshape((2,) * bit_count + tail_shape)
    axes_order = tuple(reversed(range(bit_count))) + tuple(range(bit_count, bit_count + len(tail_shape)))
    return jnp.transpose(opened, axes_order).reshape((array_in.shape[0],) + tail_shape)


def merge_forward(coeffs, weights, level_index):
    box_count, vectors, rank_size = coeffs.shape
    outer_count = box_count >> (level_index + 1)
    inner_count = 1 << level_index
    halves = coeffs.reshape(outer_count, 2, inner_count, vectors, rank_size)
    stacked = jnp.concatenate([halves[:, 0], halves[:, 1]], axis=-1).astype(jnp.float32)
    grouped = weights.reshape(outer_count, 2, inner_count, rank_size, 2 * rank_size).astype(jnp.float32)
    merged = jnp.einsum("abhrs,ahvs->abhvr", grouped, stacked)
    return merged.reshape(coeffs.shape).astype(jnp.bfloat16)


def merge_adjoint(adjoint, weights, level_index):
    box_count, vectors, rank_size = adjoint.shape
    outer_count = box_count >> (level_index + 1)
    inner_count = 1 << level_index
    halves = adjoint.reshape(outer_count, 2, inner_count, vectors, rank_size).astype(jnp.float32)
    grouped = weights.reshape(outer_count, 2, inner_count, rank_size, 2 * rank_size).astype(jnp.float32)
    summed = jnp.einsum("abhrs,abhvr->ahvs", grouped, halves)
    parts = jnp.stack([summed[..., :rank_size], summed[..., rank_size:]], axis=1)
    return parts.reshape(adjoint.shape).astype(jnp.bfloat16)


def reference(traces, observed, leaf_maps, level_maps, final_maps):
    sources = BOXES * N_HI * N_SRC
    samples = traces.reshape(TRACES, sources, POINTS).astype(jnp.float32)
    leaf_mats = leaf_maps.reshape(sources, RANK, POINTS).astype(jnp.float32)
    level_mats = level_maps.reshape(LEVELS, sources, RANK, 2 * RANK)
    final_mats = final_maps.reshape(sources, RANK, POINTS).astype(jnp.float32)
    coeffs = jnp.einsum("gaq,vgq->gva", leaf_mats, samples).astype(jnp.bfloat16)
    for level_index in range(LEVELS):
        coeffs = merge_forward(coeffs, level_mats[level_index], level_index)
    ordered = flip_order(coeffs, LEVELS).astype(jnp.float32)
    forward = jnp.einsum("tva,taq->vtq", ordered, final_mats)
    wanted = observed.reshape(TRACES, sources, POINTS).astype(jnp.float32)
    residual = (forward - wanted).astype(jnp.bfloat16)
    adjoint = jnp.einsum("taq,vtq->tva", final_mats, residual.astype(jnp.float32)).astype(jnp.bfloat16)
    adjoint = flip_order(adjoint, LEVELS)
    for level_index in reversed(range(LEVELS)):
        adjoint = merge_adjoint(adjoint, level_mats[level_index], level_index)
    gradient = jnp.einsum("gaq,gva->vgq", leaf_mats, adjoint.astype(jnp.float32)).astype(jnp.bfloat16)
    return (residual.reshape(TRACES, N_HI, N_SRC, BOXES, POINTS),
            gradient.reshape(TRACES, BOXES, N_HI, N_SRC, POINTS))
```

```python
import functools

import jax
import jax.numpy as jnp
from jax import lax
from jax.experimental import pallas as pl
from jax.experimental.pallas import tpu as pltpu
from jax.sharding import PartitionSpec as P

CHUNKS = 4
LANES = 128
BF = jnp.bfloat16
F32 = jnp.float32


def reverse_bits(value, bits):
    return int(format(value, f"0{bits}b")[::-1], 2)


def lane_block(shape, width):
    return lax.broadcasted_iota(jnp.int32, shape, len(shape) - 1) // width


def pick_lanes(product, rows, count, width):
    block = lane_block((rows, LANES), width)
    out = product[:rows]
    for b in range(1, count):
        out = jnp.where(block == b, product[b * rows:(b + 1) * rows], out)
    return out


def split_rows(pair):
    left = lane_block(pair.shape, LANES // 2) == 0
    zero = jnp.zeros(pair.shape, pair.dtype)
    return jnp.concatenate([jnp.where(left, pair, zero), jnp.where(left, zero, pair)], axis=0)


def halves_of(product, rows):
    first, second = product[:rows], product[rows:]
    left = lane_block((rows, LANES), LANES // 2) == 0
    low = jnp.where(left, first, pltpu.roll(second, LANES // 2, 1))
    high = jnp.where(left, pltpu.roll(first, LANES // 2, 1), second)
    return low, high


def is_high(level, src_bits):
    if level < src_bits:
        return (lax.axis_index("src") >> level & 1) == 1
    return (lax.axis_index("hi") >> (level - src_bits) & 1) == 1


def dot(a, b):
    return jnp.dot(a, b, preferred_element_type=F32)


def dot_nt(a, b):
    return lax.dot_general(a, b, (((1,), (1,)), ((), ())), preferred_element_type=F32)


def leaf_kernel(chunk, traces, leaf, out, held, mats, sems, wide):
    vectors, boxes, points = held.shape
    lane_boxes = LANES // vectors
    rank = mats.shape[1]
    copies = [
        pltpu.make_async_copy(traces.at[pl.ds(chunk * vectors, vectors)], held, sems.at[0]),
        pltpu.make_async_copy(leaf, mats, sems.at[1]),
    ]
    for copy in copies:
        copy.start()
    copies[0].wait()
    wide[...] = held[...].astype(F32).reshape(wide.shape)
    copies[1].wait()
    for g in range(boxes // lane_boxes):
        rows = [
            wide[pl.ds(g * lane_boxes + b, vectors, stride=boxes), :] for b in range(lane_boxes)
        ]
        stacked = jnp.concatenate(rows, axis=0).astype(BF)
        group = mats[pl.ds(g * lane_boxes, lane_boxes)].reshape(lane_boxes * rank, points)
        out[g] = pick_lanes(dot_nt(group, stacked), rank, lane_boxes, vectors).astype(BF)


def forward_group(weights, stacked, lane_boxes, rank):
    mats = weights.reshape(lane_boxes * rank, LANES)
    return pick_lanes(dot(mats, stacked), rank, lane_boxes, LANES // lane_boxes).astype(BF)


def cross_step(own, other, mats, out, high, lane_boxes):
    groups, rank = own.shape[0], own.shape[1]
    for g in range(groups):
        mine, theirs = own[g], other[g]
        take = jnp.broadcast_to(high, mine.shape)
        lower = jnp.where(take, theirs, mine)
        upper = jnp.where(take, mine, theirs)
        stacked = jnp.concatenate([lower, upper], axis=0)
        weights = mats[pl.ds(g * lane_boxes, lane_boxes)]
        out[g] = forward_group(weights, stacked, lane_boxes, rank)


def cross_kernel(level, src_bits, lane_boxes, own, other, mats, out):
    cross_step(own, other, mats, out, is_high(level, src_bits), lane_boxes)


def local_forward_kernel(level, src_bits, lane_boxes, own, other, maps, out, work):
    groups, rank = own.shape[0], own.shape[1]
    lane_bits = lane_boxes.bit_length() - 1
    box_bits = maps.shape[1].bit_length() - 1
    cross_step(own, other, maps.at[0], work.at[0], is_high(level, src_bits), lane_boxes)
    for bit in range(box_bits):
        mats = maps.at[bit + 1]
        source = work.at[bit % 2]
        target = out if bit == box_bits - 1 else work.at[(bit + 1) % 2]
        if bit < lane_bits:
            shift = LANES // lane_boxes << bit
            for g in range(groups):
                value = source[g].astype(F32)
                is_set = (lane_block(value.shape, shift) & 1) == 1
                lower = jnp.where(is_set, pltpu.roll(value, shift, 1), value)
                upper = jnp.where(is_set, value, pltpu.roll(value, LANES - shift, 1))
                stacked = jnp.concatenate([lower, upper], axis=0).astype(BF)
                weights = mats[pl.ds(g * lane_boxes, lane_boxes)]
                target[g] = forward_group(weights, stacked, lane_boxes, rank)
        else:
            inner = 1 << bit - lane_bits
            for g0 in range(groups):
                if g0 & inner:
                    continue
                stacked = jnp.concatenate([source[g0], source[g0 + inner]], axis=0)
                for g in (g0, g0 + inner):
                    weights = mats[pl.ds(g * lane_boxes, lane_boxes)]
                    target[g] = forward_group(weights, stacked, lane_boxes, rank)


def target_kernel(chunk, coeffs, final, observed, *refs):
    residual, adjoint, held, sems, wide, result = refs[-6:]
    groups, rank = coeffs.shape[0], coeffs.shape[1]
    vectors, boxes, points = held.shape
    box_bits = boxes.bit_length() - 1
    lane_boxes = LANES // vectors
    own_rows = pl.ds(chunk * vectors, vectors)
    fetch = pltpu.make_async_copy(observed.at[own_rows], held, sems.at[0])
    fetch.start()
    fetch.wait()
    wide[...] = held[...].astype(F32).reshape(wide.shape)
    for g in range(groups):
        turned = jnp.transpose(coeffs[g].astype(F32)).astype(BF)
        for pair in range(lane_boxes // 2):
            kept, mats = [], []
            for b in (2 * pair, 2 * pair + 1):
                t = reverse_bits(g * lane_boxes + b, box_bits)
                mat = final[t]
                value = dot(turned[b * vectors:(b + 1) * vectors], mat)
                value = value - wide[pl.ds(t, vectors, stride=boxes), :]
                result[pl.ds(t, vectors, stride=boxes), :] = value
                kept.append(value)
                mats.append(mat)
            rows = jnp.concatenate(kept, axis=0).astype(BF)
            product = dot_nt(rows, jnp.concatenate(mats, axis=0))
            adjoint[g * lane_boxes // 2 + pair] = pick_lanes(product, vectors, 2, rank).astype(BF)
    held[...] = result[...].reshape(held.shape).astype(BF)
    store = pltpu.make_async_copy(held, residual.at[own_rows], sems.at[1])
    store.start()
    store.wait()


def adjoint_cross_pair(value, mats, kept, sent, p, high):
    rows = value.shape[0]
    low, upper = halves_of(dot(split_rows(value), mats), rows)
    take = jnp.broadcast_to(high, low.shape)
    kept[p] = jnp.where(take, upper, low)
    sent[p] = jnp.where(take, low, upper).astype(BF)


def pair_rows(mats, p):
    rank = mats.shape[1]
    return mats[pl.ds(2 * p, 2)].reshape(2 * rank, LANES)


def local_adjoint_kernel(level, src_bits, adjoint, maps, kept, sent, work):
    pairs, vectors = adjoint.shape[0], adjoint.shape[1]
    box_bits = maps.shape[1].bit_length() - 1
    for step, bit in enumerate(reversed(range(box_bits))):
        mats = maps.at[bit + 1]
        source = adjoint if step == 0 else work.at[step % 2]
        target = work.at[(step + 1) % 2]
        if bit == 0:
            for p in range(pairs):
                target[p] = dot(source[p], pair_rows(mats, p)).astype(BF)
        else:
            inner = 1 << bit - 1
            for p0 in range(pairs):
                if p0 & inner:
                    continue
                p1 = p0 + inner
                rows = jnp.concatenate([split_rows(source[p0]), split_rows(source[p1])], axis=1)
                stacked = jnp.concatenate([pair_rows(mats, p0), pair_rows(mats, p1)], axis=0)
                low, upper = halves_of(dot(rows, stacked), vectors)
                target[p0] = low.astype(BF)
                target[p1] = upper.astype(BF)
    source = work.at[box_bits % 2]
    high = is_high(level, src_bits)
    for p in range(pairs):
        adjoint_cross_pair(source[p], pair_rows(maps.at[0], p), kept, sent, p, high)


def adjoint_cross_kernel(level, src_bits, held_part, received, mats, kept, sent):
    high = is_high(level, src_bits)
    for p in range(held_part.shape[0]):
        value = (held_part[p] + received[p].astype(F32)).astype(BF)
        adjoint_cross_pair(value, pair_rows(mats, p), kept, sent, p, high)


def gradient_kernel(chunk, held_part, received, leaf, *refs):
    gradient, held, sems, result = refs[-4:]
    pairs, vectors = held_part.shape[0], held_part.shape[1]
    boxes = leaf.shape[0]
    for p in range(pairs):
        value = (held_part[p] + received[p].astype(F32)).astype(BF)
        product = dot(split_rows(value), pair_rows(leaf, p))
        result[pl.ds(2 * p, vectors, stride=boxes), :] = product[:vectors]
        result[pl.ds(2 * p + 1, vectors, stride=boxes), :] = product[vectors:]
    held[...] = result[...].reshape(held.shape).astype(BF)
    store = pltpu.make_async_copy(
        held, gradient.at[pl.ds(chunk * vectors, vectors)], sems.at[0]
    )
    store.start()
    store.wait()


VMEM = pl.BlockSpec(memory_space=pltpu.VMEM)
ANY = pl.BlockSpec(memory_space=pl.ANY)


def call(kernel, out_shape, in_specs, out_specs, scratch, flops, moved, limit, aliases=None):
    return pl.pallas_call(
        kernel,
        out_shape=out_shape,
        in_specs=in_specs,
        out_specs=out_specs,
        scratch_shapes=scratch,
        input_output_aliases=aliases or {},
        compiler_params=pltpu.CompilerParams(vmem_limit_bytes=limit << 20),
        cost_estimate=pl.CostEstimate(flops=flops, bytes_accessed=moved, transcendentals=0),
    )


def body(traces, observed, leaf_maps, level_maps, final_maps):
    total = traces.shape[0]
    boxes, points = traces.shape[1], traces.shape[4]
    rank = leaf_maps.shape[3]
    src_count, hi_count = lax.axis_size("src"), lax.axis_size("hi")
    src_bits = src_count.bit_length() - 1
    hi_bits = hi_count.bit_length() - 1
    device_bits = src_bits + hi_bits
    box_bits = boxes.bit_length() - 1
    vectors = total // CHUNKS
    lane_boxes = LANES // vectors
    groups, pairs = boxes // lane_boxes, boxes // 2

    leaf = leaf_maps.reshape(boxes, rank, points)
    final = final_maps.reshape(boxes, rank, points)
    levels = level_maps.reshape(level_maps.shape[0], boxes, rank, 2 * rank)
    samples = traces.reshape(total, boxes, points)
    wanted = observed.reshape(total, boxes, points)

    def shape(*dims, dtype=BF):
        return jax.ShapeDtypeStruct(dims, dtype)

    forward_shape = shape(groups, rank, LANES)
    pair_shape = shape(pairs, vectors, LANES)
    kept_shape = shape(pairs, vectors, LANES, dtype=F32)
    sample_shape = shape(vectors, boxes, points)
    full_shape = shape(total, boxes, points)
    wide = pltpu.VMEM((vectors * boxes, points), F32)
    held = pltpu.VMEM((vectors, boxes, points), BF)
    sems = pltpu.SemaphoreType.DMA((2,))
    flops = 2 * boxes * rank * 2 * rank * vectors
    moved = boxes * rank * 2 * rank * 2

    def exchange(array, level):
        if level < src_bits:
            axis, count, bit = "src", src_count, level
        else:
            axis, count, bit = "hi", hi_count, level - src_bits
        return lax.ppermute(array, axis, [(i, i ^ 1 << bit) for i in range(count)])

    def reversal(array):
        pairs_of = []
        for src in range(src_count):
            for hi in range(hi_count):
                there = reverse_bits(hi * src_count + src, device_bits)
                pairs_of.append(
                    (src * hi_count + hi, there % src_count * hi_count + there // src_count)
                )
        return lax.ppermute(array, ("src", "hi"), pairs_of)

    def leaf_call(chunk):
        kernel = functools.partial(leaf_kernel, chunk)
        scratch = [held, pltpu.VMEM((boxes, rank, points), BF), sems, wide]
        return call(kernel, forward_shape, [ANY, ANY], VMEM, scratch, flops, 2 * moved, 8)

    def target_call(chunk, *operands):
        kernel = functools.partial(target_kernel, chunk)
        specs = [VMEM, VMEM, ANY] + [ANY] * (len(operands) - 3)
        return call(
            kernel, (full_shape, pair_shape), specs, (ANY, VMEM), [held, sems, wide, wide],
            2 * flops, 2 * moved, 8, {3: 0} if len(operands) > 3 else None,
        )(*operands)

    def gradient_call(chunk, *operands):
        kernel = functools.partial(gradient_kernel, chunk)
        specs = [VMEM] * 3 + [ANY] * (len(operands) - 3)
        return call(
            kernel, full_shape, specs, ANY, [held, sems, wide],
            flops, 2 * moved, 8, {3: 0} if len(operands) > 3 else None,
        )(*operands)

    def cross_call(level):
        kernel = functools.partial(cross_kernel, level, src_bits, lane_boxes)
        return call(kernel, forward_shape, [VMEM] * 3, VMEM, [], flops, moved, 4)

    def adjoint_call(level):
        kernel = functools.partial(adjoint_cross_kernel, level, src_bits)
        return call(
            kernel, (kept_shape, pair_shape), [VMEM] * 3, (VMEM, VMEM), [], flops, moved, 4
        )

    top = device_bits - 1
    count = box_bits + 1
    local_forward = call(
        functools.partial(local_forward_kernel, top, src_bits, lane_boxes),
        forward_shape,
        [VMEM] * 3,
        VMEM,
        [pltpu.VMEM((2, groups, rank, LANES), BF)],
        count * flops,
        count * moved,
        8,
    )
    local_adjoint = call(
        functools.partial(local_adjoint_kernel, top, src_bits),
        (kept_shape, pair_shape),
        [VMEM] * 2,
        (VMEM, VMEM),
        [pltpu.VMEM((2, pairs, vectors, LANES), BF)],
        count * flops,
        count * moved,
        8,
    )

    cross_maps = [levels[level] for level in range(top)]
    local_maps = levels[top:]
    residual, gradient = (), ()
    for chunk in range(CHUNKS):
        coeffs = leaf_call(chunk)(samples, leaf)
        for level in range(top):
            coeffs = cross_call(level)(coeffs, exchange(coeffs, level), cross_maps[level])
        coeffs = local_forward(coeffs, exchange(coeffs, top), local_maps)
        *residual, adjoint = target_call(chunk, reversal(coeffs), final, wanted, *residual)
        kept, sent = local_adjoint(reversal(adjoint), local_maps)
        for level in reversed(range(top)):
            kept, sent = adjoint_call(level)(kept, exchange(sent, level + 1), cross_maps[level])
        gradient = [gradient_call(chunk, kept, exchange(sent, 0), leaf, *gradient)]
    residual, gradient = residual[0], gradient[0]
    return (
        residual.reshape(total, 1, 1, boxes, points),
        gradient.reshape(total, boxes, 1, 1, points),
    )


def solution(mesh):
    placed = (
        P(None, None, "hi", "src", None),
        P(None, "hi", "src", None, None),
        P(None, "hi", "src", None, None),
        P(None, None, "hi", "src", None, None),
        P("hi", "src", None, None, None),
    )
    return jax.shard_map(
        body,
        mesh=mesh,
        in_specs=placed,
        out_specs=(P(None, "hi", "src", None, None), P(None, None, "hi", "src", None)),
        check_vma=False,
    )
```

```python
import functools

import jax
import jax.numpy as jnp
from jax import lax
from jax.experimental import pallas as pl
from jax.experimental.pallas import tpu as pltpu
from jax.sharding import PartitionSpec as P

CHUNKS = 2
LANES = 128
BF = jnp.bfloat16
F32 = jnp.float32


def reverse_bits(value, bits):
    return int(format(value, f"0{bits}b")[::-1], 2)


def lane_block(shape, width):
    return lax.broadcasted_iota(jnp.int32, shape, len(shape) - 1) // width


def pick_lanes(product, rows, count, width):
    block = lane_block((rows, LANES), width)
    out = product[:rows]
    for b in range(1, count):
        out = jnp.where(block == b, product[b * rows:(b + 1) * rows], out)
    return out


def split_rows(pair):
    left = lane_block(pair.shape, LANES // 2) == 0
    zero = jnp.zeros(pair.shape, pair.dtype)
    return jnp.concatenate([jnp.where(left, pair, zero), jnp.where(left, zero, pair)], axis=0)


def halves_of(product, rows):
    first, second = product[:rows], product[rows:]
    left = lane_block((rows, LANES), LANES // 2) == 0
    low = jnp.where(left, first, pltpu.roll(second, LANES // 2, 1))
    high = jnp.where(left, pltpu.roll(first, LANES // 2, 1), second)
    return low, high


def is_high(level, src_bits):
    if level < src_bits:
        return (lax.axis_index("src") >> level & 1) == 1
    return (lax.axis_index("hi") >> (level - src_bits) & 1) == 1


def dot(a, b):
    return jnp.dot(a, b, preferred_element_type=F32)


def dot_nt(a, b):
    return lax.dot_general(a, b, (((1,), (1,)), ((), ())), preferred_element_type=F32)


def leaf_kernel(chunk, traces, leaf, token, out, held, mats, sems, wide):
    vectors, boxes, points = held.shape
    lane_boxes = LANES // vectors
    rank = mats.shape[1]
    copies = [
        pltpu.make_async_copy(traces.at[pl.ds(chunk * vectors, vectors)], held, sems.at[0]),
        pltpu.make_async_copy(leaf, mats, sems.at[1]),
    ]
    for copy in copies:
        copy.start()
    copies[0].wait()
    wide[...] = held[...].astype(F32).reshape(wide.shape)
    copies[1].wait()
    for g in range(boxes // lane_boxes):
        rows = [
            wide[pl.ds(g * lane_boxes + b, vectors, stride=boxes), :] for b in range(lane_boxes)
        ]
        stacked = jnp.concatenate(rows, axis=0).astype(BF)
        group = mats[pl.ds(g * lane_boxes, lane_boxes)].reshape(lane_boxes * rank, points)
        out[g] = pick_lanes(dot_nt(group, stacked), rank, lane_boxes, vectors).astype(BF)


def forward_group(weights, stacked, lane_boxes, rank):
    mats = weights.reshape(lane_boxes * rank, LANES)
    return pick_lanes(dot(mats, stacked), rank, lane_boxes, LANES // lane_boxes).astype(BF)


def cross_step(own, other, mats, out, high, lane_boxes):
    groups, rank = own.shape[0], own.shape[1]
    for g in range(groups):
        mine, theirs = own[g], other[g]
        take = jnp.broadcast_to(high, mine.shape)
        lower = jnp.where(take, theirs, mine)
        upper = jnp.where(take, mine, theirs)
        stacked = jnp.concatenate([lower, upper], axis=0)
        weights = mats[pl.ds(g * lane_boxes, lane_boxes)]
        out[g] = forward_group(weights, stacked, lane_boxes, rank)


def cross_kernel(level, src_bits, lane_boxes, own, other, maps, token, out):
    cross_step(own, other, maps.at[level], out, is_high(level, src_bits), lane_boxes)


def local_forward(lane_boxes, maps, first, out, work):
    groups, rank = out.shape[0], out.shape[1]
    lane_bits = lane_boxes.bit_length() - 1
    box_bits = maps.shape[1].bit_length() - 1
    for bit in range(box_bits):
        mats = maps.at[first + bit]
        source = work.at[bit % 2]
        target = out if bit == box_bits - 1 else work.at[(bit + 1) % 2]
        if bit < lane_bits:
            shift = LANES // lane_boxes << bit
            for g in range(groups):
                value = source[g].astype(F32)
                is_set = (lane_block(value.shape, shift) & 1) == 1
                lower = jnp.where(is_set, pltpu.roll(value, shift, 1), value)
                upper = jnp.where(is_set, value, pltpu.roll(value, LANES - shift, 1))
                stacked = jnp.concatenate([lower, upper], axis=0).astype(BF)
                weights = mats[pl.ds(g * lane_boxes, lane_boxes)]
                target[g] = forward_group(weights, stacked, lane_boxes, rank)
        else:
            inner = 1 << bit - lane_bits
            for g0 in range(groups):
                if g0 & inner:
                    continue
                stacked = jnp.concatenate([source[g0], source[g0 + inner]], axis=0)
                for g in (g0, g0 + inner):
                    weights = mats[pl.ds(g * lane_boxes, lane_boxes)]
                    target[g] = forward_group(weights, stacked, lane_boxes, rank)


def prepare_kernel(final_maps, observed, token, out, final, held, sems, wide):
    vectors, boxes, points = held.shape
    rank = final.shape[1]
    box_bits = boxes.bit_length() - 1
    fetch_maps = pltpu.make_async_copy(final_maps, final, sems.at[1])
    fetch_maps.start()
    fetch = pltpu.make_async_copy(observed, held, sems.at[0])
    fetch.start()
    fetch_maps.wait()
    for p in range(boxes // 2):
        mats = pair_final(final, p, box_bits)
        out[0, p] = pick_lanes(dot_nt(mats, mats), rank, 2, rank).astype(BF)
    fetch.wait()
    wide[...] = held[...].astype(F32).reshape(wide.shape)
    for p in range(boxes // 2):
        rows = [
            wide[pl.ds(reverse_bits(k, box_bits), vectors, stride=boxes), :]
            for k in (2 * p, 2 * p + 1)
        ]
        product = dot_nt(jnp.concatenate(rows, axis=0).astype(BF), pair_final(final, p, box_bits))
        out[1, p] = pick_lanes(product, vectors, 2, rank).astype(BF)


def pair_final(final, p, box_bits):
    return jnp.concatenate(
        [final[reverse_bits(2 * p, box_bits)], final[reverse_bits(2 * p + 1, box_bits)]], axis=0
    )


def residual_kernel(chunk, coeffs, final_maps, observed, *refs):
    residual, done, final, held, sems, wide, result = refs[-7:]
    groups = coeffs.shape[0]
    vectors, boxes, points = held.shape
    box_bits = boxes.bit_length() - 1
    lane_boxes = LANES // vectors
    own_rows = pl.ds(chunk * vectors, vectors)
    fetch_maps = pltpu.make_async_copy(final_maps, final, sems.at[1])
    fetch_maps.start()
    fetch = pltpu.make_async_copy(observed.at[own_rows], held, sems.at[0])
    fetch.start()
    fetch.wait()
    wide[...] = held[...].astype(F32).reshape(wide.shape)
    fetch_maps.wait()
    done[...] = jnp.zeros(done.shape, done.dtype)
    for g in range(groups):
        turned = jnp.transpose(coeffs[g].astype(F32)).astype(BF)
        for b in range(lane_boxes):
            t = reverse_bits(g * lane_boxes + b, box_bits)
            value = dot(turned[b * vectors:(b + 1) * vectors], final[t])
            rows = pl.ds(t, vectors, stride=boxes)
            result[rows, :] = value - wide[rows, :]
    held[...] = result[...].reshape(held.shape).astype(BF)
    store = pltpu.make_async_copy(held, residual.at[own_rows], sems.at[1])
    store.start()
    store.wait()


def adjoint_cross_pair(value, mats, kept, sent, p, high):
    rows = value.shape[0]
    low, upper = halves_of(dot(split_rows(value), mats), rows)
    take = jnp.broadcast_to(high, low.shape)
    kept[p] = jnp.where(take, upper, low)
    sent[p] = jnp.where(take, low, upper).astype(BF)


def pair_rows(mats, p):
    rank = mats.shape[1]
    return mats[pl.ds(2 * p, 2)].reshape(2 * rank, LANES)


def local_adjoint(maps, first, work):
    pairs, vectors = work.shape[1], work.shape[2]
    box_bits = maps.shape[1].bit_length() - 1
    for step, bit in enumerate(reversed(range(box_bits))):
        mats = maps.at[first + bit]
        source = work.at[step % 2]
        target = work.at[(step + 1) % 2]
        if bit == 0:
            for p in range(pairs):
                target[p] = dot(source[p], pair_rows(mats, p)).astype(BF)
        else:
            inner = 1 << bit - 1
            for p0 in range(pairs):
                if p0 & inner:
                    continue
                p1 = p0 + inner
                rows = jnp.concatenate([split_rows(source[p0]), split_rows(source[p1])], axis=1)
                stacked = jnp.concatenate([pair_rows(mats, p0), pair_rows(mats, p1)], axis=0)
                low, upper = halves_of(dot(rows, stacked), vectors)
                target[p0] = low.astype(BF)
                target[p1] = upper.astype(BF)
    return work.at[box_bits % 2]


def middle_kernel(
    level, src_bits, lane_boxes, chunk, own, other, maps, normal, token,
    coeffs, kept, sent, work, pair_work,
):
    groups, rank = own.shape[0], own.shape[1]
    pairs, vectors = kept.shape[0], kept.shape[1]
    high = is_high(level, src_bits)
    cross_step(own, other, maps.at[level], work.at[0], high, lane_boxes)
    local_forward(lane_boxes, maps, level + 1, coeffs, work)
    for g in range(groups):
        turned = jnp.transpose(coeffs[g].astype(F32)).astype(BF)
        for i in range(lane_boxes // 2):
            p = g * lane_boxes // 2 + i
            product = dot(turned[2 * i * vectors:2 * (i + 1) * vectors], normal[0, p])
            value = pick_lanes(product, vectors, 2, rank)
            wanted = normal[1, p, pl.ds(chunk * vectors, vectors), :].astype(F32)
            pair_work[0, p] = (value - wanted).astype(BF)
    source = local_adjoint(maps, level + 1, pair_work)
    for p in range(pairs):
        adjoint_cross_pair(source[p], pair_rows(maps.at[level], p), kept, sent, p, high)


def adjoint_cross_kernel(level, src_bits, held_part, received, maps, token, kept, sent):
    high = is_high(level, src_bits)
    for p in range(held_part.shape[0]):
        value = (held_part[p] + received[p].astype(F32)).astype(BF)
        adjoint_cross_pair(value, pair_rows(maps.at[level], p), kept, sent, p, high)


def gradient_kernel(chunk, held_part, received, leaf, *refs):
    gradient, held, sems, result = refs[-4:]
    pairs, vectors = held_part.shape[0], held_part.shape[1]
    boxes = leaf.shape[0]
    for p in range(pairs):
        value = (held_part[p] + received[p].astype(F32)).astype(BF)
        product = dot(split_rows(value), pair_rows(leaf, p))
        result[pl.ds(2 * p, vectors, stride=boxes), :] = product[:vectors]
        result[pl.ds(2 * p + 1, vectors, stride=boxes), :] = product[vectors:]
    held[...] = result[...].reshape(held.shape).astype(BF)
    store = pltpu.make_async_copy(
        held, gradient.at[pl.ds(chunk * vectors, vectors)], sems.at[0]
    )
    store.start()
    store.wait()


VMEM = pl.BlockSpec(memory_space=pltpu.VMEM)
ANY = pl.BlockSpec(memory_space=pl.ANY)
HBM = pl.BlockSpec(memory_space=pltpu.HBM)


def call(kernel, out_shape, in_specs, out_specs, scratch, flops, moved, limit, aliases=None):
    return pl.pallas_call(
        kernel,
        out_shape=out_shape,
        in_specs=in_specs,
        out_specs=out_specs,
        scratch_shapes=scratch,
        input_output_aliases=aliases or {},
        compiler_params=pltpu.CompilerParams(vmem_limit_bytes=limit << 20),
        cost_estimate=pl.CostEstimate(flops=flops, bytes_accessed=moved, transcendentals=0),
    )


def body(traces, observed, leaf_maps, level_maps, final_maps):
    total = traces.shape[0]
    boxes, points = traces.shape[1], traces.shape[4]
    rank = leaf_maps.shape[3]
    src_count, hi_count = lax.axis_size("src"), lax.axis_size("hi")
    src_bits = src_count.bit_length() - 1
    hi_bits = hi_count.bit_length() - 1
    device_bits = src_bits + hi_bits
    box_bits = boxes.bit_length() - 1
    vectors = total // CHUNKS
    lane_boxes = LANES // vectors
    groups, pairs = boxes // lane_boxes, boxes // 2

    leaf = leaf_maps.reshape(boxes, rank, points)
    final = final_maps.reshape(boxes, rank, points)
    levels = level_maps.reshape(level_maps.shape[0], boxes, rank, 2 * rank)
    samples = traces.reshape(total, boxes, points)
    wanted = observed.reshape(total, boxes, points)

    def shape(*dims, dtype=BF):
        return jax.ShapeDtypeStruct(dims, dtype)

    forward_shape = shape(groups, rank, LANES)
    pair_shape = shape(pairs, vectors, LANES)
    kept_shape = shape(pairs, vectors, LANES, dtype=F32)
    sample_shape = shape(vectors, boxes, points)
    full_shape = shape(total, boxes, points)
    wide = pltpu.VMEM((vectors * boxes, points), F32)
    held = pltpu.VMEM((vectors, boxes, points), BF)
    sems = pltpu.SemaphoreType.DMA((2,))
    flops = 2 * boxes * rank * 2 * rank * vectors
    moved = boxes * rank * 2 * rank * 2

    def exchange(array, level):
        if level < src_bits:
            axis, count, bit = "src", src_count, level
        else:
            axis, count, bit = "hi", hi_count, level - src_bits
        return lax.ppermute(array, axis, [(i, i ^ 1 << bit) for i in range(count)])

    def reversal(array):
        pairs_of = []
        for src in range(src_count):
            for hi in range(hi_count):
                there = reverse_bits(hi * src_count + src, device_bits)
                pairs_of.append(
                    (src * hi_count + hi, there % src_count * hi_count + there // src_count)
                )
        return lax.ppermute(array, ("src", "hi"), pairs_of)

    def leaf_call(chunk):
        kernel = functools.partial(leaf_kernel, chunk)
        scratch = [held, pltpu.VMEM((boxes, rank, points), BF), sems, wide]
        return call(kernel, forward_shape, [HBM, HBM, ANY], VMEM, scratch, flops, 2 * moved, 8)

    def prepare(*operands):
        scratch = [
            pltpu.VMEM((boxes, rank, points), BF), pltpu.VMEM((total, boxes, points), BF), sems,
            pltpu.VMEM((total * boxes, points), F32),
        ]
        return call(
            prepare_kernel, shape(2, pairs, total, LANES), [HBM, HBM, ANY], VMEM, scratch,
            4 * flops, 4 * moved, 8,
        )(*operands)

    def residual_call(chunk, *operands):
        kernel = functools.partial(residual_kernel, chunk)
        specs = [VMEM, HBM, HBM, ANY] + [HBM] * (len(operands) - 4)
        scratch = [pltpu.VMEM((boxes, rank, points), BF), held, sems, wide, wide]
        return call(
            kernel, (full_shape, shape(8, LANES, dtype=F32)), specs, (HBM, VMEM), scratch,
            flops, 2 * moved, 8, {4: 0} if len(operands) > 4 else None,
        )(*operands)

    def gradient_call(chunk, *operands):
        kernel = functools.partial(gradient_kernel, chunk)
        specs = [VMEM] * 3 + [HBM] * (len(operands) - 3)
        return call(
            kernel, full_shape, specs, HBM, [held, sems, wide],
            flops, 2 * moved, 8, {3: 0} if len(operands) > 3 else None,
        )(*operands)

    def cross_call(level):
        kernel = functools.partial(cross_kernel, level, src_bits, lane_boxes)
        return call(kernel, forward_shape, [VMEM] * 3 + [ANY], VMEM, [], flops, moved, 4)

    def adjoint_call(level):
        kernel = functools.partial(adjoint_cross_kernel, level, src_bits)
        return call(
            kernel, (kept_shape, pair_shape), [VMEM] * 3 + [ANY], (VMEM, VMEM), [], flops, moved, 4
        )

    def middle_call(chunk):
        kernel = functools.partial(middle_kernel, top, src_bits, lane_boxes, chunk)
        scratch = [
            pltpu.VMEM((2, groups, rank, LANES), BF),
            pltpu.VMEM((2, pairs, vectors, LANES), BF),
        ]
        return call(
            kernel, (forward_shape, kept_shape, pair_shape), [VMEM] * 4 + [ANY], (VMEM,) * 3,
            scratch, 15 * flops, 15 * moved, 8,
        )

    top = device_bits - 1
    token = leaf
    coeffs, kept, sent, target = [None] * CHUNKS, [None] * CHUNKS, [None] * CHUNKS, [None] * CHUNKS
    every = range(CHUNKS)
    for c in every:
        coeffs[c] = token = leaf_call(c)(samples, leaf, token)
    normal = None
    for level in range(top):
        for c in every:
            maps = levels if level else levels[:1]
            token = cross_call(level)(coeffs[c], exchange(coeffs[c], level), maps, token)
            coeffs[c] = token
        if level == 0:
            normal = token = prepare(final, wanted, token)
            normal = reversal(normal)
    for c in every:
        target[c], kept[c], sent[c] = middle_call(c)(
            coeffs[c], exchange(coeffs[c], top), levels, normal, token
        )
        token = sent[c]
    residual, gradient = (), ()
    for level in reversed(range(top)):
        for c in every:
            kept[c], sent[c] = adjoint_call(level)(
                kept[c], exchange(sent[c], level + 1), levels, token
            )
            token = sent[c]
        if level == 1:
            for c in every:
                operands = (reversal(target[c]), final, wanted, token, *residual)
                *residual, token = residual_call(c, *operands)
    for c in every:
        gradient = [gradient_call(c, kept[c], exchange(sent[c], 0), leaf, *gradient)]
    residual, gradient = residual[0], gradient[0]
    return (
        residual.reshape(total, 1, 1, boxes, points),
        gradient.reshape(total, boxes, 1, 1, points),
    )


def solution(mesh):
    placed = (
        P(None, None, "hi", "src", None),
        P(None, "hi", "src", None, None),
        P(None, "hi", "src", None, None),
        P(None, None, "hi", "src", None, None),
        P("hi", "src", None, None, None),
    )
    return jax.shard_map(
        body,
        mesh=mesh,
        in_specs=placed,
        out_specs=(P(None, "hi", "src", None, None), P(None, None, "hi", "src", None)),
        check_vma=False,
    )
```

```python
import functools

import jax
import jax.numpy as jnp
from jax import lax
from jax.experimental import pallas as pl
from jax.experimental.pallas import tpu as pltpu
from jax.sharding import PartitionSpec as P

CHUNKS = 2
LANES = 128
BF = jnp.bfloat16
F32 = jnp.float32


def reverse_bits(value, bits):
    return int(format(value, f"0{bits}b")[::-1], 2)


def lane_block(shape, width):
    return lax.broadcasted_iota(jnp.int32, shape, len(shape) - 1) // width


def pick_lanes(product, rows, count, width):
    block = lane_block((rows, LANES), width)
    out = product[:rows]
    for b in range(1, count):
        out = jnp.where(block == b, product[b * rows:(b + 1) * rows], out)
    return out


def split_rows(pair):
    left = lane_block(pair.shape, LANES // 2) == 0
    zero = jnp.zeros(pair.shape, pair.dtype)
    return jnp.concatenate([jnp.where(left, pair, zero), jnp.where(left, zero, pair)], axis=0)


def halves_of(product, rows):
    first, second = product[:rows], product[rows:]
    left = lane_block((rows, LANES), LANES // 2) == 0
    low = jnp.where(left, first, pltpu.roll(second, LANES // 2, 1))
    high = jnp.where(left, pltpu.roll(first, LANES // 2, 1), second)
    return low, high


def is_high(level, src_bits):
    if level < src_bits:
        return (lax.axis_index("src") >> level & 1) == 1
    return (lax.axis_index("hi") >> (level - src_bits) & 1) == 1


def shear_x(device):
    return device ^ reverse_bits(device >> 4 & 3, 2) << 1


def shear_y(device):
    return device ^ reverse_bits(device >> 1 & 3, 2) << 4


def swap_ends(device):
    return device & 62 | device >> 6 | (device & 1) << 6


def dot(a, b):
    return jnp.dot(a, b, preferred_element_type=F32)


def dot_nt(a, b):
    return lax.dot_general(a, b, (((1,), (1,)), ((), ())), preferred_element_type=F32)


def leaf_kernel(chunk, traces, leaf, token, out, held, mats, sems, wide):
    vectors, boxes, points = held.shape
    lane_boxes = LANES // vectors
    rank = mats.shape[1]
    copies = [
        pltpu.make_async_copy(traces.at[pl.ds(chunk * vectors, vectors)], held, sems.at[0]),
        pltpu.make_async_copy(leaf, mats, sems.at[1]),
    ]
    for copy in copies:
        copy.start()
    copies[0].wait()
    wide[...] = held[...].astype(F32).reshape(wide.shape)
    copies[1].wait()
    for g in range(boxes // lane_boxes):
        rows = [
            wide[pl.ds(g * lane_boxes + b, vectors, stride=boxes), :] for b in range(lane_boxes)
        ]
        stacked = jnp.concatenate(rows, axis=0).astype(BF)
        group = mats[pl.ds(g * lane_boxes, lane_boxes)].reshape(lane_boxes * rank, points)
        out[g] = pick_lanes(dot_nt(group, stacked), rank, lane_boxes, vectors).astype(BF)


def forward_group(weights, stacked, lane_boxes, rank):
    mats = weights.reshape(lane_boxes * rank, LANES)
    return pick_lanes(dot(mats, stacked), rank, lane_boxes, LANES // lane_boxes).astype(BF)


def cross_step(own, other, mats, out, high, lane_boxes):
    groups, rank = own.shape[0], own.shape[1]
    for g in range(groups):
        mine, theirs = own[g], other[g]
        take = jnp.broadcast_to(high, mine.shape)
        lower = jnp.where(take, theirs, mine)
        upper = jnp.where(take, mine, theirs)
        stacked = jnp.concatenate([lower, upper], axis=0)
        weights = mats[pl.ds(g * lane_boxes, lane_boxes)]
        out[g] = forward_group(weights, stacked, lane_boxes, rank)


def cross_kernel(level, src_bits, lane_boxes, own, other, maps, *refs):
    cross_step(own, other, maps.at[level], refs[-1], is_high(level, src_bits), lane_boxes)


def local_forward(lane_boxes, maps, first, out, work):
    groups, rank = out.shape[0], out.shape[1]
    lane_bits = lane_boxes.bit_length() - 1
    box_bits = maps.shape[1].bit_length() - 1
    for bit in range(box_bits):
        mats = maps.at[first + bit]
        source = work.at[bit % 2]
        target = out if bit == box_bits - 1 else work.at[(bit + 1) % 2]
        if bit < lane_bits:
            shift = LANES // lane_boxes << bit
            for g in range(groups):
                value = source[g].astype(F32)
                is_set = (lane_block(value.shape, shift) & 1) == 1
                lower = jnp.where(is_set, pltpu.roll(value, shift, 1), value)
                upper = jnp.where(is_set, value, pltpu.roll(value, LANES - shift, 1))
                stacked = jnp.concatenate([lower, upper], axis=0).astype(BF)
                weights = mats[pl.ds(g * lane_boxes, lane_boxes)]
                target[g] = forward_group(weights, stacked, lane_boxes, rank)
        else:
            inner = 1 << bit - lane_bits
            for g0 in range(groups):
                if g0 & inner:
                    continue
                stacked = jnp.concatenate([source[g0], source[g0 + inner]], axis=0)
                for g in (g0, g0 + inner):
                    weights = mats[pl.ds(g * lane_boxes, lane_boxes)]
                    target[g] = forward_group(weights, stacked, lane_boxes, rank)


def prepare_kernel(final_maps, observed, token, gram, right, final, held, sems, wide):
    vectors, boxes, points = held.shape
    rank = final.shape[1]
    box_bits = boxes.bit_length() - 1
    fetch_maps = pltpu.make_async_copy(final_maps, final, sems.at[1])
    fetch_maps.start()
    fetch = pltpu.make_async_copy(observed, held, sems.at[0])
    fetch.start()
    fetch_maps.wait()
    for p in range(boxes // 2):
        mats = pair_final(final, p, box_bits)
        gram[p] = pick_lanes(dot_nt(mats, mats), rank, 2, rank).astype(BF)
    fetch.wait()
    wide[...] = held[...].astype(F32).reshape(wide.shape)
    for p in range(boxes // 2):
        rows = [
            wide[pl.ds(reverse_bits(k, box_bits), vectors, stride=boxes), :]
            for k in (2 * p, 2 * p + 1)
        ]
        product = dot_nt(jnp.concatenate(rows, axis=0).astype(BF), pair_final(final, p, box_bits))
        right[p] = pick_lanes(product, vectors, 2, rank).astype(BF)


def pair_final(final, p, box_bits):
    return jnp.concatenate(
        [final[reverse_bits(2 * p, box_bits)], final[reverse_bits(2 * p + 1, box_bits)]], axis=0
    )


def residual_kernel(chunks, *refs):
    coeffs = refs[:chunks]
    final_maps, observed, token, residual, done, final, held, sems, wide = refs[chunks:]
    groups = coeffs[0].shape[0]
    total, boxes, points = held.shape
    vectors = total // chunks
    box_bits = boxes.bit_length() - 1
    lane_boxes = LANES // vectors
    fetch = pltpu.make_async_copy(observed, held, sems.at[0])
    fetch.start()
    fetch_maps = pltpu.make_async_copy(final_maps, final, sems.at[1])
    fetch_maps.start()
    fetch.wait()
    wide[...] = held[...].astype(F32).reshape(wide.shape)
    fetch_maps.wait()
    done[...] = jnp.zeros(done.shape, done.dtype)
    for g in range(groups):
        turned = [jnp.transpose(part[g].astype(F32)).astype(BF) for part in coeffs]
        for b in range(lane_boxes):
            t = reverse_bits(g * lane_boxes + b, box_bits)
            own = [part[b * vectors:(b + 1) * vectors] for part in turned]
            value = dot(jnp.concatenate(own, axis=0), final[t])
            rows = pl.ds(t, total, stride=boxes)
            wide[rows, :] = value - wide[rows, :]
    held[...] = wide[...].reshape(held.shape).astype(BF)
    store = pltpu.make_async_copy(held, residual, sems.at[0])
    store.start()
    store.wait()


def adjoint_cross_pair(value, mats, kept, sent, p, high):
    rows = value.shape[0]
    low, upper = halves_of(dot(split_rows(value), mats), rows)
    take = jnp.broadcast_to(high, low.shape)
    kept[p] = jnp.where(take, upper, low)
    sent[p] = jnp.where(take, low, upper).astype(BF)


def pair_rows(mats, p):
    rank = mats.shape[1]
    return mats[pl.ds(2 * p, 2)].reshape(2 * rank, LANES)


def local_adjoint(maps, first, work):
    pairs, vectors = work.shape[1], work.shape[2]
    box_bits = maps.shape[1].bit_length() - 1
    for step, bit in enumerate(reversed(range(box_bits))):
        mats = maps.at[first + bit]
        source = work.at[step % 2]
        target = work.at[(step + 1) % 2]
        if bit == 0:
            for p in range(pairs):
                target[p] = dot(source[p], pair_rows(mats, p)).astype(BF)
        else:
            inner = 1 << bit - 1
            for p0 in range(pairs):
                if p0 & inner:
                    continue
                p1 = p0 + inner
                rows = jnp.concatenate([split_rows(source[p0]), split_rows(source[p1])], axis=1)
                stacked = jnp.concatenate([pair_rows(mats, p0), pair_rows(mats, p1)], axis=0)
                low, upper = halves_of(dot(rows, stacked), vectors)
                target[p0] = low.astype(BF)
                target[p1] = upper.astype(BF)
    return work.at[box_bits % 2]


def middle_kernel(
    level, src_bits, lane_boxes, chunk, own, other, maps, gram, right, *refs,
):
    coeffs, kept, sent, work, pair_work = refs[-5:]
    groups, rank = own.shape[0], own.shape[1]
    pairs, vectors = kept.shape[0], kept.shape[1]
    high = is_high(level, src_bits)
    cross_step(own, other, maps.at[level], work.at[0], high, lane_boxes)
    local_forward(lane_boxes, maps, level + 1, coeffs, work)
    for g in range(groups):
        turned = jnp.transpose(coeffs[g].astype(F32)).astype(BF)
        for i in range(lane_boxes // 2):
            p = g * lane_boxes // 2 + i
            product = dot(turned[2 * i * vectors:2 * (i + 1) * vectors], gram[p])
            value = pick_lanes(product, vectors, 2, rank)
            wanted = right[p, pl.ds(chunk * vectors, vectors), :].astype(F32)
            pair_work[0, p] = (value - wanted).astype(BF)
    source = local_adjoint(maps, level + 1, pair_work)
    for p in range(pairs):
        adjoint_cross_pair(source[p], pair_rows(maps.at[level], p), kept, sent, p, high)


def adjoint_cross_kernel(level, src_bits, held_part, received, maps, *refs):
    kept, sent = refs[-2:]
    high = is_high(level, src_bits)
    for p in range(held_part.shape[0]):
        value = (held_part[p] + received[p].astype(F32)).astype(BF)
        adjoint_cross_pair(value, pair_rows(maps.at[level], p), kept, sent, p, high)


def gradient_kernel(chunk, held_part, received, leaf, *refs):
    gradient, held, sems, result = refs[-4:]
    pairs, vectors = held_part.shape[0], held_part.shape[1]
    boxes = leaf.shape[0]
    for p in range(pairs):
        value = (held_part[p] + received[p].astype(F32)).astype(BF)
        product = dot(split_rows(value), pair_rows(leaf, p))
        result[pl.ds(2 * p, vectors, stride=boxes), :] = product[:vectors]
        result[pl.ds(2 * p + 1, vectors, stride=boxes), :] = product[vectors:]
    held[...] = result[...].reshape(held.shape).astype(BF)
    store = pltpu.make_async_copy(
        held, gradient.at[pl.ds(chunk * vectors, vectors)], sems.at[0]
    )
    store.start()
    store.wait()


VMEM = pl.BlockSpec(memory_space=pltpu.VMEM)
ANY = pl.BlockSpec(memory_space=pl.ANY)
HBM = pl.BlockSpec(memory_space=pltpu.HBM)


def call(kernel, out_shape, in_specs, out_specs, scratch, flops, moved, limit, aliases=None):
    return pl.pallas_call(
        kernel,
        out_shape=out_shape,
        in_specs=in_specs,
        out_specs=out_specs,
        scratch_shapes=scratch,
        input_output_aliases=aliases or {},
        compiler_params=pltpu.CompilerParams(vmem_limit_bytes=limit << 20),
        cost_estimate=pl.CostEstimate(flops=flops, bytes_accessed=moved, transcendentals=0),
    )


def body(traces, observed, leaf_maps, level_maps, final_maps):
    total = traces.shape[0]
    boxes, points = traces.shape[1], traces.shape[4]
    rank = leaf_maps.shape[3]
    src_count, hi_count = lax.axis_size("src"), lax.axis_size("hi")
    src_bits = src_count.bit_length() - 1
    hi_bits = hi_count.bit_length() - 1
    device_bits = src_bits + hi_bits
    box_bits = boxes.bit_length() - 1
    vectors = total // CHUNKS
    lane_boxes = LANES // vectors
    groups, pairs = boxes // lane_boxes, boxes // 2

    leaf = leaf_maps.reshape(boxes, rank, points)
    final = final_maps.reshape(boxes, rank, points)
    levels = level_maps.reshape(level_maps.shape[0], boxes, rank, 2 * rank)
    samples = traces.reshape(total, boxes, points)
    wanted = observed.reshape(total, boxes, points)

    def shape(*dims, dtype=BF):
        return jax.ShapeDtypeStruct(dims, dtype)

    forward_shape = shape(groups, rank, LANES)
    pair_shape = shape(pairs, vectors, LANES)
    kept_shape = shape(pairs, vectors, LANES, dtype=F32)
    sample_shape = shape(vectors, boxes, points)
    full_shape = shape(total, boxes, points)
    wide = pltpu.VMEM((vectors * boxes, points), F32)
    held = pltpu.VMEM((vectors, boxes, points), BF)
    sems = pltpu.SemaphoreType.DMA((2,))
    flops = 2 * boxes * rank * 2 * rank * vectors
    moved = boxes * rank * 2 * rank * 2

    def exchange(array, level):
        if level < src_bits:
            axis, count, bit = "src", src_count, level
        else:
            axis, count, bit = "hi", hi_count, level - src_bits
        return lax.ppermute(array, axis, [(i, i ^ 1 << bit) for i in range(count)])

    def move(array, after, route):
        if after is not None:
            array, _ = lax.optimization_barrier((array, after))
        pairs_of = []
        for src in range(src_count):
            for hi in range(hi_count):
                there = route(hi * src_count + src)
                pairs_of.append(
                    (src * hi_count + hi, there % src_count * hi_count + there // src_count)
                )
        return lax.ppermute(array, ("src", "hi"), pairs_of)

    for device in range(src_count * hi_count):
        along = shear_y(shear_x(swap_ends(shear_y(device))))
        assert along == reverse_bits(device, device_bits)

    def leaf_call(chunk):
        kernel = functools.partial(leaf_kernel, chunk)
        scratch = [held, pltpu.VMEM((boxes, rank, points), BF), sems, wide]
        return call(kernel, forward_shape, [HBM, HBM, ANY], VMEM, scratch, flops, 2 * moved, 8)

    def prepare(*operands):
        scratch = [
            pltpu.VMEM((boxes, rank, points), BF), pltpu.VMEM((total, boxes, points), BF), sems,
            pltpu.VMEM((total * boxes, points), F32),
        ]
        return call(
            prepare_kernel, (shape(pairs, rank, LANES), shape(pairs, total, LANES)),
            [HBM, HBM, ANY], (VMEM, VMEM), scratch,
            4 * flops, 4 * moved, 8,
        )(*operands)

    def residual_call(*operands):
        scratch = [
            pltpu.VMEM((boxes, rank, points), BF), pltpu.VMEM((total, boxes, points), BF), sems,
            pltpu.VMEM((total * boxes, points), F32),
        ]
        return call(
            functools.partial(residual_kernel, CHUNKS), (full_shape, shape(8, LANES, dtype=F32)),
            [VMEM] * CHUNKS + [HBM, HBM, ANY], (HBM, VMEM), scratch, 2 * flops, 4 * moved, 8,
        )(*operands)

    def gradient_call(chunk, *operands):
        kernel = functools.partial(gradient_kernel, chunk)
        specs = [VMEM] * 3 + [HBM] * (len(operands) - 3)
        return call(
            kernel, full_shape, specs, HBM, [held, sems, wide],
            flops, 2 * moved, 8, {3: 0} if len(operands) > 3 else None,
        )(*operands)

    def cross_call(level, *operands):
        kernel = functools.partial(cross_kernel, level, src_bits, lane_boxes)
        specs = [VMEM] * 3 + [ANY] * (len(operands) - 3)
        return call(kernel, forward_shape, specs, VMEM, [], flops, moved, 4)(*operands)

    def adjoint_call(level, *operands):
        kernel = functools.partial(adjoint_cross_kernel, level, src_bits)
        specs = [VMEM] * 3 + [ANY] * (len(operands) - 3)
        return call(
            kernel, (kept_shape, pair_shape), specs, (VMEM, VMEM), [], flops, moved, 4
        )(*operands)

    def middle_call(chunk, *operands):
        kernel = functools.partial(middle_kernel, top, src_bits, lane_boxes, chunk)
        scratch = [
            pltpu.VMEM((2, groups, rank, LANES), BF),
            pltpu.VMEM((2, pairs, vectors, LANES), BF),
        ]
        specs = [VMEM] * 5 + [ANY] * (len(operands) - 5)
        return call(
            kernel, (forward_shape, kept_shape, pair_shape), specs, (VMEM,) * 3,
            scratch, 15 * flops, 15 * moved, 8,
        )(*operands)

    top = device_bits - 1
    every, last = range(CHUNKS), CHUNKS - 1
    coeffs, kept, sent = [None] * CHUNKS, [None] * CHUNKS, [None] * CHUNKS
    token = leaf
    for c in every:
        coeffs[c] = token = leaf_call(c)(samples, leaf, token)
    for level in range(top):
        maps = levels if level else levels[:1]
        for c in every:
            operands = (coeffs[c], exchange(coeffs[c], level), maps, token)
            coeffs[c] = token = cross_call(level, *operands)
            if (level, c) == (0, last):
                gram, right = prepare(final, wanted, token)
                token = right
            if (level, c) == (0, last):
                gram, right = (move(x, token, lambda d: swap_ends(shear_y(d))) for x in (gram, right))
            if (level, c) == (3, 0):
                gram, right = (move(x, token, shear_x) for x in (gram, right))
            if (level, c) == (top - 1, 0):
                gram, right = (move(x, token, shear_y) for x in (gram, right))
    target = [None] * CHUNKS
    for c in every:
        operands = (coeffs[c], exchange(coeffs[c], top), levels, gram, right, token)
        target[c], kept[c], sent[c] = middle_call(c, *operands)
        token = sent[c]
    target = [move(x, None, shear_y) for x in target]
    for level in reversed(range(top)):
        for c in every:
            operands = (kept[c], exchange(sent[c], level + 1), levels, token)
            kept[c], sent[c] = adjoint_call(level, *operands)
            token = sent[c]
            if (level, c) == (top - 1, 0):
                target = [move(x, token, lambda d: swap_ends(shear_x(d))) for x in target]
            if (level, c) == (top - 3, 0):
                target = [move(x, token, shear_y) for x in target]
        if level == top - 4:
            residual, token = residual_call(*target, final, wanted, token)
    gradient = ()
    for c in every:
        gradient = [gradient_call(c, kept[c], exchange(sent[c], 0), leaf, *gradient)]
    gradient = gradient[0]
    return (
        residual.reshape(total, 1, 1, boxes, points),
        gradient.reshape(total, boxes, 1, 1, points),
    )


def solution(mesh):
    placed = (
        P(None, None, "hi", "src", None),
        P(None, "hi", "src", None, None),
        P(None, "hi", "src", None, None),
        P(None, None, "hi", "src", None, None),
        P("hi", "src", None, None, None),
    )
    return jax.shard_map(
        body,
        mesh=mesh,
        in_specs=placed,
        out_specs=(P(None, "hi", "src", None, None), P(None, None, "hi", "src", None)),
        check_vma=False,
    )
```

```python
import functools

import jax
import jax.numpy as jnp
from jax import lax
from jax.experimental import pallas as pl
from jax.experimental.pallas import tpu as pltpu
from jax.sharding import PartitionSpec as P

CHUNKS = 2
LANES = 128
BF = jnp.bfloat16
F32 = jnp.float32


def reverse_bits(value, bits):
    return int(format(value, f"0{bits}b")[::-1], 2)


def lane_block(shape, width):
    return lax.broadcasted_iota(jnp.int32, shape, len(shape) - 1) // width


def pick_lanes(product, rows, count, width):
    block = lane_block((rows, LANES), width)
    out = product[:rows]
    for b in range(1, count):
        out = jnp.where(block == b, product[b * rows:(b + 1) * rows], out)
    return out


def split_rows(pair):
    left = lane_block(pair.shape, LANES // 2) == 0
    zero = jnp.zeros(pair.shape, pair.dtype)
    return jnp.concatenate([jnp.where(left, pair, zero), jnp.where(left, zero, pair)], axis=0)


def halves_of(product, rows):
    first, second = product[:rows], product[rows:]
    left = lane_block((rows, LANES), LANES // 2) == 0
    low = jnp.where(left, first, pltpu.roll(second, LANES // 2, 1))
    high = jnp.where(left, pltpu.roll(first, LANES // 2, 1), second)
    return low, high


def is_high(level, src_bits):
    if level < src_bits:
        return (lax.axis_index("src") >> level & 1) == 1
    return (lax.axis_index("hi") >> (level - src_bits) & 1) == 1


def shear_x(device):
    return device ^ reverse_bits(device >> 4 & 3, 2) << 1


def shear_y(device):
    return device ^ reverse_bits(device >> 1 & 3, 2) << 4


def swap_ends(device):
    return device & 62 | device >> 6 | (device & 1) << 6


def first_hop(device):
    return shear_y(device)


def second_hop(device):
    return swap_ends(shear_y(shear_x(device)))


def dot(a, b):
    return jnp.dot(a, b, preferred_element_type=F32)


def dot_nt(a, b):
    return lax.dot_general(a, b, (((1,), (1,)), ((), ())), preferred_element_type=F32)


def leaf_kernel(chunk, traces, leaf, token, out, held, mats, sems, wide):
    vectors, boxes, points = held.shape
    lane_boxes = LANES // vectors
    rank = mats.shape[1]
    copies = [
        pltpu.make_async_copy(traces.at[pl.ds(chunk * vectors, vectors)], held, sems.at[0]),
        pltpu.make_async_copy(leaf, mats, sems.at[1]),
    ]
    for copy in copies:
        copy.start()
    copies[0].wait()
    wide[...] = held[...].astype(F32).reshape(wide.shape)
    copies[1].wait()
    for g in range(boxes // lane_boxes):
        rows = [
            wide[pl.ds(g * lane_boxes + b, vectors, stride=boxes), :] for b in range(lane_boxes)
        ]
        stacked = jnp.concatenate(rows, axis=0).astype(BF)
        group = mats[pl.ds(g * lane_boxes, lane_boxes)].reshape(lane_boxes * rank, points)
        out[g] = pick_lanes(dot_nt(group, stacked), rank, lane_boxes, vectors).astype(BF)


def forward_group(weights, stacked, lane_boxes, rank):
    mats = weights.reshape(lane_boxes * rank, LANES)
    return pick_lanes(dot(mats, stacked), rank, lane_boxes, LANES // lane_boxes).astype(BF)


def cross_step(own, other, mats, out, high, lane_boxes):
    groups, rank = own.shape[0], own.shape[1]
    for g in range(groups):
        mine, theirs = own[g], other[g]
        take = jnp.broadcast_to(high, mine.shape)
        lower = jnp.where(take, theirs, mine)
        upper = jnp.where(take, mine, theirs)
        stacked = jnp.concatenate([lower, upper], axis=0)
        weights = mats[pl.ds(g * lane_boxes, lane_boxes)]
        out[g] = forward_group(weights, stacked, lane_boxes, rank)


def cross_kernel(level, src_bits, lane_boxes, own, other, maps, *refs):
    mats = maps.at[level if maps.shape[0] > 1 else 0]
    cross_step(own, other, mats, refs[-1], is_high(level, src_bits), lane_boxes)


def local_forward(lane_boxes, maps, first, out, work):
    groups, rank = out.shape[0], out.shape[1]
    lane_bits = lane_boxes.bit_length() - 1
    box_bits = maps.shape[1].bit_length() - 1
    for bit in range(box_bits):
        mats = maps.at[first + bit]
        source = work.at[bit % 2]
        target = out if bit == box_bits - 1 else work.at[(bit + 1) % 2]
        if bit < lane_bits:
            shift = LANES // lane_boxes << bit
            for g in range(groups):
                value = source[g].astype(F32)
                is_set = (lane_block(value.shape, shift) & 1) == 1
                lower = jnp.where(is_set, pltpu.roll(value, shift, 1), value)
                upper = jnp.where(is_set, value, pltpu.roll(value, LANES - shift, 1))
                stacked = jnp.concatenate([lower, upper], axis=0).astype(BF)
                weights = mats[pl.ds(g * lane_boxes, lane_boxes)]
                target[g] = forward_group(weights, stacked, lane_boxes, rank)
        else:
            inner = 1 << bit - lane_bits
            for g0 in range(groups):
                if g0 & inner:
                    continue
                stacked = jnp.concatenate([source[g0], source[g0 + inner]], axis=0)
                for g in (g0, g0 + inner):
                    weights = mats[pl.ds(g * lane_boxes, lane_boxes)]
                    target[g] = forward_group(weights, stacked, lane_boxes, rank)


def target_kernel(chunk, coeffs, final, observed, token, *refs):
    residual, adjoint, held, sems, wide, result = refs[-6:]
    groups, rank = coeffs.shape[0], coeffs.shape[1]
    vectors, boxes, points = held.shape
    box_bits = boxes.bit_length() - 1
    lane_boxes = LANES // vectors
    own_rows = pl.ds(chunk * vectors, vectors)
    fetch = pltpu.make_async_copy(observed.at[own_rows], held, sems.at[0])
    fetch.start()
    fetch.wait()
    wide[...] = held[...].astype(F32).reshape(wide.shape)
    for g in range(groups):
        turned = jnp.transpose(coeffs[g].astype(F32)).astype(BF)
        for pair in range(lane_boxes // 2):
            kept, mats = [], []
            for b in (2 * pair, 2 * pair + 1):
                t = reverse_bits(g * lane_boxes + b, box_bits)
                mat = final[t]
                rows = pl.ds(t, vectors, stride=boxes)
                value = dot(turned[b * vectors:(b + 1) * vectors], mat) - wide[rows, :]
                result[rows, :] = value
                kept.append(value)
                mats.append(mat)
            rows = jnp.concatenate(kept, axis=0).astype(BF)
            product = dot_nt(rows, jnp.concatenate(mats, axis=0))
            adjoint[g * lane_boxes // 2 + pair] = pick_lanes(product, vectors, 2, rank).astype(BF)
    held[...] = result[...].reshape(held.shape).astype(BF)
    store = pltpu.make_async_copy(held, residual.at[own_rows], sems.at[1])
    store.start()
    store.wait()


def adjoint_cross_pair(value, mats, kept, sent, p, high):
    rows = value.shape[0]
    low, upper = halves_of(dot(split_rows(value), mats), rows)
    take = jnp.broadcast_to(high, low.shape)
    kept[p] = jnp.where(take, upper, low)
    sent[p] = jnp.where(take, low, upper).astype(BF)


def pair_rows(mats, p):
    rank = mats.shape[1]
    return mats[pl.ds(2 * p, 2)].reshape(2 * rank, LANES)


def local_forward_kernel(level, src_bits, lane_boxes, own, other, maps, token, coeffs, work):
    high = is_high(level, src_bits)
    cross_step(own, other, maps.at[level], work.at[0], high, lane_boxes)
    local_forward(lane_boxes, maps, level + 1, coeffs, work)


def local_adjoint_kernel(level, src_bits, adjoint, maps, token, kept, sent, work):
    pairs, vectors = work.shape[1], work.shape[2]
    box_bits = maps.shape[1].bit_length() - 1
    for step, bit in enumerate(reversed(range(box_bits))):
        mats = maps.at[level + 1 + bit]
        source = work.at[step % 2] if step else adjoint
        target = work.at[(step + 1) % 2]
        if bit == 0:
            for p in range(pairs):
                target[p] = dot(source[p], pair_rows(mats, p)).astype(BF)
        else:
            inner = 1 << bit - 1
            for p0 in range(pairs):
                if p0 & inner:
                    continue
                p1 = p0 + inner
                rows = jnp.concatenate([split_rows(source[p0]), split_rows(source[p1])], axis=1)
                stacked = jnp.concatenate([pair_rows(mats, p0), pair_rows(mats, p1)], axis=0)
                low, upper = halves_of(dot(rows, stacked), vectors)
                target[p0] = low.astype(BF)
                target[p1] = upper.astype(BF)
    source = work.at[box_bits % 2]
    high = is_high(level, src_bits)
    for p in range(pairs):
        adjoint_cross_pair(source[p], pair_rows(maps.at[level], p), kept, sent, p, high)


def adjoint_cross_kernel(level, src_bits, held_part, received, maps, *refs):
    kept, sent = refs[-2:]
    high = is_high(level, src_bits)
    for p in range(held_part.shape[0]):
        value = (held_part[p] + received[p].astype(F32)).astype(BF)
        adjoint_cross_pair(value, pair_rows(maps.at[level], p), kept, sent, p, high)


def gradient_kernel(chunk, held_part, received, leaf, *refs):
    gradient, held, sems, result = refs[-4:]
    pairs, vectors = held_part.shape[0], held_part.shape[1]
    boxes = leaf.shape[0]
    for p in range(pairs):
        value = (held_part[p] + received[p].astype(F32)).astype(BF)
        product = dot(split_rows(value), pair_rows(leaf, p))
        result[pl.ds(2 * p, vectors, stride=boxes), :] = product[:vectors]
        result[pl.ds(2 * p + 1, vectors, stride=boxes), :] = product[vectors:]
    held[...] = result[...].reshape(held.shape).astype(BF)
    store = pltpu.make_async_copy(
        held, gradient.at[pl.ds(chunk * vectors, vectors)], sems.at[0]
    )
    store.start()
    store.wait()


VMEM = pl.BlockSpec(memory_space=pltpu.VMEM)
ANY = pl.BlockSpec(memory_space=pl.ANY)
HBM = pl.BlockSpec(memory_space=pltpu.HBM)


def call(kernel, out_shape, in_specs, out_specs, scratch, flops, moved, limit, aliases=None):
    return pl.pallas_call(
        kernel,
        out_shape=out_shape,
        in_specs=in_specs,
        out_specs=out_specs,
        scratch_shapes=scratch,
        input_output_aliases=aliases or {},
        compiler_params=pltpu.CompilerParams(vmem_limit_bytes=limit << 20),
        cost_estimate=pl.CostEstimate(flops=flops, bytes_accessed=moved, transcendentals=0),
    )


def body(traces, observed, leaf_maps, level_maps, final_maps):
    total = traces.shape[0]
    boxes, points = traces.shape[1], traces.shape[4]
    rank = leaf_maps.shape[3]
    src_count, hi_count = lax.axis_size("src"), lax.axis_size("hi")
    src_bits = src_count.bit_length() - 1
    hi_bits = hi_count.bit_length() - 1
    device_bits = src_bits + hi_bits
    box_bits = boxes.bit_length() - 1
    vectors = total // CHUNKS
    lane_boxes = LANES // vectors
    groups, pairs = boxes // lane_boxes, boxes // 2

    leaf = leaf_maps.reshape(boxes, rank, points)
    final = final_maps.reshape(boxes, rank, points)
    levels = level_maps.reshape(level_maps.shape[0], boxes, rank, 2 * rank)
    samples = traces.reshape(total, boxes, points)
    wanted = observed.reshape(total, boxes, points)

    def shape(*dims, dtype=BF):
        return jax.ShapeDtypeStruct(dims, dtype)

    forward_shape = shape(groups, rank, LANES)
    pair_shape = shape(pairs, vectors, LANES)
    kept_shape = shape(pairs, vectors, LANES, dtype=F32)
    sample_shape = shape(vectors, boxes, points)
    full_shape = shape(total, boxes, points)
    wide = pltpu.VMEM((vectors * boxes, points), F32)
    held = pltpu.VMEM((vectors, boxes, points), BF)
    sems = pltpu.SemaphoreType.DMA((2,))
    flops = 2 * boxes * rank * 2 * rank * vectors
    moved = boxes * rank * 2 * rank * 2

    def exchange(array, level):
        if level < src_bits:
            axis, count, bit = "src", src_count, level
        else:
            axis, count, bit = "hi", hi_count, level - src_bits
        return lax.ppermute(array, axis, [(i, i ^ 1 << bit) for i in range(count)])

    def move(array, route):
        pairs_of = []
        for src in range(src_count):
            for hi in range(hi_count):
                there = route(hi * src_count + src)
                pairs_of.append(
                    (src * hi_count + hi, there % src_count * hi_count + there // src_count)
                )
        return lax.ppermute(array, ("src", "hi"), pairs_of)

    def reversal(array):
        return move(move(array, first_hop), second_hop)

    for device in range(src_count * hi_count):
        assert second_hop(first_hop(device)) == reverse_bits(device, device_bits)

    def leaf_call(chunk):
        kernel = functools.partial(leaf_kernel, chunk)
        scratch = [held, pltpu.VMEM((boxes, rank, points), BF), sems, wide]
        return call(kernel, forward_shape, [HBM, HBM, ANY], VMEM, scratch, flops, 2 * moved, 8)

    def target_call(chunk, *operands):
        kernel = functools.partial(target_kernel, chunk)
        specs = [VMEM, VMEM, HBM, ANY] + [HBM] * (len(operands) - 4)
        return call(
            kernel, (full_shape, pair_shape), specs, (HBM, VMEM), [held, sems, wide, wide],
            2 * flops, 4 * moved, 8, {4: 0} if len(operands) > 4 else None,
        )(*operands)

    def gradient_call(chunk, *operands):
        kernel = functools.partial(gradient_kernel, chunk)
        specs = [VMEM] * 3 + [HBM] * (len(operands) - 3)
        return call(
            kernel, full_shape, specs, HBM, [held, sems, wide],
            flops, 2 * moved, 8, {3: 0} if len(operands) > 3 else None,
        )(*operands)

    def cross_call(level, *operands):
        kernel = functools.partial(cross_kernel, level, src_bits, lane_boxes)
        specs = [VMEM] * 3 + [ANY] * (len(operands) - 3)
        return call(kernel, forward_shape, specs, VMEM, [], flops, moved, 4)(*operands)

    def adjoint_call(level, *operands):
        kernel = functools.partial(adjoint_cross_kernel, level, src_bits)
        specs = [VMEM] * 3 + [ANY] * (len(operands) - 3)
        return call(
            kernel, (kept_shape, pair_shape), specs, (VMEM, VMEM), [], flops, moved, 4
        )(*operands)

    def local_forward_call(*operands):
        kernel = functools.partial(local_forward_kernel, top, src_bits, lane_boxes)
        scratch = [pltpu.VMEM((2, groups, rank, LANES), BF)]
        return call(
            kernel, forward_shape, [VMEM] * 3 + [ANY], VMEM, scratch, 7 * flops, 7 * moved, 8
        )(*operands)

    def local_adjoint_call(*operands):
        kernel = functools.partial(local_adjoint_kernel, top, src_bits)
        scratch = [pltpu.VMEM((2, pairs, vectors, LANES), BF)]
        return call(
            kernel, (kept_shape, pair_shape), [VMEM] * 2 + [ANY], (VMEM, VMEM), scratch,
            7 * flops, 7 * moved, 8,
        )(*operands)

    top = device_bits - 1
    every = range(CHUNKS)
    coeffs, kept, sent = [None] * CHUNKS, [None] * CHUNKS, [None] * CHUNKS
    token = leaf
    for c in every:
        coeffs[c] = token = leaf_call(c)(samples, leaf, token)
    for level in range(top):
        maps = levels[level:level + 1] if level < 2 else levels
        for c in every:
            coeffs[c] = token = cross_call(
                level, coeffs[c], exchange(coeffs[c], level), maps, token
            )
    for c in every:
        coeffs[c] = token = local_forward_call(
            coeffs[c], exchange(coeffs[c], top), levels, token
        )
    residual = ()
    for c in every:
        *residual, sent[c] = target_call(c, reversal(coeffs[c]), final, wanted, token, *residual)
        token = sent[c]
    for c in every:
        kept[c], sent[c] = local_adjoint_call(reversal(sent[c]), levels, token)
        token = sent[c]
    for level in reversed(range(top)):
        for c in every:
            kept[c], sent[c] = adjoint_call(
                level, kept[c], exchange(sent[c], level + 1), levels, token
            )
            token = sent[c]
    residual = residual[0]
    gradient = ()
    for c in every:
        gradient = [gradient_call(c, kept[c], exchange(sent[c], 0), leaf, *gradient)]
    gradient = gradient[0]
    return (
        residual.reshape(total, 1, 1, boxes, points),
        gradient.reshape(total, boxes, 1, 1, points),
    )


def solution(mesh):
    placed = (
        P(None, None, "hi", "src", None),
        P(None, "hi", "src", None, None),
        P(None, "hi", "src", None, None),
        P(None, None, "hi", "src", None, None),
        P("hi", "src", None, None, None),
    )
    return jax.shard_map(
        body,
        mesh=mesh,
        in_specs=placed,
        out_specs=(P(None, "hi", "src", None, None), P(None, None, "hi", "src", None)),
        check_vma=False,
    )
```

```python
import functools

import jax
import jax.numpy as jnp
from jax import lax
from jax.experimental import pallas as pl
from jax.experimental.pallas import tpu as pltpu
from jax.sharding import PartitionSpec as P

CHUNKS = 2
LANES = 128
BF = jnp.bfloat16
F32 = jnp.float32


def reverse_bits(value, bits):
    return int(format(value, f"0{bits}b")[::-1], 2)


def lane_block(shape, width):
    return lax.broadcasted_iota(jnp.int32, shape, len(shape) - 1) // width


def pick_lanes(product, rows, count, width):
    block = lane_block((rows, LANES), width)
    out = product[:rows]
    for b in range(1, count):
        out = jnp.where(block == b, product[b * rows:(b + 1) * rows], out)
    return out


def split_rows(pair):
    left = lane_block(pair.shape, LANES // 2) == 0
    zero = jnp.zeros(pair.shape, pair.dtype)
    return jnp.concatenate([jnp.where(left, pair, zero), jnp.where(left, zero, pair)], axis=0)


def halves_of(product, rows):
    first, second = product[:rows], product[rows:]
    left = lane_block((rows, LANES), LANES // 2) == 0
    low = jnp.where(left, first, pltpu.roll(second, LANES // 2, 1))
    high = jnp.where(left, pltpu.roll(first, LANES // 2, 1), second)
    return low, high


def is_high(level, src_bits):
    if level < src_bits:
        return (lax.axis_index("src") >> level & 1) == 1
    return (lax.axis_index("hi") >> (level - src_bits) & 1) == 1


def dot(a, b):
    return jnp.dot(a, b, preferred_element_type=F32)


def dot_nt(a, b):
    return lax.dot_general(a, b, (((1,), (1,)), ((), ())), preferred_element_type=F32)


def leaf_kernel(chunk, traces, leaf, token, out, held, mats, sems, wide):
    vectors, boxes, points = held.shape
    lane_boxes = LANES // vectors
    rank = mats.shape[1]
    copies = [
        pltpu.make_async_copy(traces.at[pl.ds(chunk * vectors, vectors)], held, sems.at[0]),
        pltpu.make_async_copy(leaf, mats, sems.at[1]),
    ]
    for copy in copies:
        copy.start()
    copies[0].wait()
    wide[...] = held[...].astype(F32).reshape(wide.shape)
    copies[1].wait()
    for g in range(boxes // lane_boxes):
        rows = [
            wide[pl.ds(g * lane_boxes + b, vectors, stride=boxes), :] for b in range(lane_boxes)
        ]
        stacked = jnp.concatenate(rows, axis=0).astype(BF)
        group = mats[pl.ds(g * lane_boxes, lane_boxes)].reshape(lane_boxes * rank, points)
        out[g] = pick_lanes(dot_nt(group, stacked), rank, lane_boxes, vectors).astype(BF)


def forward_group(weights, stacked, lane_boxes, rank):
    mats = weights.reshape(lane_boxes * rank, LANES)
    return pick_lanes(dot(mats, stacked), rank, lane_boxes, LANES // lane_boxes).astype(BF)


def cross_step(own, other, mats, out, high, lane_boxes):
    groups, rank = own.shape[0], own.shape[1]
    for g in range(groups):
        mine, theirs = own[g], other[g]
        take = jnp.broadcast_to(high, mine.shape)
        lower = jnp.where(take, theirs, mine)
        upper = jnp.where(take, mine, theirs)
        stacked = jnp.concatenate([lower, upper], axis=0)
        weights = mats[pl.ds(g * lane_boxes, lane_boxes)]
        out[g] = forward_group(weights, stacked, lane_boxes, rank)


def cross_kernel(level, src_bits, lane_boxes, own, other, maps, *refs):
    mats = maps.at[level if maps.shape[0] > 1 else 0]
    cross_step(own, other, mats, refs[-1], is_high(level, src_bits), lane_boxes)


def local_forward(lane_boxes, maps, first, out, work):
    groups, rank = out.shape[0], out.shape[1]
    lane_bits = lane_boxes.bit_length() - 1
    box_bits = maps.shape[1].bit_length() - 1
    for bit in range(box_bits):
        mats = maps.at[first + bit]
        source = work.at[bit % 2]
        target = out if bit == box_bits - 1 else work.at[(bit + 1) % 2]
        if bit < lane_bits:
            shift = LANES // lane_boxes << bit
            for g in range(groups):
                value = source[g].astype(F32)
                is_set = (lane_block(value.shape, shift) & 1) == 1
                lower = jnp.where(is_set, pltpu.roll(value, shift, 1), value)
                upper = jnp.where(is_set, value, pltpu.roll(value, LANES - shift, 1))
                stacked = jnp.concatenate([lower, upper], axis=0).astype(BF)
                weights = mats[pl.ds(g * lane_boxes, lane_boxes)]
                target[g] = forward_group(weights, stacked, lane_boxes, rank)
        else:
            inner = 1 << bit - lane_bits
            for g0 in range(groups):
                if g0 & inner:
                    continue
                stacked = jnp.concatenate([source[g0], source[g0 + inner]], axis=0)
                for g in (g0, g0 + inner):
                    weights = mats[pl.ds(g * lane_boxes, lane_boxes)]
                    target[g] = forward_group(weights, stacked, lane_boxes, rank)


def order_kernel(observed, token, out, held, sems, wide):
    total, boxes, points = held.shape
    fetch = pltpu.make_async_copy(observed, held, sems.at[0])
    fetch.start()
    fetch.wait()
    wide[...] = held[...].astype(F32).reshape(wide.shape)
    for t in range(boxes):
        out[t] = wide[pl.ds(t, total, stride=boxes), :].astype(BF)


def target_kernel(chunk, coeffs, final, wanted, token, residual, adjoint):
    groups, rank = coeffs.shape[0], coeffs.shape[1]
    boxes, vectors = residual.shape[0], residual.shape[1]
    box_bits = boxes.bit_length() - 1
    lane_boxes = LANES // vectors
    for g in range(groups):
        turned = jnp.transpose(coeffs[g].astype(F32)).astype(BF)
        for pair in range(lane_boxes // 2):
            kept, mats = [], []
            for b in (2 * pair, 2 * pair + 1):
                t = reverse_bits(g * lane_boxes + b, box_bits)
                mat = final[t]
                value = dot(turned[b * vectors:(b + 1) * vectors], mat)
                target = wanted[t, pl.ds(chunk * vectors, vectors), :].astype(F32)
                value = (value - target).astype(BF)
                residual[t] = value
                kept.append(value)
                mats.append(mat)
            product = dot_nt(jnp.concatenate(kept, axis=0), jnp.concatenate(mats, axis=0))
            adjoint[g * lane_boxes // 2 + pair] = pick_lanes(product, vectors, 2, rank).astype(BF)


def residual_kernel(chunks, *refs):
    parts = refs[:chunks]
    token, residual, done, held, sems, wide = refs[chunks:]
    boxes, vectors = parts[0].shape[0], parts[0].shape[1]
    for t in range(boxes):
        rows = jnp.concatenate([part[t].astype(F32) for part in parts], axis=0)
        wide[pl.ds(t, chunks * vectors, stride=boxes), :] = rows
    held[...] = wide[...].reshape(held.shape).astype(BF)
    done[...] = jnp.zeros(done.shape, done.dtype)
    store = pltpu.make_async_copy(held, residual, sems.at[0])
    store.start()
    store.wait()


def adjoint_cross_pair(value, mats, kept, sent, p, high):
    rows = value.shape[0]
    low, upper = halves_of(dot(split_rows(value), mats), rows)
    take = jnp.broadcast_to(high, low.shape)
    kept[p] = jnp.where(take, upper, low)
    sent[p] = jnp.where(take, low, upper).astype(BF)


def pair_rows(mats, p):
    rank = mats.shape[1]
    return mats[pl.ds(2 * p, 2)].reshape(2 * rank, LANES)


def local_forward_kernel(level, src_bits, lane_boxes, own, other, maps, token, coeffs, work):
    high = is_high(level, src_bits)
    cross_step(own, other, maps.at[level], work.at[0], high, lane_boxes)
    local_forward(lane_boxes, maps, level + 1, coeffs, work)


def local_adjoint_kernel(level, src_bits, adjoint, maps, token, kept, sent, work):
    pairs, vectors = work.shape[1], work.shape[2]
    box_bits = maps.shape[1].bit_length() - 1
    for step, bit in enumerate(reversed(range(box_bits))):
        mats = maps.at[level + 1 + bit]
        source = work.at[step % 2] if step else adjoint
        target = work.at[(step + 1) % 2]
        if bit == 0:
            for p in range(pairs):
                target[p] = dot(source[p], pair_rows(mats, p)).astype(BF)
        else:
            inner = 1 << bit - 1
            for p0 in range(pairs):
                if p0 & inner:
                    continue
                p1 = p0 + inner
                rows = jnp.concatenate([split_rows(source[p0]), split_rows(source[p1])], axis=1)
                stacked = jnp.concatenate([pair_rows(mats, p0), pair_rows(mats, p1)], axis=0)
                low, upper = halves_of(dot(rows, stacked), vectors)
                target[p0] = low.astype(BF)
                target[p1] = upper.astype(BF)
    source = work.at[box_bits % 2]
    high = is_high(level, src_bits)
    for p in range(pairs):
        adjoint_cross_pair(source[p], pair_rows(maps.at[level], p), kept, sent, p, high)


def adjoint_cross_kernel(level, src_bits, held_part, received, maps, *refs):
    kept, sent = refs[-2:]
    high = is_high(level, src_bits)
    for p in range(held_part.shape[0]):
        value = (held_part[p] + received[p].astype(F32)).astype(BF)
        adjoint_cross_pair(value, pair_rows(maps.at[level], p), kept, sent, p, high)


def gradient_kernel(chunk, held_part, received, leaf, *refs):
    gradient, held, sems, result = refs[-4:]
    pairs, vectors = held_part.shape[0], held_part.shape[1]
    boxes = leaf.shape[0]
    for p in range(pairs):
        value = (held_part[p] + received[p].astype(F32)).astype(BF)
        product = dot(split_rows(value), pair_rows(leaf, p))
        result[pl.ds(2 * p, vectors, stride=boxes), :] = product[:vectors]
        result[pl.ds(2 * p + 1, vectors, stride=boxes), :] = product[vectors:]
    held[...] = result[...].reshape(held.shape).astype(BF)
    store = pltpu.make_async_copy(
        held, gradient.at[pl.ds(chunk * vectors, vectors)], sems.at[0]
    )
    store.start()
    store.wait()


VMEM = pl.BlockSpec(memory_space=pltpu.VMEM)
ANY = pl.BlockSpec(memory_space=pl.ANY)
HBM = pl.BlockSpec(memory_space=pltpu.HBM)


def call(kernel, out_shape, in_specs, out_specs, scratch, flops, moved, limit, aliases=None):
    return pl.pallas_call(
        kernel,
        out_shape=out_shape,
        in_specs=in_specs,
        out_specs=out_specs,
        scratch_shapes=scratch,
        input_output_aliases=aliases or {},
        compiler_params=pltpu.CompilerParams(vmem_limit_bytes=limit << 20),
        cost_estimate=pl.CostEstimate(flops=flops, bytes_accessed=moved, transcendentals=0),
    )


def body(traces, observed, leaf_maps, level_maps, final_maps):
    total = traces.shape[0]
    boxes, points = traces.shape[1], traces.shape[4]
    rank = leaf_maps.shape[3]
    src_count, hi_count = lax.axis_size("src"), lax.axis_size("hi")
    src_bits = src_count.bit_length() - 1
    hi_bits = hi_count.bit_length() - 1
    device_bits = src_bits + hi_bits
    box_bits = boxes.bit_length() - 1
    vectors = total // CHUNKS
    lane_boxes = LANES // vectors
    groups, pairs = boxes // lane_boxes, boxes // 2

    leaf = leaf_maps.reshape(boxes, rank, points)
    final = final_maps.reshape(boxes, rank, points)
    levels = level_maps.reshape(level_maps.shape[0], boxes, rank, 2 * rank)
    samples = traces.reshape(total, boxes, points)
    wanted = observed.reshape(total, boxes, points)

    def shape(*dims, dtype=BF):
        return jax.ShapeDtypeStruct(dims, dtype)

    forward_shape = shape(groups, rank, LANES)
    pair_shape = shape(pairs, vectors, LANES)
    kept_shape = shape(pairs, vectors, LANES, dtype=F32)
    sample_shape = shape(vectors, boxes, points)
    full_shape = shape(total, boxes, points)
    wide = pltpu.VMEM((vectors * boxes, points), F32)
    held = pltpu.VMEM((vectors, boxes, points), BF)
    sems = pltpu.SemaphoreType.DMA((2,))
    flops = 2 * boxes * rank * 2 * rank * vectors
    moved = boxes * rank * 2 * rank * 2

    def exchange(array, level):
        if level < src_bits:
            axis, count, bit = "src", src_count, level
        else:
            axis, count, bit = "hi", hi_count, level - src_bits
        return lax.ppermute(array, axis, [(i, i ^ 1 << bit) for i in range(count)])

    def reversal(array):
        pairs_of = []
        for src in range(src_count):
            for hi in range(hi_count):
                there = reverse_bits(hi * src_count + src, device_bits)
                pairs_of.append(
                    (src * hi_count + hi, there % src_count * hi_count + there // src_count)
                )
        return lax.ppermute(array, ("src", "hi"), pairs_of)

    def leaf_call(chunk):
        kernel = functools.partial(leaf_kernel, chunk)
        scratch = [held, pltpu.VMEM((boxes, rank, points), BF), sems, wide]
        return call(kernel, forward_shape, [HBM, HBM, ANY], VMEM, scratch, flops, 2 * moved, 8)

    whole = [
        pltpu.VMEM((total, boxes, points), BF), sems, pltpu.VMEM((total * boxes, points), F32)
    ]

    def order_call(*operands):
        return call(
            order_kernel, shape(boxes, total, points), [HBM, ANY], VMEM, whole, 0, 2 * moved, 8
        )(*operands)

    def target_call(chunk, *operands):
        kernel = functools.partial(target_kernel, chunk)
        return call(
            kernel, (shape(boxes, vectors, points), pair_shape), [VMEM] * 3 + [ANY],
            (VMEM, VMEM), [], 2 * flops, 4 * moved, 8,
        )(*operands)

    def residual_call(*operands):
        return call(
            functools.partial(residual_kernel, CHUNKS), (full_shape, shape(8, LANES, dtype=F32)),
            [VMEM] * CHUNKS + [ANY], (HBM, VMEM), whole, 0, 2 * moved, 8,
        )(*operands)

    def gradient_call(chunk, *operands):
        kernel = functools.partial(gradient_kernel, chunk)
        specs = [VMEM] * 3 + [HBM] * (len(operands) - 3)
        return call(
            kernel, full_shape, specs, HBM, [held, sems, wide],
            flops, 2 * moved, 8, {3: 0} if len(operands) > 3 else None,
        )(*operands)

    def cross_call(level, *operands):
        kernel = functools.partial(cross_kernel, level, src_bits, lane_boxes)
        specs = [VMEM] * 3 + [ANY] * (len(operands) - 3)
        return call(kernel, forward_shape, specs, VMEM, [], flops, moved, 4)(*operands)

    def adjoint_call(level, *operands):
        kernel = functools.partial(adjoint_cross_kernel, level, src_bits)
        specs = [VMEM] * 3 + [ANY] * (len(operands) - 3)
        return call(
            kernel, (kept_shape, pair_shape), specs, (VMEM, VMEM), [], flops, moved, 4
        )(*operands)

    def local_forward_call(*operands):
        kernel = functools.partial(local_forward_kernel, top, src_bits, lane_boxes)
        scratch = [pltpu.VMEM((2, groups, rank, LANES), BF)]
        return call(
            kernel, forward_shape, [VMEM] * 3 + [ANY], VMEM, scratch, 7 * flops, 7 * moved, 8
        )(*operands)

    def local_adjoint_call(*operands):
        kernel = functools.partial(local_adjoint_kernel, top, src_bits)
        scratch = [pltpu.VMEM((2, pairs, vectors, LANES), BF)]
        return call(
            kernel, (kept_shape, pair_shape), [VMEM] * 2 + [ANY], (VMEM, VMEM), scratch,
            7 * flops, 7 * moved, 8,
        )(*operands)

    top = device_bits - 1
    every = range(CHUNKS)
    coeffs, kept, sent = [None] * CHUNKS, [None] * CHUNKS, [None] * CHUNKS
    token = leaf
    for c in every:
        coeffs[c] = token = leaf_call(c)(samples, leaf, token)
    for level in range(top):
        maps = levels[level:level + 1] if level < 2 else levels
        for c in every:
            coeffs[c] = token = cross_call(
                level, coeffs[c], exchange(coeffs[c], level), maps, token
            )
        if level == 2:
            wanted = token = order_call(wanted, token)
    for c in every:
        coeffs[c] = token = local_forward_call(
            coeffs[c], exchange(coeffs[c], top), levels, token
        )
    residual = [None] * CHUNKS
    for c in every:
        residual[c], sent[c] = target_call(c, reversal(coeffs[c]), final, wanted, token)
        token = sent[c]
    for c in every:
        kept[c], sent[c] = local_adjoint_call(reversal(sent[c]), levels, token)
        token = sent[c]
    for level in reversed(range(top)):
        for c in every:
            kept[c], sent[c] = adjoint_call(
                level, kept[c], exchange(sent[c], level + 1), levels, token
            )
            token = sent[c]
        if level == top - 2:
            residual, token = residual_call(*residual, token)
    gradient = ()
    for c in every:
        gradient = [gradient_call(c, kept[c], exchange(sent[c], 0), leaf, *gradient)]
    gradient = gradient[0]
    return (
        residual.reshape(total, 1, 1, boxes, points),
        gradient.reshape(total, boxes, 1, 1, points),
    )


def solution(mesh):
    placed = (
        P(None, None, "hi", "src", None),
        P(None, "hi", "src", None, None),
        P(None, "hi", "src", None, None),
        P(None, None, "hi", "src", None, None),
        P("hi", "src", None, None, None),
    )
    return jax.shard_map(
        body,
        mesh=mesh,
        in_specs=placed,
        out_specs=(P(None, "hi", "src", None, None), P(None, None, "hi", "src", None)),
        check_vma=False,
    )
```

```python
import functools

import jax
import jax.numpy as jnp
from jax import lax
from jax.experimental import pallas as pl
from jax.experimental.pallas import tpu as pltpu
from jax.sharding import PartitionSpec as P

CHUNKS = 2
PARTS = 4
EARLY = 2
LAG = 0
GAP = 2
LANES = 128
BF = jnp.bfloat16
F32 = jnp.float32


def reverse_bits(value, bits):
    return int(format(value, f"0{bits}b")[::-1], 2)


def lane_block(shape, width):
    return lax.broadcasted_iota(jnp.int32, shape, len(shape) - 1) // width


def pick_lanes(product, rows, count, width):
    block = lane_block((rows, LANES), width)
    out = product[:rows]
    for b in range(1, count):
        out = jnp.where(block == b, product[b * rows:(b + 1) * rows], out)
    return out


def split_rows(pair):
    left = lane_block(pair.shape, LANES // 2) == 0
    zero = jnp.zeros(pair.shape, pair.dtype)
    return jnp.concatenate([jnp.where(left, pair, zero), jnp.where(left, zero, pair)], axis=0)


def halves_of(product, rows):
    first, second = product[:rows], product[rows:]
    left = lane_block((rows, LANES), LANES // 2) == 0
    low = jnp.where(left, first, pltpu.roll(second, LANES // 2, 1))
    high = jnp.where(left, pltpu.roll(first, LANES // 2, 1), second)
    return low, high


def is_high(level, src_bits):
    if level < src_bits:
        return (lax.axis_index("src") >> level & 1) == 1
    return (lax.axis_index("hi") >> (level - src_bits) & 1) == 1


def dot(a, b):
    return jnp.dot(a, b, preferred_element_type=F32)


def dot_nt(a, b):
    return lax.dot_general(a, b, (((1,), (1,)), ((), ())), preferred_element_type=F32)


def leaf_kernel(chunks, traces, leaf, *refs):
    outs = refs[:chunks]
    held, mats, sems, wide = refs[chunks:]
    total, boxes, points = held.shape
    vectors = total // chunks
    lane_boxes = LANES // vectors
    rank = mats.shape[1]
    copies = [
        pltpu.make_async_copy(
            traces.at[pl.ds(c * vectors, vectors)], held.at[pl.ds(c * vectors, vectors)], sems.at[c]
        )
        for c in range(chunks)
    ]
    copies.append(pltpu.make_async_copy(leaf, mats, sems.at[chunks]))
    for copy in copies:
        copy.start()
    for c in range(chunks):
        copies[c].wait()
        rows = held[pl.ds(c * vectors, vectors)].astype(F32)
        wide[...] = rows.reshape(wide.shape)
        if c == 0:
            copies[chunks].wait()
        for g in range(boxes // lane_boxes):
            rows = [
                wide[pl.ds(g * lane_boxes + b, vectors, stride=boxes), :]
                for b in range(lane_boxes)
            ]
            stacked = jnp.concatenate(rows, axis=0).astype(BF)
            group = mats[pl.ds(g * lane_boxes, lane_boxes)].reshape(lane_boxes * rank, points)
            outs[c][g] = pick_lanes(dot_nt(group, stacked), rank, lane_boxes, vectors).astype(BF)


def forward_group(weights, stacked, lane_boxes, rank):
    mats = weights.reshape(lane_boxes * rank, LANES)
    return pick_lanes(dot(mats, stacked), rank, lane_boxes, LANES // lane_boxes).astype(BF)


def cross_step(own, other, mats, out, high, lane_boxes):
    groups, rank = own.shape[0], own.shape[1]
    for g in range(groups):
        mine, theirs = own[g], other[g]
        take = jnp.broadcast_to(high, mine.shape)
        lower = jnp.where(take, theirs, mine)
        upper = jnp.where(take, mine, theirs)
        stacked = jnp.concatenate([lower, upper], axis=0)
        weights = mats[pl.ds(g * lane_boxes, lane_boxes)]
        out[g] = forward_group(weights, stacked, lane_boxes, rank)


def cross_kernel(level, src_bits, lane_boxes, own, other, maps, *refs):
    mats = maps.at[level if maps.shape[0] > 1 else 0]
    cross_step(own, other, mats, refs[-1], is_high(level, src_bits), lane_boxes)


def local_forward(lane_boxes, maps, first, out, work):
    groups, rank = out.shape[0], out.shape[1]
    lane_bits = lane_boxes.bit_length() - 1
    box_bits = maps.shape[1].bit_length() - 1
    for bit in range(box_bits):
        mats = maps.at[first + bit]
        source = work.at[bit % 2]
        target = out if bit == box_bits - 1 else work.at[(bit + 1) % 2]
        if bit < lane_bits:
            shift = LANES // lane_boxes << bit
            for g in range(groups):
                value = source[g].astype(F32)
                is_set = (lane_block(value.shape, shift) & 1) == 1
                lower = jnp.where(is_set, pltpu.roll(value, shift, 1), value)
                upper = jnp.where(is_set, value, pltpu.roll(value, LANES - shift, 1))
                stacked = jnp.concatenate([lower, upper], axis=0).astype(BF)
                weights = mats[pl.ds(g * lane_boxes, lane_boxes)]
                target[g] = forward_group(weights, stacked, lane_boxes, rank)
        else:
            inner = 1 << bit - lane_bits
            for g0 in range(groups):
                if g0 & inner:
                    continue
                stacked = jnp.concatenate([source[g0], source[g0 + inner]], axis=0)
                for g in (g0, g0 + inner):
                    weights = mats[pl.ds(g * lane_boxes, lane_boxes)]
                    target[g] = forward_group(weights, stacked, lane_boxes, rank)


def order_kernel(observed, token, out, held, sems, wide):
    total, boxes, points = held.shape
    fetch = pltpu.make_async_copy(observed, held, sems.at[0])
    fetch.start()
    fetch.wait()
    wide[...] = held[...].astype(F32).reshape(wide.shape)
    for t in range(boxes):
        out[t] = wide[pl.ds(t, total, stride=boxes), :].astype(BF)


def target_kernel(chunk, coeffs, final, wanted, token, residual, adjoint):
    groups, rank = coeffs.shape[0], coeffs.shape[1]
    boxes, vectors = residual.shape[0], residual.shape[1]
    box_bits = boxes.bit_length() - 1
    lane_boxes = LANES // vectors
    for g in range(groups):
        turned = jnp.transpose(coeffs[g].astype(F32)).astype(BF)
        for pair in range(lane_boxes // 2):
            kept, mats = [], []
            for b in (2 * pair, 2 * pair + 1):
                t = reverse_bits(g * lane_boxes + b, box_bits)
                mat = final[t]
                value = dot(turned[b * vectors:(b + 1) * vectors], mat)
                target = wanted[t, pl.ds(chunk * vectors, vectors), :].astype(F32)
                value = (value - target).astype(BF)
                residual[t] = value
                kept.append(value)
                mats.append(mat)
            product = dot_nt(jnp.concatenate(kept, axis=0), jnp.concatenate(mats, axis=0))
            adjoint[g * lane_boxes // 2 + pair] = pick_lanes(product, vectors, 2, rank).astype(BF)


def residual_kernel(chunk, part, token, *refs):
    residual, done, held, sems, wide = refs[-5:]
    boxes, vectors = part.shape[0], part.shape[1]
    for t in range(boxes):
        wide[pl.ds(t, vectors, stride=boxes), :] = part[t].astype(F32)
    held[...] = wide[...].reshape(held.shape).astype(BF)
    done[...] = jnp.zeros(done.shape, done.dtype)
    store = pltpu.make_async_copy(
        held, residual.at[pl.ds(chunk * vectors, vectors)], sems.at[0]
    )
    store.start()
    store.wait()


def adjoint_cross_pair(value, mats, kept, sent, p, high):
    rows = value.shape[0]
    low, upper = halves_of(dot(split_rows(value), mats), rows)
    take = jnp.broadcast_to(high, low.shape)
    kept[p] = jnp.where(take, upper, low)
    sent[p] = jnp.where(take, low, upper).astype(BF)


def pair_rows(mats, p):
    rank = mats.shape[1]
    return mats[pl.ds(2 * p, 2)].reshape(2 * rank, LANES)


def local_forward_kernel(level, src_bits, lane_boxes, own, other, maps, token, coeffs, work):
    high = is_high(level, src_bits)
    cross_step(own, other, maps.at[level], work.at[0], high, lane_boxes)
    local_forward(lane_boxes, maps, level + 1, coeffs, work)


def local_adjoint_kernel(level, src_bits, adjoint, maps, token, kept, sent, work):
    pairs, vectors = work.shape[1], work.shape[2]
    box_bits = maps.shape[1].bit_length() - 1
    for step, bit in enumerate(reversed(range(box_bits))):
        mats = maps.at[level + 1 + bit]
        source = work.at[step % 2] if step else adjoint
        target = work.at[(step + 1) % 2]
        if bit == 0:
            for p in range(pairs):
                target[p] = dot(source[p], pair_rows(mats, p)).astype(BF)
        else:
            inner = 1 << bit - 1
            for p0 in range(pairs):
                if p0 & inner:
                    continue
                p1 = p0 + inner
                rows = jnp.concatenate([split_rows(source[p0]), split_rows(source[p1])], axis=1)
                stacked = jnp.concatenate([pair_rows(mats, p0), pair_rows(mats, p1)], axis=0)
                low, upper = halves_of(dot(rows, stacked), vectors)
                target[p0] = low.astype(BF)
                target[p1] = upper.astype(BF)
    source = work.at[box_bits % 2]
    high = is_high(level, src_bits)
    for p in range(pairs):
        adjoint_cross_pair(source[p], pair_rows(maps.at[level], p), kept, sent, p, high)


def adjoint_cross_kernel(level, src_bits, held_part, received, maps, *refs):
    kept, sent = refs[-2:]
    high = is_high(level, src_bits)
    for p in range(held_part.shape[0]):
        value = (held_part[p] + received[p].astype(F32)).astype(BF)
        adjoint_cross_pair(value, pair_rows(maps.at[level], p), kept, sent, p, high)


def gradient_kernel(chunk, held_part, received, leaf, *refs):
    gradient, held, sems, result = refs[-4:]
    pairs, vectors = held_part.shape[0], held_part.shape[1]
    boxes, points = held.shape[1], held.shape[2]
    stores = []
    for part in range(PARTS):
        for p in range(part * pairs // PARTS, (part + 1) * pairs // PARTS):
            value = (held_part[p] + received[p].astype(F32)).astype(BF)
            product = dot(split_rows(value), pair_rows(leaf, p))
            result[pl.ds(2 * p, vectors, stride=boxes), :] = product[:vectors]
            result[pl.ds(2 * p + 1, vectors, stride=boxes), :] = product[vectors:]
        own = pl.ds(part * boxes // PARTS, boxes // PARTS)
        for v in range(vectors):
            rows = result[pl.ds(v * boxes + part * boxes // PARTS, boxes // PARTS), :]
            held[v, own, :] = rows.astype(BF)
        store = pltpu.make_async_copy(
            held.at[:, own, :],
            gradient.at[pl.ds(chunk * vectors, vectors), own, :],
            sems.at[part],
        )
        store.start()
        stores.append(store)
    for store in stores:
        store.wait()


VMEM = pl.BlockSpec(memory_space=pltpu.VMEM)
ANY = pl.BlockSpec(memory_space=pl.ANY)
HBM = pl.BlockSpec(memory_space=pltpu.HBM)


def call(kernel, out_shape, in_specs, out_specs, scratch, flops, moved, limit, aliases=None):
    return pl.pallas_call(
        kernel,
        out_shape=out_shape,
        in_specs=in_specs,
        out_specs=out_specs,
        scratch_shapes=scratch,
        input_output_aliases=aliases or {},
        compiler_params=pltpu.CompilerParams(vmem_limit_bytes=limit << 20),
        cost_estimate=pl.CostEstimate(flops=flops, bytes_accessed=moved, transcendentals=0),
    )


def body(traces, observed, leaf_maps, level_maps, final_maps):
    total = traces.shape[0]
    boxes, points = traces.shape[1], traces.shape[4]
    rank = leaf_maps.shape[3]
    src_count, hi_count = lax.axis_size("src"), lax.axis_size("hi")
    src_bits = src_count.bit_length() - 1
    hi_bits = hi_count.bit_length() - 1
    device_bits = src_bits + hi_bits
    box_bits = boxes.bit_length() - 1
    vectors = total // CHUNKS
    lane_boxes = LANES // vectors
    groups, pairs = boxes // lane_boxes, boxes // 2

    leaf = leaf_maps.reshape(boxes, rank, points)
    final = final_maps.reshape(boxes, rank, points)
    levels = level_maps.reshape(level_maps.shape[0], boxes, rank, 2 * rank)
    samples = traces.reshape(total, boxes, points)
    wanted = observed.reshape(total, boxes, points)

    def shape(*dims, dtype=BF):
        return jax.ShapeDtypeStruct(dims, dtype)

    forward_shape = shape(groups, rank, LANES)
    pair_shape = shape(pairs, vectors, LANES)
    kept_shape = shape(pairs, vectors, LANES, dtype=F32)
    sample_shape = shape(vectors, boxes, points)
    full_shape = shape(total, boxes, points)
    wide = pltpu.VMEM((vectors * boxes, points), F32)
    held = pltpu.VMEM((vectors, boxes, points), BF)
    sems = pltpu.SemaphoreType.DMA((2,))
    flops = 2 * boxes * rank * 2 * rank * vectors
    moved = boxes * rank * 2 * rank * 2

    def exchange(array, level):
        if level < src_bits:
            axis, count, bit = "src", src_count, level
        else:
            axis, count, bit = "hi", hi_count, level - src_bits
        return lax.ppermute(array, axis, [(i, i ^ 1 << bit) for i in range(count)])

    def reversal(array):
        pairs_of = []
        for src in range(src_count):
            for hi in range(hi_count):
                there = reverse_bits(hi * src_count + src, device_bits)
                pairs_of.append(
                    (src * hi_count + hi, there % src_count * hi_count + there // src_count)
                )
        return lax.ppermute(array, ("src", "hi"), pairs_of)

    def leaf_call(*operands):
        scratch = [
            pltpu.VMEM((total, boxes, points), BF), pltpu.VMEM((boxes, rank, points), BF),
            pltpu.SemaphoreType.DMA((CHUNKS + 1,)), wide,
        ]
        return call(
            functools.partial(leaf_kernel, CHUNKS),
            (forward_shape,) * CHUNKS, [HBM] * 2, (VMEM,) * CHUNKS, scratch,
            CHUNKS * flops, 4 * moved, 8,
        )(*operands)

    whole = [
        pltpu.VMEM((total, boxes, points), BF), sems, pltpu.VMEM((total * boxes, points), F32)
    ]

    def order_call(*operands):
        return call(
            order_kernel, shape(boxes, total, points), [HBM, ANY], VMEM, whole, 0, 2 * moved, 8
        )(*operands)

    def target_call(chunk, *operands):
        kernel = functools.partial(target_kernel, chunk)
        return call(
            kernel, (shape(boxes, vectors, points), pair_shape), [VMEM] * 3 + [ANY],
            (VMEM, VMEM), [], 2 * flops, 4 * moved, 8,
        )(*operands)

    done_shape = shape(8, LANES, dtype=F32)

    def residual_call(chunk, *operands):
        return call(
            functools.partial(residual_kernel, chunk), (full_shape, done_shape),
            [VMEM, ANY] + [HBM] * (len(operands) - 2), (HBM, VMEM), [held, sems, wide],
            0, 2 * moved, 8, {2: 0} if len(operands) > 2 else None,
        )(*operands)

    def gradient_call(chunk, *operands):
        return call(
            functools.partial(gradient_kernel, chunk), full_shape,
            [VMEM] * 3 + [HBM] * (len(operands) - 3), HBM,
            [held, pltpu.SemaphoreType.DMA((PARTS,)), wide],
            flops, 2 * moved, 8, {3: 0} if len(operands) > 3 else None,
        )(*operands)

    def cross_call(level, *operands):
        kernel = functools.partial(cross_kernel, level, src_bits, lane_boxes)
        specs = [VMEM] * 3 + [ANY] * (len(operands) - 3)
        return call(kernel, forward_shape, specs, VMEM, [], flops, moved, 4)(*operands)

    def adjoint_call(level, *operands):
        kernel = functools.partial(adjoint_cross_kernel, level, src_bits)
        specs = [VMEM] * 3 + [ANY] * (len(operands) - 3)
        return call(
            kernel, (kept_shape, pair_shape), specs, (VMEM, VMEM), [], flops, moved, 4
        )(*operands)

    def local_forward_call(*operands):
        kernel = functools.partial(local_forward_kernel, top, src_bits, lane_boxes)
        scratch = [pltpu.VMEM((2, groups, rank, LANES), BF)]
        return call(
            kernel, forward_shape, [VMEM] * 3 + [ANY], VMEM, scratch, 7 * flops, 7 * moved, 8
        )(*operands)

    def local_adjoint_call(*operands):
        kernel = functools.partial(local_adjoint_kernel, top, src_bits)
        scratch = [pltpu.VMEM((2, pairs, vectors, LANES), BF)]
        return call(
            kernel, (kept_shape, pair_shape), [VMEM] * 2 + [ANY], (VMEM, VMEM), scratch,
            7 * flops, 7 * moved, 8,
        )(*operands)

    top = device_bits - 1
    every = range(CHUNKS)
    coeffs, kept, sent = [None] * CHUNKS, [None] * CHUNKS, [None] * CHUNKS
    coeffs = list(leaf_call(samples, leaf))
    token = coeffs[0]
    by_box = [None] * CHUNKS
    residual, gradient = (), ()
    first_back = top + 1 + 2 * GAP
    stages = first_back + top
    for step in range(stages + LAG * (CHUNKS - 1)):
        for c in every:
            stage = step - LAG * c
            if 0 <= stage < top:
                level = stage
                maps = levels[level:level + 1] if level < EARLY else levels
                coeffs[c] = token = cross_call(
                    level, coeffs[c], exchange(coeffs[c], level), maps, token
                )
            elif stage == top:
                coeffs[c] = token = local_forward_call(
                    coeffs[c], exchange(coeffs[c], top), levels, token
                )
            elif stage == top + GAP:
                by_box[c], sent[c] = target_call(c, reversal(coeffs[c]), final, wanted, token)
                token = sent[c]
            elif stage == top + 2 * GAP:
                kept[c], sent[c] = local_adjoint_call(reversal(sent[c]), levels, token)
                token = sent[c]
            elif first_back <= stage < stages:
                level = top - 1 - (stage - first_back)
                kept[c], sent[c] = adjoint_call(
                    level, kept[c], exchange(sent[c], level + 1), levels, token
                )
                token = sent[c]
            if (stage, c) == (2, CHUNKS - 1):
                wanted = token = order_call(wanted, token)
            if stage == first_back + 2:
                *residual, token = residual_call(c, by_box[c], token, *residual)
    for c in every:
        gradient = [gradient_call(c, kept[c], exchange(sent[c], 0), leaf, *gradient)]
    residual, gradient = residual[0], gradient[0]
    return (
        residual.reshape(total, 1, 1, boxes, points),
        gradient.reshape(total, boxes, 1, 1, points),
    )


def solution(mesh):
    placed = (
        P(None, None, "hi", "src", None),
        P(None, "hi", "src", None, None),
        P(None, "hi", "src", None, None),
        P(None, None, "hi", "src", None, None),
        P("hi", "src", None, None, None),
    )
    return jax.shard_map(
        body,
        mesh=mesh,
        in_specs=placed,
        out_specs=(P(None, "hi", "src", None, None), P(None, None, "hi", "src", None)),
        check_vma=False,
    )
```

```python
import functools

import jax
import jax.numpy as jnp
from jax import lax
from jax.experimental import pallas as pl
from jax.experimental.pallas import tpu as pltpu
from jax.sharding import PartitionSpec as P

CHUNKS = 2
PARTS = 4
EARLY = 3
LAG = 2
GAP = 2
LANES = 128
BF = jnp.bfloat16
F32 = jnp.float32


def reverse_bits(value, bits):
    return int(format(value, f"0{bits}b")[::-1], 2)


def lane_block(shape, width):
    return lax.broadcasted_iota(jnp.int32, shape, len(shape) - 1) // width


def pick_lanes(product, rows, count, width):
    block = lane_block((rows, LANES), width)
    out = product[:rows]
    for b in range(1, count):
        out = jnp.where(block == b, product[b * rows:(b + 1) * rows], out)
    return out


def split_rows(pair):
    left = lane_block(pair.shape, LANES // 2) == 0
    zero = jnp.zeros(pair.shape, pair.dtype)
    return jnp.concatenate([jnp.where(left, pair, zero), jnp.where(left, zero, pair)], axis=0)


def halves_of(product, rows):
    first, second = product[:rows], product[rows:]
    left = lane_block((rows, LANES), LANES // 2) == 0
    low = jnp.where(left, first, pltpu.roll(second, LANES // 2, 1))
    high = jnp.where(left, pltpu.roll(first, LANES // 2, 1), second)
    return low, high


def is_high(level, src_bits):
    if level < src_bits:
        return (lax.axis_index("src") >> level & 1) == 1
    return (lax.axis_index("hi") >> (level - src_bits) & 1) == 1


def dot(a, b):
    return jnp.dot(a, b, preferred_element_type=F32)


def dot_nt(a, b):
    return lax.dot_general(a, b, (((1,), (1,)), ((), ())), preferred_element_type=F32)


def leaf_kernel(chunks, traces, leaf, *refs):
    outs = refs[:chunks]
    held, mats, sems, wide = refs[chunks:]
    total, boxes, points = held.shape
    vectors = total // chunks
    lane_boxes = LANES // vectors
    rank = mats.shape[1]
    copies = [
        pltpu.make_async_copy(
            traces.at[pl.ds(c * vectors, vectors)], held.at[pl.ds(c * vectors, vectors)], sems.at[c]
        )
        for c in range(chunks)
    ]
    copies.append(pltpu.make_async_copy(leaf, mats, sems.at[chunks]))
    for copy in copies:
        copy.start()
    for c in range(chunks):
        copies[c].wait()
        rows = held[pl.ds(c * vectors, vectors)].astype(F32)
        wide[...] = rows.reshape(wide.shape)
        if c == 0:
            copies[chunks].wait()
        for g in range(boxes // lane_boxes):
            rows = [
                wide[pl.ds(g * lane_boxes + b, vectors, stride=boxes), :]
                for b in range(lane_boxes)
            ]
            stacked = jnp.concatenate(rows, axis=0).astype(BF)
            group = mats[pl.ds(g * lane_boxes, lane_boxes)].reshape(lane_boxes * rank, points)
            outs[c][g] = pick_lanes(dot_nt(group, stacked), rank, lane_boxes, vectors).astype(BF)


def forward_group(weights, stacked, lane_boxes, rank):
    mats = weights.reshape(lane_boxes * rank, LANES)
    return pick_lanes(dot(mats, stacked), rank, lane_boxes, LANES // lane_boxes).astype(BF)


def cross_step(own, other, mats, out, high, lane_boxes):
    groups, rank = own.shape[0], own.shape[1]
    for g in range(groups):
        mine, theirs = own[g], other[g]
        take = jnp.broadcast_to(high, mine.shape)
        lower = jnp.where(take, theirs, mine)
        upper = jnp.where(take, mine, theirs)
        stacked = jnp.concatenate([lower, upper], axis=0)
        weights = mats[pl.ds(g * lane_boxes, lane_boxes)]
        out[g] = forward_group(weights, stacked, lane_boxes, rank)


def cross_kernel(level, src_bits, lane_boxes, own, other, maps, *refs):
    mats = maps.at[level if maps.shape[0] > 1 else 0]
    cross_step(own, other, mats, refs[-1], is_high(level, src_bits), lane_boxes)


def local_forward(lane_boxes, maps, first, out, work):
    groups, rank = out.shape[0], out.shape[1]
    lane_bits = lane_boxes.bit_length() - 1
    box_bits = maps.shape[1].bit_length() - 1
    for bit in range(box_bits):
        mats = maps.at[first + bit]
        source = work.at[bit % 2]
        target = out if bit == box_bits - 1 else work.at[(bit + 1) % 2]
        if bit < lane_bits:
            shift = LANES // lane_boxes << bit
            for g in range(groups):
                value = source[g].astype(F32)
                is_set = (lane_block(value.shape, shift) & 1) == 1
                lower = jnp.where(is_set, pltpu.roll(value, shift, 1), value)
                upper = jnp.where(is_set, value, pltpu.roll(value, LANES - shift, 1))
                stacked = jnp.concatenate([lower, upper], axis=0).astype(BF)
                weights = mats[pl.ds(g * lane_boxes, lane_boxes)]
                target[g] = forward_group(weights, stacked, lane_boxes, rank)
        else:
            inner = 1 << bit - lane_bits
            for g0 in range(groups):
                if g0 & inner:
                    continue
                stacked = jnp.concatenate([source[g0], source[g0 + inner]], axis=0)
                for g in (g0, g0 + inner):
                    weights = mats[pl.ds(g * lane_boxes, lane_boxes)]
                    target[g] = forward_group(weights, stacked, lane_boxes, rank)


def order_kernel(observed, token, out, held, sems, wide):
    total, boxes, points = held.shape
    fetch = pltpu.make_async_copy(observed, held, sems.at[0])
    fetch.start()
    fetch.wait()
    wide[...] = held[...].astype(F32).reshape(wide.shape)
    for t in range(boxes):
        out[t] = wide[pl.ds(t, total, stride=boxes), :].astype(BF)


def target_kernel(chunk, coeffs, final, wanted, token, residual, adjoint):
    groups, rank = coeffs.shape[0], coeffs.shape[1]
    boxes, vectors = residual.shape[0], residual.shape[1]
    box_bits = boxes.bit_length() - 1
    lane_boxes = LANES // vectors
    for g in range(groups):
        turned = jnp.transpose(coeffs[g].astype(F32)).astype(BF)
        for pair in range(lane_boxes // 2):
            kept, mats = [], []
            for b in (2 * pair, 2 * pair + 1):
                t = reverse_bits(g * lane_boxes + b, box_bits)
                mat = final[t]
                value = dot(turned[b * vectors:(b + 1) * vectors], mat)
                target = wanted[t, pl.ds(chunk * vectors, vectors), :].astype(F32)
                value = (value - target).astype(BF)
                residual[t] = value
                kept.append(value)
                mats.append(mat)
            product = dot_nt(jnp.concatenate(kept, axis=0), jnp.concatenate(mats, axis=0))
            adjoint[g * lane_boxes // 2 + pair] = pick_lanes(product, vectors, 2, rank).astype(BF)


def residual_kernel(chunk, part, token, *refs):
    residual, done, held, sems, wide = refs[-5:]
    boxes, vectors = part.shape[0], part.shape[1]
    for t in range(boxes):
        wide[pl.ds(t, vectors, stride=boxes), :] = part[t].astype(F32)
    held[...] = wide[...].reshape(held.shape).astype(BF)
    done[...] = jnp.zeros(done.shape, done.dtype)
    store = pltpu.make_async_copy(
        held, residual.at[pl.ds(chunk * vectors, vectors)], sems.at[0]
    )
    store.start()
    store.wait()


def adjoint_cross_pair(value, mats, kept, sent, p, high):
    rows = value.shape[0]
    low, upper = halves_of(dot(split_rows(value), mats), rows)
    take = jnp.broadcast_to(high, low.shape)
    kept[p] = jnp.where(take, upper, low)
    sent[p] = jnp.where(take, low, upper).astype(BF)


def pair_rows(mats, p):
    rank = mats.shape[1]
    return mats[pl.ds(2 * p, 2)].reshape(2 * rank, LANES)


def local_forward_kernel(level, src_bits, lane_boxes, own, other, maps, token, coeffs, work):
    high = is_high(level, src_bits)
    cross_step(own, other, maps.at[level], work.at[0], high, lane_boxes)
    local_forward(lane_boxes, maps, level + 1, coeffs, work)


def local_adjoint_kernel(level, src_bits, adjoint, maps, token, kept, sent, work):
    pairs, vectors = work.shape[1], work.shape[2]
    box_bits = maps.shape[1].bit_length() - 1
    for step, bit in enumerate(reversed(range(box_bits))):
        mats = maps.at[level + 1 + bit]
        source = work.at[step % 2] if step else adjoint
        target = work.at[(step + 1) % 2]
        if bit == 0:
            for p in range(pairs):
                target[p] = dot(source[p], pair_rows(mats, p)).astype(BF)
        else:
            inner = 1 << bit - 1
            for p0 in range(pairs):
                if p0 & inner:
                    continue
                p1 = p0 + inner
                rows = jnp.concatenate([split_rows(source[p0]), split_rows(source[p1])], axis=1)
                stacked = jnp.concatenate([pair_rows(mats, p0), pair_rows(mats, p1)], axis=0)
                low, upper = halves_of(dot(rows, stacked), vectors)
                target[p0] = low.astype(BF)
                target[p1] = upper.astype(BF)
    source = work.at[box_bits % 2]
    high = is_high(level, src_bits)
    for p in range(pairs):
        adjoint_cross_pair(source[p], pair_rows(maps.at[level], p), kept, sent, p, high)


def adjoint_cross_kernel(level, src_bits, held_part, received, maps, *refs):
    kept, sent = refs[-2:]
    high = is_high(level, src_bits)
    for p in range(held_part.shape[0]):
        value = (held_part[p] + received[p].astype(F32)).astype(BF)
        adjoint_cross_pair(value, pair_rows(maps.at[level], p), kept, sent, p, high)


def gradient_kernel(chunk, held_part, received, leaf, token, *refs):
    gradient, done, held, sems, result = refs[-5:]
    done[...] = jnp.zeros(done.shape, done.dtype)
    pairs, vectors = held_part.shape[0], held_part.shape[1]
    boxes, points = held.shape[1], held.shape[2]
    stores = []
    for part in range(PARTS):
        for p in range(part * pairs // PARTS, (part + 1) * pairs // PARTS):
            value = (held_part[p] + received[p].astype(F32)).astype(BF)
            product = dot(split_rows(value), pair_rows(leaf, p))
            result[pl.ds(2 * p, vectors, stride=boxes), :] = product[:vectors]
            result[pl.ds(2 * p + 1, vectors, stride=boxes), :] = product[vectors:]
        own = pl.ds(part * boxes // PARTS, boxes // PARTS)
        for v in range(vectors):
            rows = result[pl.ds(v * boxes + part * boxes // PARTS, boxes // PARTS), :]
            held[v, own, :] = rows.astype(BF)
        store = pltpu.make_async_copy(
            held.at[:, own, :],
            gradient.at[pl.ds(chunk * vectors, vectors), own, :],
            sems.at[part],
        )
        store.start()
        stores.append(store)
    for store in stores:
        store.wait()


VMEM = pl.BlockSpec(memory_space=pltpu.VMEM)
ANY = pl.BlockSpec(memory_space=pl.ANY)
HBM = pl.BlockSpec(memory_space=pltpu.HBM)


def call(kernel, out_shape, in_specs, out_specs, scratch, flops, moved, limit, aliases=None):
    return pl.pallas_call(
        kernel,
        out_shape=out_shape,
        in_specs=in_specs,
        out_specs=out_specs,
        scratch_shapes=scratch,
        input_output_aliases=aliases or {},
        compiler_params=pltpu.CompilerParams(vmem_limit_bytes=limit << 20),
        cost_estimate=pl.CostEstimate(flops=flops, bytes_accessed=moved, transcendentals=0),
    )


def body(traces, observed, leaf_maps, level_maps, final_maps):
    total = traces.shape[0]
    boxes, points = traces.shape[1], traces.shape[4]
    rank = leaf_maps.shape[3]
    src_count, hi_count = lax.axis_size("src"), lax.axis_size("hi")
    src_bits = src_count.bit_length() - 1
    hi_bits = hi_count.bit_length() - 1
    device_bits = src_bits + hi_bits
    box_bits = boxes.bit_length() - 1
    vectors = total // CHUNKS
    lane_boxes = LANES // vectors
    groups, pairs = boxes // lane_boxes, boxes // 2

    leaf = leaf_maps.reshape(boxes, rank, points)
    final = final_maps.reshape(boxes, rank, points)
    levels = level_maps.reshape(level_maps.shape[0], boxes, rank, 2 * rank)
    samples = traces.reshape(total, boxes, points)
    wanted = observed.reshape(total, boxes, points)

    def shape(*dims, dtype=BF):
        return jax.ShapeDtypeStruct(dims, dtype)

    forward_shape = shape(groups, rank, LANES)
    pair_shape = shape(pairs, vectors, LANES)
    kept_shape = shape(pairs, vectors, LANES, dtype=F32)
    sample_shape = shape(vectors, boxes, points)
    full_shape = shape(total, boxes, points)
    wide = pltpu.VMEM((vectors * boxes, points), F32)
    held = pltpu.VMEM((vectors, boxes, points), BF)
    sems = pltpu.SemaphoreType.DMA((2,))
    flops = 2 * boxes * rank * 2 * rank * vectors
    moved = boxes * rank * 2 * rank * 2

    def exchange(array, level):
        if level < src_bits:
            axis, count, bit = "src", src_count, level
        else:
            axis, count, bit = "hi", hi_count, level - src_bits
        return lax.ppermute(array, axis, [(i, i ^ 1 << bit) for i in range(count)])

    def reversal(array):
        pairs_of = []
        for src in range(src_count):
            for hi in range(hi_count):
                there = reverse_bits(hi * src_count + src, device_bits)
                pairs_of.append(
                    (src * hi_count + hi, there % src_count * hi_count + there // src_count)
                )
        return lax.ppermute(array, ("src", "hi"), pairs_of)

    def leaf_call(*operands):
        scratch = [
            pltpu.VMEM((total, boxes, points), BF), pltpu.VMEM((boxes, rank, points), BF),
            pltpu.SemaphoreType.DMA((CHUNKS + 1,)), wide,
        ]
        return call(
            functools.partial(leaf_kernel, CHUNKS),
            (forward_shape,) * CHUNKS, [HBM] * 2, (VMEM,) * CHUNKS, scratch,
            CHUNKS * flops, 4 * moved, 8,
        )(*operands)

    whole = [
        pltpu.VMEM((total, boxes, points), BF), sems, pltpu.VMEM((total * boxes, points), F32)
    ]

    def order_call(*operands):
        return call(
            order_kernel, shape(boxes, total, points), [HBM, ANY], VMEM, whole, 0, 2 * moved, 8
        )(*operands)

    def target_call(chunk, *operands):
        kernel = functools.partial(target_kernel, chunk)
        return call(
            kernel, (shape(boxes, vectors, points), pair_shape), [VMEM] * 3 + [ANY],
            (VMEM, VMEM), [], 2 * flops, 4 * moved, 8,
        )(*operands)

    done_shape = shape(8, LANES, dtype=F32)

    def residual_call(chunk, *operands):
        return call(
            functools.partial(residual_kernel, chunk), (full_shape, done_shape),
            [VMEM, ANY] + [HBM] * (len(operands) - 2), (HBM, VMEM), [held, sems, wide],
            0, 2 * moved, 8, {2: 0} if len(operands) > 2 else None,
        )(*operands)

    def gradient_call(chunk, *operands):
        return call(
            functools.partial(gradient_kernel, chunk), (full_shape, done_shape),
            [VMEM] * 3 + [ANY] + [HBM] * (len(operands) - 4), (HBM, VMEM),
            [held, pltpu.SemaphoreType.DMA((PARTS,)), wide],
            flops, 2 * moved, 8, {4: 0} if len(operands) > 4 else None,
        )(*operands)

    def cross_call(level, *operands):
        kernel = functools.partial(cross_kernel, level, src_bits, lane_boxes)
        specs = [VMEM] * 3 + [ANY] * (len(operands) - 3)
        return call(kernel, forward_shape, specs, VMEM, [], flops, moved, 4)(*operands)

    def adjoint_call(level, *operands):
        kernel = functools.partial(adjoint_cross_kernel, level, src_bits)
        specs = [VMEM] * 3 + [ANY] * (len(operands) - 3)
        return call(
            kernel, (kept_shape, pair_shape), specs, (VMEM, VMEM), [], flops, moved, 4
        )(*operands)

    def local_forward_call(*operands):
        kernel = functools.partial(local_forward_kernel, top, src_bits, lane_boxes)
        scratch = [pltpu.VMEM((2, groups, rank, LANES), BF)]
        return call(
            kernel, forward_shape, [VMEM] * 3 + [ANY], VMEM, scratch, 7 * flops, 7 * moved, 8
        )(*operands)

    def local_adjoint_call(*operands):
        kernel = functools.partial(local_adjoint_kernel, top, src_bits)
        scratch = [pltpu.VMEM((2, pairs, vectors, LANES), BF)]
        return call(
            kernel, (kept_shape, pair_shape), [VMEM] * 2 + [ANY], (VMEM, VMEM), scratch,
            7 * flops, 7 * moved, 8,
        )(*operands)

    top = device_bits - 1
    every = range(CHUNKS)
    coeffs, kept, sent = [None] * CHUNKS, [None] * CHUNKS, [None] * CHUNKS
    coeffs = list(leaf_call(samples, leaf))
    token = coeffs[0]
    by_box = [None] * CHUNKS
    residual, gradient = (), ()
    first_back = top + 1 + 2 * GAP
    stages = first_back + top
    for step in range(stages + 1 + LAG * (CHUNKS - 1)):
        for c in every:
            stage = step - LAG * c
            if 0 <= stage < top:
                level = stage
                maps = levels[level:level + 1] if level < EARLY else levels
                coeffs[c] = token = cross_call(
                    level, coeffs[c], exchange(coeffs[c], level), maps, token
                )
            elif stage == top:
                coeffs[c] = token = local_forward_call(
                    coeffs[c], exchange(coeffs[c], top), levels, token
                )
            elif stage == top + GAP:
                by_box[c], sent[c] = target_call(c, reversal(coeffs[c]), final, wanted, token)
                token = sent[c]
            elif stage == top + 2 * GAP:
                kept[c], sent[c] = local_adjoint_call(reversal(sent[c]), levels, token)
                token = sent[c]
            elif first_back <= stage < stages:
                level = top - 1 - (stage - first_back)
                kept[c], sent[c] = adjoint_call(
                    level, kept[c], exchange(sent[c], level + 1), levels, token
                )
                token = sent[c]
            elif stage == stages:
                *gradient, token = gradient_call(
                    c, kept[c], exchange(sent[c], 0), leaf, token, *gradient
                )
            if (stage, c) == (2, CHUNKS - 1):
                wanted = token = order_call(wanted, token)
            if stage == first_back + 2:
                *residual, token = residual_call(c, by_box[c], token, *residual)
    residual, gradient = residual[0], gradient[0]
    return (
        residual.reshape(total, 1, 1, boxes, points),
        gradient.reshape(total, boxes, 1, 1, points),
    )


def solution(mesh):
    placed = (
        P(None, None, "hi", "src", None),
        P(None, "hi", "src", None, None),
        P(None, "hi", "src", None, None),
        P(None, None, "hi", "src", None, None),
        P("hi", "src", None, None, None),
    )
    return jax.shard_map(
        body,
        mesh=mesh,
        in_specs=placed,
        out_specs=(P(None, "hi", "src", None, None), P(None, None, "hi", "src", None)),
        check_vma=False,
    )
```

```python
import functools

import jax
import jax.numpy as jnp
from jax import lax
from jax.experimental import pallas as pl
from jax.experimental.pallas import tpu as pltpu
from jax.sharding import PartitionSpec as P

CHUNKS = 2
PARTS = 4
EARLY = 3
LAG = 1
GAP = 2
LANES = 128
BF = jnp.bfloat16
F32 = jnp.float32


def reverse_bits(value, bits):
    return int(format(value, f"0{bits}b")[::-1], 2)


def lane_block(shape, width):
    return lax.broadcasted_iota(jnp.int32, shape, len(shape) - 1) // width


def pick_lanes(product, rows, count, width):
    block = lane_block((rows, LANES), width)
    out = product[:rows]
    for b in range(1, count):
        out = jnp.where(block == b, product[b * rows:(b + 1) * rows], out)
    return out


def split_rows(pair):
    left = lane_block(pair.shape, LANES // 2) == 0
    zero = jnp.zeros(pair.shape, pair.dtype)
    return jnp.concatenate([jnp.where(left, pair, zero), jnp.where(left, zero, pair)], axis=0)


def halves_of(product, rows):
    first, second = product[:rows], product[rows:]
    left = lane_block((rows, LANES), LANES // 2) == 0
    low = jnp.where(left, first, pltpu.roll(second, LANES // 2, 1))
    high = jnp.where(left, pltpu.roll(first, LANES // 2, 1), second)
    return low, high


def is_high(level, src_bits):
    if level < src_bits:
        return (lax.axis_index("src") >> level & 1) == 1
    return (lax.axis_index("hi") >> (level - src_bits) & 1) == 1


def dot(a, b):
    return jnp.dot(a, b, preferred_element_type=F32)


def dot_nt(a, b):
    return lax.dot_general(a, b, (((1,), (1,)), ((), ())), preferred_element_type=F32)


def leaf_kernel(chunks, traces, leaf, *refs):
    outs = refs[:chunks]
    held, mats, sems, wide = refs[chunks:]
    total, boxes, points = held.shape
    vectors = total // chunks
    lane_boxes = LANES // vectors
    rank = mats.shape[1]
    copies = [
        pltpu.make_async_copy(
            traces.at[pl.ds(c * vectors, vectors)], held.at[pl.ds(c * vectors, vectors)], sems.at[c]
        )
        for c in range(chunks)
    ]
    copies.append(pltpu.make_async_copy(leaf, mats, sems.at[chunks]))
    for copy in copies:
        copy.start()
    for c in range(chunks):
        copies[c].wait()
        rows = held[pl.ds(c * vectors, vectors)].astype(F32)
        wide[...] = rows.reshape(wide.shape)
        if c == 0:
            copies[chunks].wait()
        for g in range(boxes // lane_boxes):
            rows = [
                wide[pl.ds(g * lane_boxes + b, vectors, stride=boxes), :]
                for b in range(lane_boxes)
            ]
            stacked = jnp.concatenate(rows, axis=0).astype(BF)
            group = mats[pl.ds(g * lane_boxes, lane_boxes)].reshape(lane_boxes * rank, points)
            outs[c][g] = pick_lanes(dot_nt(group, stacked), rank, lane_boxes, vectors).astype(BF)


def forward_group(weights, stacked, lane_boxes, rank):
    mats = weights.reshape(lane_boxes * rank, LANES)
    return pick_lanes(dot(mats, stacked), rank, lane_boxes, LANES // lane_boxes).astype(BF)


def cross_step(own, other, mats, out, high, lane_boxes):
    groups, rank = own.shape[0], own.shape[1]
    for g in range(groups):
        mine, theirs = own[g], other[g]
        take = jnp.broadcast_to(high, mine.shape)
        lower = jnp.where(take, theirs, mine)
        upper = jnp.where(take, mine, theirs)
        stacked = jnp.concatenate([lower, upper], axis=0)
        weights = mats[pl.ds(g * lane_boxes, lane_boxes)]
        out[g] = forward_group(weights, stacked, lane_boxes, rank)


def cross_kernel(level, src_bits, lane_boxes, own, other, maps, *refs):
    mats = maps.at[level if maps.shape[0] > 1 else 0]
    cross_step(own, other, mats, refs[-1], is_high(level, src_bits), lane_boxes)


def local_forward(lane_boxes, maps, first, out, work):
    groups, rank = out.shape[0], out.shape[1]
    lane_bits = lane_boxes.bit_length() - 1
    box_bits = maps.shape[1].bit_length() - 1
    for bit in range(box_bits):
        mats = maps.at[first + bit]
        source = work.at[bit % 2]
        target = out if bit == box_bits - 1 else work.at[(bit + 1) % 2]
        if bit < lane_bits:
            shift = LANES // lane_boxes << bit
            for g in range(groups):
                value = source[g].astype(F32)
                is_set = (lane_block(value.shape, shift) & 1) == 1
                lower = jnp.where(is_set, pltpu.roll(value, shift, 1), value)
                upper = jnp.where(is_set, value, pltpu.roll(value, LANES - shift, 1))
                stacked = jnp.concatenate([lower, upper], axis=0).astype(BF)
                weights = mats[pl.ds(g * lane_boxes, lane_boxes)]
                target[g] = forward_group(weights, stacked, lane_boxes, rank)
        else:
            inner = 1 << bit - lane_bits
            for g0 in range(groups):
                if g0 & inner:
                    continue
                stacked = jnp.concatenate([source[g0], source[g0 + inner]], axis=0)
                for g in (g0, g0 + inner):
                    weights = mats[pl.ds(g * lane_boxes, lane_boxes)]
                    target[g] = forward_group(weights, stacked, lane_boxes, rank)


def order_kernel(observed, token, out, held, sems, wide):
    total, boxes, points = held.shape
    fetch = pltpu.make_async_copy(observed, held, sems.at[0])
    fetch.start()
    fetch.wait()
    wide[...] = held[...].astype(F32).reshape(wide.shape)
    for t in range(boxes):
        out[t] = wide[pl.ds(t, total, stride=boxes), :].astype(BF)


def target_kernel(chunk, coeffs, final, wanted, token, residual, adjoint):
    groups, rank = coeffs.shape[0], coeffs.shape[1]
    boxes, vectors = residual.shape[0], residual.shape[1]
    box_bits = boxes.bit_length() - 1
    lane_boxes = LANES // vectors
    for g in range(groups):
        turned = jnp.transpose(coeffs[g].astype(F32)).astype(BF)
        for pair in range(lane_boxes // 2):
            kept, mats = [], []
            for b in (2 * pair, 2 * pair + 1):
                t = reverse_bits(g * lane_boxes + b, box_bits)
                mat = final[t]
                value = dot(turned[b * vectors:(b + 1) * vectors], mat)
                target = wanted[t, pl.ds(chunk * vectors, vectors), :].astype(F32)
                value = (value - target).astype(BF)
                residual[t] = value
                kept.append(value)
                mats.append(mat)
            product = dot_nt(jnp.concatenate(kept, axis=0), jnp.concatenate(mats, axis=0))
            adjoint[g * lane_boxes // 2 + pair] = pick_lanes(product, vectors, 2, rank).astype(BF)


def residual_kernel(chunk, part, token, *refs):
    residual, done, held, sems, wide = refs[-5:]
    boxes, vectors = part.shape[0], part.shape[1]
    for t in range(boxes):
        wide[pl.ds(t, vectors, stride=boxes), :] = part[t].astype(F32)
    held[...] = wide[...].reshape(held.shape).astype(BF)
    done[...] = jnp.zeros(done.shape, done.dtype)
    store = pltpu.make_async_copy(
        held, residual.at[pl.ds(chunk * vectors, vectors)], sems.at[0]
    )
    store.start()
    store.wait()


def adjoint_cross_pair(value, mats, kept, sent, p, high):
    rows = value.shape[0]
    low, upper = halves_of(dot(split_rows(value), mats), rows)
    take = jnp.broadcast_to(high, low.shape)
    kept[p] = jnp.where(take, upper, low)
    sent[p] = jnp.where(take, low, upper).astype(BF)


def pair_rows(mats, p):
    rank = mats.shape[1]
    return mats[pl.ds(2 * p, 2)].reshape(2 * rank, LANES)


def local_forward_kernel(level, src_bits, lane_boxes, own, other, maps, token, coeffs, work):
    high = is_high(level, src_bits)
    cross_step(own, other, maps.at[level], work.at[0], high, lane_boxes)
    local_forward(lane_boxes, maps, level + 1, coeffs, work)


def local_adjoint_kernel(level, src_bits, adjoint, maps, token, kept, sent, work):
    pairs, vectors = work.shape[1], work.shape[2]
    box_bits = maps.shape[1].bit_length() - 1
    for step, bit in enumerate(reversed(range(box_bits))):
        mats = maps.at[level + 1 + bit]
        source = work.at[step % 2] if step else adjoint
        target = work.at[(step + 1) % 2]
        if bit == 0:
            for p in range(pairs):
                target[p] = dot(source[p], pair_rows(mats, p)).astype(BF)
        else:
            inner = 1 << bit - 1
            for p0 in range(pairs):
                if p0 & inner:
                    continue
                p1 = p0 + inner
                rows = jnp.concatenate([split_rows(source[p0]), split_rows(source[p1])], axis=1)
                stacked = jnp.concatenate([pair_rows(mats, p0), pair_rows(mats, p1)], axis=0)
                low, upper = halves_of(dot(rows, stacked), vectors)
                target[p0] = low.astype(BF)
                target[p1] = upper.astype(BF)
    source = work.at[box_bits % 2]
    high = is_high(level, src_bits)
    for p in range(pairs):
        adjoint_cross_pair(source[p], pair_rows(maps.at[level], p), kept, sent, p, high)


def adjoint_cross_kernel(level, src_bits, held_part, received, maps, *refs):
    kept, sent = refs[-2:]
    high = is_high(level, src_bits)
    for p in range(held_part.shape[0]):
        value = (held_part[p] + received[p].astype(F32)).astype(BF)
        adjoint_cross_pair(value, pair_rows(maps.at[level], p), kept, sent, p, high)


def gradient_kernel(chunk, held_part, received, leaf, token, *refs):
    gradient, done, held, sems, result = refs[-5:]
    done[...] = jnp.zeros(done.shape, done.dtype)
    pairs, vectors = held_part.shape[0], held_part.shape[1]
    boxes, points = held.shape[1], held.shape[2]
    stores = []
    for part in range(PARTS):
        for p in range(part * pairs // PARTS, (part + 1) * pairs // PARTS):
            value = (held_part[p] + received[p].astype(F32)).astype(BF)
            product = dot(split_rows(value), pair_rows(leaf, p))
            result[pl.ds(2 * p, vectors, stride=boxes), :] = product[:vectors]
            result[pl.ds(2 * p + 1, vectors, stride=boxes), :] = product[vectors:]
        own = pl.ds(part * boxes // PARTS, boxes // PARTS)
        for v in range(vectors):
            rows = result[pl.ds(v * boxes + part * boxes // PARTS, boxes // PARTS), :]
            held[v, own, :] = rows.astype(BF)
        store = pltpu.make_async_copy(
            held.at[:, own, :],
            gradient.at[pl.ds(chunk * vectors, vectors), own, :],
            sems.at[part],
        )
        store.start()
        stores.append(store)
    for store in stores:
        store.wait()


VMEM = pl.BlockSpec(memory_space=pltpu.VMEM)
ANY = pl.BlockSpec(memory_space=pl.ANY)
HBM = pl.BlockSpec(memory_space=pltpu.HBM)


def call(kernel, out_shape, in_specs, out_specs, scratch, flops, moved, limit, aliases=None):
    return pl.pallas_call(
        kernel,
        out_shape=out_shape,
        in_specs=in_specs,
        out_specs=out_specs,
        scratch_shapes=scratch,
        input_output_aliases=aliases or {},
        compiler_params=pltpu.CompilerParams(vmem_limit_bytes=limit << 20),
        cost_estimate=pl.CostEstimate(flops=flops, bytes_accessed=moved, transcendentals=0),
    )


def body(traces, observed, leaf_maps, level_maps, final_maps):
    total = traces.shape[0]
    boxes, points = traces.shape[1], traces.shape[4]
    rank = leaf_maps.shape[3]
    src_count, hi_count = lax.axis_size("src"), lax.axis_size("hi")
    src_bits = src_count.bit_length() - 1
    hi_bits = hi_count.bit_length() - 1
    device_bits = src_bits + hi_bits
    box_bits = boxes.bit_length() - 1
    vectors = total // CHUNKS
    lane_boxes = LANES // vectors
    groups, pairs = boxes // lane_boxes, boxes // 2

    leaf = leaf_maps.reshape(boxes, rank, points)
    final = final_maps.reshape(boxes, rank, points)
    levels = level_maps.reshape(level_maps.shape[0], boxes, rank, 2 * rank)
    samples = traces.reshape(total, boxes, points)
    wanted = observed.reshape(total, boxes, points)

    def shape(*dims, dtype=BF):
        return jax.ShapeDtypeStruct(dims, dtype)

    forward_shape = shape(groups, rank, LANES)
    pair_shape = shape(pairs, vectors, LANES)
    kept_shape = shape(pairs, vectors, LANES, dtype=F32)
    sample_shape = shape(vectors, boxes, points)
    full_shape = shape(total, boxes, points)
    wide = pltpu.VMEM((vectors * boxes, points), F32)
    held = pltpu.VMEM((vectors, boxes, points), BF)
    sems = pltpu.SemaphoreType.DMA((2,))
    flops = 2 * boxes * rank * 2 * rank * vectors
    moved = boxes * rank * 2 * rank * 2

    def exchange(array, level):
        if level < src_bits:
            axis, count, bit = "src", src_count, level
        else:
            axis, count, bit = "hi", hi_count, level - src_bits
        return lax.ppermute(array, axis, [(i, i ^ 1 << bit) for i in range(count)])

    def reversal(array):
        pairs_of = []
        for src in range(src_count):
            for hi in range(hi_count):
                there = reverse_bits(hi * src_count + src, device_bits)
                pairs_of.append(
                    (src * hi_count + hi, there % src_count * hi_count + there // src_count)
                )
        return lax.ppermute(array, ("src", "hi"), pairs_of)

    def leaf_call(*operands):
        scratch = [
            pltpu.VMEM((total, boxes, points), BF), pltpu.VMEM((boxes, rank, points), BF),
            pltpu.SemaphoreType.DMA((CHUNKS + 1,)), wide,
        ]
        return call(
            functools.partial(leaf_kernel, CHUNKS),
            (forward_shape,) * CHUNKS, [HBM] * 2, (VMEM,) * CHUNKS, scratch,
            CHUNKS * flops, 4 * moved, 8,
        )(*operands)

    whole = [
        pltpu.VMEM((total, boxes, points), BF), sems, pltpu.VMEM((total * boxes, points), F32)
    ]

    def order_call(*operands):
        return call(
            order_kernel, shape(boxes, total, points), [HBM, ANY], VMEM, whole, 0, 2 * moved, 8
        )(*operands)

    def target_call(chunk, *operands):
        kernel = functools.partial(target_kernel, chunk)
        return call(
            kernel, (shape(boxes, vectors, points), pair_shape), [VMEM] * 3 + [ANY],
            (VMEM, VMEM), [], 2 * flops, 4 * moved, 8,
        )(*operands)

    done_shape = shape(8, LANES, dtype=F32)

    def residual_call(chunk, *operands):
        return call(
            functools.partial(residual_kernel, chunk), (full_shape, done_shape),
            [VMEM, ANY] + [HBM] * (len(operands) - 2), (HBM, VMEM), [held, sems, wide],
            0, 2 * moved, 8, {2: 0} if len(operands) > 2 else None,
        )(*operands)

    def gradient_call(chunk, *operands):
        return call(
            functools.partial(gradient_kernel, chunk), (full_shape, done_shape),
            [VMEM] * 3 + [ANY] + [HBM] * (len(operands) - 4), (HBM, VMEM),
            [held, pltpu.SemaphoreType.DMA((PARTS,)), wide],
            flops, 2 * moved, 8, {4: 0} if len(operands) > 4 else None,
        )(*operands)

    def cross_call(level, *operands):
        kernel = functools.partial(cross_kernel, level, src_bits, lane_boxes)
        specs = [VMEM] * 3 + [ANY] * (len(operands) - 3)
        return call(kernel, forward_shape, specs, VMEM, [], flops, moved, 4)(*operands)

    def adjoint_call(level, *operands):
        kernel = functools.partial(adjoint_cross_kernel, level, src_bits)
        specs = [VMEM] * 3 + [ANY] * (len(operands) - 3)
        return call(
            kernel, (kept_shape, pair_shape), specs, (VMEM, VMEM), [], flops, moved, 4
        )(*operands)

    def local_forward_call(*operands):
        kernel = functools.partial(local_forward_kernel, top, src_bits, lane_boxes)
        scratch = [pltpu.VMEM((2, groups, rank, LANES), BF)]
        return call(
            kernel, forward_shape, [VMEM] * 3 + [ANY], VMEM, scratch, 7 * flops, 7 * moved, 8
        )(*operands)

    def local_adjoint_call(*operands):
        kernel = functools.partial(local_adjoint_kernel, top, src_bits)
        scratch = [pltpu.VMEM((2, pairs, vectors, LANES), BF)]
        return call(
            kernel, (kept_shape, pair_shape), [VMEM] * 2 + [ANY], (VMEM, VMEM), scratch,
            7 * flops, 7 * moved, 8,
        )(*operands)

    top = device_bits - 1
    every = range(CHUNKS)
    coeffs, kept, sent = [None] * CHUNKS, [None] * CHUNKS, [None] * CHUNKS
    coeffs = list(leaf_call(samples, leaf))
    token = coeffs[0]
    by_box = [None] * CHUNKS
    residual, gradient = (), ()
    first_back = top + 1 + 2 * GAP
    stages = first_back + top
    for step in range(stages + 1 + LAG * (CHUNKS - 1)):
        for c in every:
            stage = step - LAG * c
            if 0 <= stage < top:
                level = stage
                maps = levels[level:level + 1] if level < EARLY else levels
                coeffs[c] = token = cross_call(
                    level, coeffs[c], exchange(coeffs[c], level), maps, token
                )
            elif stage == top:
                coeffs[c] = token = local_forward_call(
                    coeffs[c], exchange(coeffs[c], top), levels, token
                )
            elif stage == top + GAP:
                by_box[c], sent[c] = target_call(c, reversal(coeffs[c]), final, wanted, token)
                token = sent[c]
            elif stage == top + 2 * GAP:
                kept[c], sent[c] = local_adjoint_call(reversal(sent[c]), levels, token)
                token = sent[c]
            elif first_back <= stage < stages:
                level = top - 1 - (stage - first_back)
                kept[c], sent[c] = adjoint_call(
                    level, kept[c], exchange(sent[c], level + 1), levels, token
                )
                token = sent[c]
            elif stage == stages:
                *gradient, token = gradient_call(
                    c, kept[c], exchange(sent[c], 0), leaf, token, *gradient
                )
            if (stage, c) == (2, CHUNKS - 1):
                wanted = token = order_call(wanted, token)
            if stage == first_back + 2:
                *residual, token = residual_call(c, by_box[c], token, *residual)
    residual, gradient = residual[0], gradient[0]
    return (
        residual.reshape(total, 1, 1, boxes, points),
        gradient.reshape(total, boxes, 1, 1, points),
    )


def solution(mesh):
    placed = (
        P(None, None, "hi", "src", None),
        P(None, "hi", "src", None, None),
        P(None, "hi", "src", None, None),
        P(None, None, "hi", "src", None, None),
        P("hi", "src", None, None, None),
    )
    return jax.shard_map(
        body,
        mesh=mesh,
        in_specs=placed,
        out_specs=(P(None, "hi", "src", None, None), P(None, None, "hi", "src", None)),
        check_vma=False,
    )
```

```python
import functools

import jax
import jax.numpy as jnp
from jax import lax
from jax.experimental import pallas as pl
from jax.experimental.pallas import tpu as pltpu
from jax.sharding import PartitionSpec as P

CHUNKS = 2
PARTS = 4
EARLY = 3
LAG = 1
GAP = 2
LANES = 128
BF = jnp.bfloat16
F32 = jnp.float32


def reverse_bits(value, bits):
    return int(format(value, f"0{bits}b")[::-1], 2)


def lane_block(shape, width):
    return lax.broadcasted_iota(jnp.int32, shape, len(shape) - 1) // width


def pick_lanes(product, rows, count, width):
    block = lane_block((rows, LANES), width)
    out = product[:rows]
    for b in range(1, count):
        out = jnp.where(block == b, product[b * rows:(b + 1) * rows], out)
    return out


def split_rows(pair):
    left = lane_block(pair.shape, LANES // 2) == 0
    zero = jnp.zeros(pair.shape, pair.dtype)
    return jnp.concatenate([jnp.where(left, pair, zero), jnp.where(left, zero, pair)], axis=0)


def halves_of(product, rows):
    first, second = product[:rows], product[rows:]
    left = lane_block((rows, LANES), LANES // 2) == 0
    low = jnp.where(left, first, pltpu.roll(second, LANES // 2, 1))
    high = jnp.where(left, pltpu.roll(first, LANES // 2, 1), second)
    return low, high


def is_high(level, src_bits):
    if level < src_bits:
        return (lax.axis_index("src") >> level & 1) == 1
    return (lax.axis_index("hi") >> (level - src_bits) & 1) == 1


def dot(a, b):
    return jnp.dot(a, b, preferred_element_type=F32)


def dot_nt(a, b):
    return lax.dot_general(a, b, (((1,), (1,)), ((), ())), preferred_element_type=F32)


def leaf_kernel(chunks, traces, leaf, *refs):
    outs = refs[:chunks]
    held, mats, sems, wide = refs[chunks:]
    total, boxes, points = held.shape
    vectors = total // chunks
    lane_boxes = LANES // vectors
    rank = mats.shape[1]
    copies = [
        pltpu.make_async_copy(
            traces.at[pl.ds(c * vectors, vectors)], held.at[pl.ds(c * vectors, vectors)], sems.at[c]
        )
        for c in range(chunks)
    ]
    copies.append(pltpu.make_async_copy(leaf, mats, sems.at[chunks]))
    for copy in copies:
        copy.start()
    for c in range(chunks):
        copies[c].wait()
        rows = held[pl.ds(c * vectors, vectors)].astype(F32)
        wide[...] = rows.reshape(wide.shape)
        if c == 0:
            copies[chunks].wait()
        for g in range(boxes // lane_boxes):
            rows = [
                wide[pl.ds(g * lane_boxes + b, vectors, stride=boxes), :]
                for b in range(lane_boxes)
            ]
            stacked = jnp.concatenate(rows, axis=0).astype(BF)
            group = mats[pl.ds(g * lane_boxes, lane_boxes)].reshape(lane_boxes * rank, points)
            outs[c][g] = pick_lanes(dot_nt(group, stacked), rank, lane_boxes, vectors).astype(BF)


def forward_group(weights, stacked, lane_boxes, rank):
    mats = weights.reshape(lane_boxes * rank, LANES)
    return pick_lanes(dot(mats, stacked), rank, lane_boxes, LANES // lane_boxes).astype(BF)


def cross_step(own, other, mats, out, high, lane_boxes):
    groups, rank = own.shape[0], own.shape[1]
    for g in range(groups):
        mine, theirs = own[g], other[g]
        take = jnp.broadcast_to(high, mine.shape)
        lower = jnp.where(take, theirs, mine)
        upper = jnp.where(take, mine, theirs)
        stacked = jnp.concatenate([lower, upper], axis=0)
        weights = mats[pl.ds(g * lane_boxes, lane_boxes)]
        out[g] = forward_group(weights, stacked, lane_boxes, rank)


def cross_kernel(level, src_bits, lane_boxes, own, other, maps, *refs):
    mats = maps.at[level if maps.shape[0] > 1 else 0]
    cross_step(own, other, mats, refs[-1], is_high(level, src_bits), lane_boxes)


def local_forward(lane_boxes, maps, first, out, work):
    groups, rank = out.shape[0], out.shape[1]
    lane_bits = lane_boxes.bit_length() - 1
    box_bits = maps.shape[1].bit_length() - 1
    for bit in range(box_bits):
        mats = maps.at[first + bit]
        source = work.at[bit % 2]
        target = out if bit == box_bits - 1 else work.at[(bit + 1) % 2]
        if bit < lane_bits:
            shift = LANES // lane_boxes << bit
            for g in range(groups):
                value = source[g].astype(F32)
                is_set = (lane_block(value.shape, shift) & 1) == 1
                lower = jnp.where(is_set, pltpu.roll(value, shift, 1), value)
                upper = jnp.where(is_set, value, pltpu.roll(value, LANES - shift, 1))
                stacked = jnp.concatenate([lower, upper], axis=0).astype(BF)
                weights = mats[pl.ds(g * lane_boxes, lane_boxes)]
                target[g] = forward_group(weights, stacked, lane_boxes, rank)
        else:
            inner = 1 << bit - lane_bits
            for g0 in range(groups):
                if g0 & inner:
                    continue
                stacked = jnp.concatenate([source[g0], source[g0 + inner]], axis=0)
                for g in (g0, g0 + inner):
                    weights = mats[pl.ds(g * lane_boxes, lane_boxes)]
                    target[g] = forward_group(weights, stacked, lane_boxes, rank)


def order_kernel(observed, token, out, held, sems, wide):
    total, boxes, points = held.shape
    fetch = pltpu.make_async_copy(observed, held, sems.at[0])
    fetch.start()
    fetch.wait()
    wide[...] = held[...].astype(F32).reshape(wide.shape)
    for t in range(boxes):
        out[t] = wide[pl.ds(t, total, stride=boxes), :].astype(BF)


def target_kernel(chunk, coeffs, final, wanted, token, residual, adjoint):
    groups, rank = coeffs.shape[0], coeffs.shape[1]
    boxes, vectors = residual.shape[0], residual.shape[1]
    box_bits = boxes.bit_length() - 1
    lane_boxes = LANES // vectors
    for g in range(groups):
        turned = jnp.transpose(coeffs[g].astype(F32)).astype(BF)
        for pair in range(lane_boxes // 2):
            kept, mats = [], []
            for b in (2 * pair, 2 * pair + 1):
                t = reverse_bits(g * lane_boxes + b, box_bits)
                mat = final[t]
                value = dot(turned[b * vectors:(b + 1) * vectors], mat)
                target = wanted[t, pl.ds(chunk * vectors, vectors), :].astype(F32)
                value = (value - target).astype(BF)
                residual[t] = value
                kept.append(value)
                mats.append(mat)
            product = dot_nt(jnp.concatenate(kept, axis=0), jnp.concatenate(mats, axis=0))
            adjoint[g * lane_boxes // 2 + pair] = pick_lanes(product, vectors, 2, rank).astype(BF)


def residual_kernel(chunk, part, token, *refs):
    residual, done, held, sems, wide = refs[-5:]
    boxes, vectors = part.shape[0], part.shape[1]
    for t in range(boxes):
        wide[pl.ds(t, vectors, stride=boxes), :] = part[t].astype(F32)
    held[...] = wide[...].reshape(held.shape).astype(BF)
    done[...] = jnp.zeros(done.shape, done.dtype)
    store = pltpu.make_async_copy(
        held, residual.at[pl.ds(chunk * vectors, vectors)], sems.at[0]
    )
    store.start()
    store.wait()


def adjoint_cross_pair(value, mats, kept, sent, p, high):
    rows = value.shape[0]
    low, upper = halves_of(dot(split_rows(value), mats), rows)
    take = jnp.broadcast_to(high, low.shape)
    kept[p] = jnp.where(take, upper, low)
    sent[p] = jnp.where(take, low, upper).astype(BF)


def pair_rows(mats, p):
    rank = mats.shape[1]
    return mats[pl.ds(2 * p, 2)].reshape(2 * rank, LANES)


def local_forward_kernel(level, src_bits, lane_boxes, own, other, maps, token, coeffs, work):
    high = is_high(level, src_bits)
    cross_step(own, other, maps.at[level], work.at[0], high, lane_boxes)
    local_forward(lane_boxes, maps, level + 1, coeffs, work)


def local_adjoint_kernel(level, src_bits, adjoint, maps, token, kept, sent, work):
    pairs, vectors = work.shape[1], work.shape[2]
    box_bits = maps.shape[1].bit_length() - 1
    for step, bit in enumerate(reversed(range(box_bits))):
        mats = maps.at[level + 1 + bit]
        source = work.at[step % 2] if step else adjoint
        target = work.at[(step + 1) % 2]
        if bit == 0:
            for p in range(pairs):
                target[p] = dot(source[p], pair_rows(mats, p)).astype(BF)
        else:
            inner = 1 << bit - 1
            for p0 in range(pairs):
                if p0 & inner:
                    continue
                p1 = p0 + inner
                rows = jnp.concatenate([split_rows(source[p0]), split_rows(source[p1])], axis=1)
                stacked = jnp.concatenate([pair_rows(mats, p0), pair_rows(mats, p1)], axis=0)
                low, upper = halves_of(dot(rows, stacked), vectors)
                target[p0] = low.astype(BF)
                target[p1] = upper.astype(BF)
    source = work.at[box_bits % 2]
    high = is_high(level, src_bits)
    for p in range(pairs):
        adjoint_cross_pair(source[p], pair_rows(maps.at[level], p), kept, sent, p, high)


def adjoint_cross_kernel(level, src_bits, held_part, received, maps, *refs):
    kept, sent = refs[-2:]
    high = is_high(level, src_bits)
    for p in range(held_part.shape[0]):
        value = (held_part[p] + received[p].astype(F32)).astype(BF)
        adjoint_cross_pair(value, pair_rows(maps.at[level], p), kept, sent, p, high)


def gradient_kernel(chunk, held_part, received, leaf, token, *refs):
    gradient, done, held, sems, result = refs[-5:]
    done[...] = jnp.zeros(done.shape, done.dtype)
    pairs, vectors = held_part.shape[0], held_part.shape[1]
    boxes, points = held.shape[1], held.shape[2]
    stores = []
    for part in range(PARTS):
        for p in range(part * pairs // PARTS, (part + 1) * pairs // PARTS):
            value = (held_part[p] + received[p].astype(F32)).astype(BF)
            product = dot(split_rows(value), pair_rows(leaf, p))
            result[pl.ds(2 * p, vectors, stride=boxes), :] = product[:vectors]
            result[pl.ds(2 * p + 1, vectors, stride=boxes), :] = product[vectors:]
        own = pl.ds(part * boxes // PARTS, boxes // PARTS)
        for v in range(vectors):
            rows = result[pl.ds(v * boxes + part * boxes // PARTS, boxes // PARTS), :]
            held[v, own, :] = rows.astype(BF)
        store = pltpu.make_async_copy(
            held.at[:, own, :],
            gradient.at[pl.ds(chunk * vectors, vectors), own, :],
            sems.at[part],
        )
        store.start()
        stores.append(store)
    for store in stores:
        store.wait()


VMEM = pl.BlockSpec(memory_space=pltpu.VMEM)
ANY = pl.BlockSpec(memory_space=pl.ANY)
HBM = pl.BlockSpec(memory_space=pltpu.HBM)


def call(kernel, out_shape, in_specs, out_specs, scratch, flops, moved, limit, aliases=None):
    return pl.pallas_call(
        kernel,
        out_shape=out_shape,
        in_specs=in_specs,
        out_specs=out_specs,
        scratch_shapes=scratch,
        input_output_aliases=aliases or {},
        compiler_params=pltpu.CompilerParams(vmem_limit_bytes=limit << 20),
        cost_estimate=pl.CostEstimate(flops=flops, bytes_accessed=moved, transcendentals=0),
    )


def body(traces, observed, leaf_maps, level_maps, final_maps):
    total = traces.shape[0]
    boxes, points = traces.shape[1], traces.shape[4]
    rank = leaf_maps.shape[3]
    src_count, hi_count = lax.axis_size("src"), lax.axis_size("hi")
    src_bits = src_count.bit_length() - 1
    hi_bits = hi_count.bit_length() - 1
    device_bits = src_bits + hi_bits
    box_bits = boxes.bit_length() - 1
    vectors = total // CHUNKS
    lane_boxes = LANES // vectors
    groups, pairs = boxes // lane_boxes, boxes // 2

    leaf = leaf_maps.reshape(boxes, rank, points)
    final = final_maps.reshape(boxes, rank, points)
    levels = level_maps.reshape(level_maps.shape[0], boxes, rank, 2 * rank)
    samples = traces.reshape(total, boxes, points)
    wanted = observed.reshape(total, boxes, points)

    def shape(*dims, dtype=BF):
        return jax.ShapeDtypeStruct(dims, dtype)

    forward_shape = shape(groups, rank, LANES)
    pair_shape = shape(pairs, vectors, LANES)
    kept_shape = shape(pairs, vectors, LANES, dtype=F32)
    sample_shape = shape(vectors, boxes, points)
    full_shape = shape(total, boxes, points)
    wide = pltpu.VMEM((vectors * boxes, points), F32)
    held = pltpu.VMEM((vectors, boxes, points), BF)
    sems = pltpu.SemaphoreType.DMA((2,))
    flops = 2 * boxes * rank * 2 * rank * vectors
    moved = boxes * rank * 2 * rank * 2

    def exchange(array, level):
        if level < src_bits:
            axis, count, bit = "src", src_count, level
        else:
            axis, count, bit = "hi", hi_count, level - src_bits
        return lax.ppermute(array, axis, [(i, i ^ 1 << bit) for i in range(count)])

    def reversal(array):
        pairs_of = []
        for src in range(src_count):
            for hi in range(hi_count):
                there = reverse_bits(hi * src_count + src, device_bits)
                pairs_of.append(
                    (src * hi_count + hi, there % src_count * hi_count + there // src_count)
                )
        return lax.ppermute(array, ("src", "hi"), pairs_of)

    def leaf_call(*operands):
        scratch = [
            pltpu.VMEM((total, boxes, points), BF), pltpu.VMEM((boxes, rank, points), BF),
            pltpu.SemaphoreType.DMA((CHUNKS + 1,)), wide,
        ]
        return call(
            functools.partial(leaf_kernel, CHUNKS),
            (forward_shape,) * CHUNKS, [HBM] * 2, (VMEM,) * CHUNKS, scratch,
            CHUNKS * flops, 4 * moved, 8,
        )(*operands)

    whole = [
        pltpu.VMEM((total, boxes, points), BF), sems, pltpu.VMEM((total * boxes, points), F32)
    ]

    def order_call(*operands):
        return call(
            order_kernel, shape(boxes, total, points), [HBM, ANY], VMEM, whole, 0, 2 * moved, 8
        )(*operands)

    def target_call(chunk, *operands):
        kernel = functools.partial(target_kernel, chunk)
        return call(
            kernel, (shape(boxes, vectors, points), pair_shape), [VMEM] * 3 + [ANY],
            (VMEM, VMEM), [], 2 * flops, 4 * moved, 8,
        )(*operands)

    done_shape = shape(8, LANES, dtype=F32)

    def residual_call(chunk, *operands):
        return call(
            functools.partial(residual_kernel, chunk), (full_shape, done_shape),
            [VMEM, ANY] + [HBM] * (len(operands) - 2), (HBM, VMEM), [held, sems, wide],
            0, 2 * moved, 8, {2: 0} if len(operands) > 2 else None,
        )(*operands)

    def gradient_call(chunk, *operands):
        return call(
            functools.partial(gradient_kernel, chunk), (full_shape, done_shape),
            [VMEM] * 3 + [ANY] + [HBM] * (len(operands) - 4), (HBM, VMEM),
            [held, pltpu.SemaphoreType.DMA((PARTS,)), wide],
            flops, 2 * moved, 8, {4: 0} if len(operands) > 4 else None,
        )(*operands)

    def cross_call(level, *operands):
        kernel = functools.partial(cross_kernel, level, src_bits, lane_boxes)
        specs = [VMEM] * 3 + [ANY] * (len(operands) - 3)
        return call(kernel, forward_shape, specs, VMEM, [], flops, moved, 4)(*operands)

    def adjoint_call(level, *operands):
        kernel = functools.partial(adjoint_cross_kernel, level, src_bits)
        specs = [VMEM] * 3 + [ANY] * (len(operands) - 3)
        return call(
            kernel, (kept_shape, pair_shape), specs, (VMEM, VMEM), [], flops, moved, 4
        )(*operands)

    def local_forward_call(*operands):
        kernel = functools.partial(local_forward_kernel, top, src_bits, lane_boxes)
        scratch = [pltpu.VMEM((2, groups, rank, LANES), BF)]
        return call(
            kernel, forward_shape, [VMEM] * 3 + [ANY], VMEM, scratch, 7 * flops, 7 * moved, 8
        )(*operands)

    def local_adjoint_call(*operands):
        kernel = functools.partial(local_adjoint_kernel, top, src_bits)
        scratch = [pltpu.VMEM((2, pairs, vectors, LANES), BF)]
        return call(
            kernel, (kept_shape, pair_shape), [VMEM] * 2 + [ANY], (VMEM, VMEM), scratch,
            7 * flops, 7 * moved, 8,
        )(*operands)

    top = device_bits - 1
    every = range(CHUNKS)
    coeffs, kept, sent = [None] * CHUNKS, [None] * CHUNKS, [None] * CHUNKS
    coeffs = list(leaf_call(samples, leaf))
    token = coeffs[0]
    by_box = [None] * CHUNKS
    residual, gradient = (), ()
    first_back = top + 1 + 2 * GAP
    stages = first_back + top
    for step in range(stages + 1 + LAG * (CHUNKS - 1)):
        for c in every if step < first_back else reversed(every):
            stage = step - LAG * c
            if 0 <= stage < top:
                level = stage
                maps = levels[level:level + 1] if level < EARLY else levels
                coeffs[c] = token = cross_call(
                    level, coeffs[c], exchange(coeffs[c], level), maps, token
                )
            elif stage == top:
                coeffs[c] = token = local_forward_call(
                    coeffs[c], exchange(coeffs[c], top), levels, token
                )
            elif stage == top + GAP:
                by_box[c], sent[c] = target_call(c, reversal(coeffs[c]), final, wanted, token)
                token = sent[c]
            elif stage == top + 2 * GAP:
                kept[c], sent[c] = local_adjoint_call(reversal(sent[c]), levels, token)
                token = sent[c]
            elif first_back <= stage < stages:
                level = top - 1 - (stage - first_back)
                kept[c], sent[c] = adjoint_call(
                    level, kept[c], exchange(sent[c], level + 1), levels, token
                )
                token = sent[c]
            elif stage == stages:
                *gradient, token = gradient_call(
                    c, kept[c], exchange(sent[c], 0), leaf, token, *gradient
                )
            if (stage, c) == (2, CHUNKS - 1):
                wanted = token = order_call(wanted, token)
            if stage == first_back + 2:
                *residual, token = residual_call(c, by_box[c], token, *residual)
    residual, gradient = residual[0], gradient[0]
    return (
        residual.reshape(total, 1, 1, boxes, points),
        gradient.reshape(total, boxes, 1, 1, points),
    )


def solution(mesh):
    placed = (
        P(None, None, "hi", "src", None),
        P(None, "hi", "src", None, None),
        P(None, "hi", "src", None, None),
        P(None, None, "hi", "src", None, None),
        P("hi", "src", None, None, None),
    )
    return jax.shard_map(
        body,
        mesh=mesh,
        in_specs=placed,
        out_specs=(P(None, "hi", "src", None, None), P(None, None, "hi", "src", None)),
        check_vma=False,
    )
```

```python
import functools

import jax
import jax.numpy as jnp
from jax import lax
from jax.experimental import pallas as pl
from jax.experimental.pallas import tpu as pltpu
from jax.sharding import PartitionSpec as P

CHUNKS = 2
PARTS = 4
EARLY = 3
LAG = 1
GAP = 2
LANES = 128
BF = jnp.bfloat16
F32 = jnp.float32


def reverse_bits(value, bits):
    return int(format(value, f"0{bits}b")[::-1], 2)


def lane_block(shape, width):
    return lax.broadcasted_iota(jnp.int32, shape, len(shape) - 1) // width


def pick_lanes(product, rows, count, width):
    block = lane_block((rows, LANES), width)
    out = product[:rows]
    for b in range(1, count):
        out = jnp.where(block == b, product[b * rows:(b + 1) * rows], out)
    return out


def split_rows(pair):
    left = lane_block(pair.shape, LANES // 2) == 0
    zero = jnp.zeros(pair.shape, pair.dtype)
    return jnp.concatenate([jnp.where(left, pair, zero), jnp.where(left, zero, pair)], axis=0)


def halves_of(product, rows):
    first, second = product[:rows], product[rows:]
    left = lane_block((rows, LANES), LANES // 2) == 0
    low = jnp.where(left, first, pltpu.roll(second, LANES // 2, 1))
    high = jnp.where(left, pltpu.roll(first, LANES // 2, 1), second)
    return low, high


def is_high(level, src_bits):
    if level < src_bits:
        return (lax.axis_index("src") >> level & 1) == 1
    return (lax.axis_index("hi") >> (level - src_bits) & 1) == 1


def dot(a, b):
    return jnp.dot(a, b, preferred_element_type=F32)


def dot_nt(a, b):
    return lax.dot_general(a, b, (((1,), (1,)), ((), ())), preferred_element_type=F32)


def leaf_kernel(chunks, traces, leaf, *refs):
    outs = refs[:chunks]
    held, mats, sems, wide = refs[chunks:]
    total, boxes, points = held.shape
    vectors = total // chunks
    lane_boxes = LANES // vectors
    rank = mats.shape[1]
    copies = [
        pltpu.make_async_copy(
            traces.at[pl.ds(c * vectors, vectors)], held.at[pl.ds(c * vectors, vectors)], sems.at[c]
        )
        for c in range(chunks)
    ]
    copies.append(pltpu.make_async_copy(leaf, mats, sems.at[chunks]))
    for copy in copies:
        copy.start()
    for c in range(chunks):
        copies[c].wait()
        rows = held[pl.ds(c * vectors, vectors)].astype(F32)
        wide[...] = rows.reshape(wide.shape)
        if c == 0:
            copies[chunks].wait()
        for g in range(boxes // lane_boxes):
            rows = [
                wide[pl.ds(g * lane_boxes + b, vectors, stride=boxes), :]
                for b in range(lane_boxes)
            ]
            stacked = jnp.concatenate(rows, axis=0).astype(BF)
            group = mats[pl.ds(g * lane_boxes, lane_boxes)].reshape(lane_boxes * rank, points)
            outs[c][g] = pick_lanes(dot_nt(group, stacked), rank, lane_boxes, vectors).astype(BF)


def forward_group(weights, stacked, lane_boxes, rank):
    mats = weights.reshape(lane_boxes * rank, LANES)
    return pick_lanes(dot(mats, stacked), rank, lane_boxes, LANES // lane_boxes).astype(BF)


def cross_step(own, other, mats, out, high, lane_boxes):
    groups, rank = own.shape[0], own.shape[1]
    for g in range(groups):
        mine, theirs = own[g], other[g]
        take = jnp.broadcast_to(high, mine.shape)
        lower = jnp.where(take, theirs, mine)
        upper = jnp.where(take, mine, theirs)
        stacked = jnp.concatenate([lower, upper], axis=0)
        weights = mats[pl.ds(g * lane_boxes, lane_boxes)]
        out[g] = forward_group(weights, stacked, lane_boxes, rank)


def cross_kernel(level, src_bits, lane_boxes, own, other, maps, *refs):
    mats = maps.at[level if maps.shape[0] > 1 else 0]
    cross_step(own, other, mats, refs[-1], is_high(level, src_bits), lane_boxes)


def local_forward(lane_boxes, maps, first, out, work):
    groups, rank = out.shape[0], out.shape[1]
    lane_bits = lane_boxes.bit_length() - 1
    box_bits = maps.shape[1].bit_length() - 1
    for bit in range(box_bits):
        mats = maps.at[first + bit]
        source = work.at[bit % 2]
        target = out if bit == box_bits - 1 else work.at[(bit + 1) % 2]
        if bit < lane_bits:
            shift = LANES // lane_boxes << bit
            for g in range(groups):
                value = source[g].astype(F32)
                is_set = (lane_block(value.shape, shift) & 1) == 1
                lower = jnp.where(is_set, pltpu.roll(value, shift, 1), value)
                upper = jnp.where(is_set, value, pltpu.roll(value, LANES - shift, 1))
                stacked = jnp.concatenate([lower, upper], axis=0).astype(BF)
                weights = mats[pl.ds(g * lane_boxes, lane_boxes)]
                target[g] = forward_group(weights, stacked, lane_boxes, rank)
        else:
            inner = 1 << bit - lane_bits
            for g0 in range(groups):
                if g0 & inner:
                    continue
                stacked = jnp.concatenate([source[g0], source[g0 + inner]], axis=0)
                for g in (g0, g0 + inner):
                    weights = mats[pl.ds(g * lane_boxes, lane_boxes)]
                    target[g] = forward_group(weights, stacked, lane_boxes, rank)


def order_kernel(observed, token, out, held, sems, wide):
    total, boxes, points = held.shape
    fetch = pltpu.make_async_copy(observed, held, sems.at[0])
    fetch.start()
    fetch.wait()
    wide[...] = held[...].astype(F32).reshape(wide.shape)
    for t in range(boxes):
        out[t] = wide[pl.ds(t, total, stride=boxes), :].astype(BF)


def target_kernel(chunk, coeffs, final, wanted, token, residual, adjoint):
    groups, rank = coeffs.shape[0], coeffs.shape[1]
    boxes, vectors = residual.shape[0], residual.shape[1]
    box_bits = boxes.bit_length() - 1
    lane_boxes = LANES // vectors
    for g in range(groups):
        turned = jnp.transpose(coeffs[g].astype(F32)).astype(BF)
        for pair in range(lane_boxes // 2):
            kept, mats = [], []
            for b in (2 * pair, 2 * pair + 1):
                t = reverse_bits(g * lane_boxes + b, box_bits)
                mat = final[t]
                value = dot(turned[b * vectors:(b + 1) * vectors], mat)
                target = wanted[t, pl.ds(chunk * vectors, vectors), :].astype(F32)
                value = (value - target).astype(BF)
                residual[t] = value
                kept.append(value)
                mats.append(mat)
            product = dot_nt(jnp.concatenate(kept, axis=0), jnp.concatenate(mats, axis=0))
            adjoint[g * lane_boxes // 2 + pair] = pick_lanes(product, vectors, 2, rank).astype(BF)


def residual_kernel(chunk, part, token, *refs):
    residual, done, held, sems, wide = refs[-5:]
    boxes, vectors = part.shape[0], part.shape[1]
    for t in range(boxes):
        wide[pl.ds(t, vectors, stride=boxes), :] = part[t].astype(F32)
    held[...] = wide[...].reshape(held.shape).astype(BF)
    done[...] = jnp.zeros(done.shape, done.dtype)
    store = pltpu.make_async_copy(
        held, residual.at[pl.ds(chunk * vectors, vectors)], sems.at[0]
    )
    store.start()
    store.wait()


def adjoint_cross_pair(value, mats, kept, sent, p, high):
    rows = value.shape[0]
    low, upper = halves_of(dot(split_rows(value), mats), rows)
    take = jnp.broadcast_to(high, low.shape)
    kept[p] = jnp.where(take, upper, low)
    sent[p] = jnp.where(take, low, upper).astype(BF)


def pair_rows(mats, p):
    rank = mats.shape[1]
    return mats[pl.ds(2 * p, 2)].reshape(2 * rank, LANES)


def local_forward_kernel(level, src_bits, lane_boxes, own, other, maps, token, coeffs, work):
    high = is_high(level, src_bits)
    cross_step(own, other, maps.at[level], work.at[0], high, lane_boxes)
    local_forward(lane_boxes, maps, level + 1, coeffs, work)


def local_adjoint_kernel(level, src_bits, adjoint, maps, token, kept, sent, work):
    pairs, vectors = work.shape[1], work.shape[2]
    box_bits = maps.shape[1].bit_length() - 1
    for step, bit in enumerate(reversed(range(box_bits))):
        mats = maps.at[level + 1 + bit]
        source = work.at[step % 2] if step else adjoint
        target = work.at[(step + 1) % 2]
        if bit == 0:
            for p in range(pairs):
                target[p] = dot(source[p], pair_rows(mats, p)).astype(BF)
        else:
            inner = 1 << bit - 1
            for p0 in range(pairs):
                if p0 & inner:
                    continue
                p1 = p0 + inner
                rows = jnp.concatenate([split_rows(source[p0]), split_rows(source[p1])], axis=1)
                stacked = jnp.concatenate([pair_rows(mats, p0), pair_rows(mats, p1)], axis=0)
                low, upper = halves_of(dot(rows, stacked), vectors)
                target[p0] = low.astype(BF)
                target[p1] = upper.astype(BF)
    source = work.at[box_bits % 2]
    high = is_high(level, src_bits)
    for p in range(pairs):
        adjoint_cross_pair(source[p], pair_rows(maps.at[level], p), kept, sent, p, high)


def adjoint_cross_kernel(level, src_bits, held_part, received, maps, *refs):
    kept, sent = refs[-2:]
    high = is_high(level, src_bits)
    for p in range(held_part.shape[0]):
        value = (held_part[p] + received[p].astype(F32)).astype(BF)
        adjoint_cross_pair(value, pair_rows(maps.at[level], p), kept, sent, p, high)


def gradient_kernel(chunk, held_part, received, leaf, token, *refs):
    gradient, done, held, sems, result = refs[-5:]
    done[...] = jnp.zeros(done.shape, done.dtype)
    pairs, vectors = held_part.shape[0], held_part.shape[1]
    boxes, points = held.shape[1], held.shape[2]
    stores = []
    for part in range(PARTS):
        for p in range(part * pairs // PARTS, (part + 1) * pairs // PARTS):
            value = (held_part[p] + received[p].astype(F32)).astype(BF)
            product = dot(split_rows(value), pair_rows(leaf, p))
            result[pl.ds(2 * p, vectors, stride=boxes), :] = product[:vectors]
            result[pl.ds(2 * p + 1, vectors, stride=boxes), :] = product[vectors:]
        own = pl.ds(part * boxes // PARTS, boxes // PARTS)
        for v in range(vectors):
            rows = result[pl.ds(v * boxes + part * boxes // PARTS, boxes // PARTS), :]
            held[v, own, :] = rows.astype(BF)
        store = pltpu.make_async_copy(
            held.at[:, own, :],
            gradient.at[pl.ds(chunk * vectors, vectors), own, :],
            sems.at[part],
        )
        store.start()
        stores.append(store)
    for store in stores:
        store.wait()


VMEM = pl.BlockSpec(memory_space=pltpu.VMEM)
ANY = pl.BlockSpec(memory_space=pl.ANY)
HBM = pl.BlockSpec(memory_space=pltpu.HBM)


def call(kernel, out_shape, in_specs, out_specs, scratch, flops, moved, limit, aliases=None):
    return pl.pallas_call(
        kernel,
        out_shape=out_shape,
        in_specs=in_specs,
        out_specs=out_specs,
        scratch_shapes=scratch,
        input_output_aliases=aliases or {},
        compiler_params=pltpu.CompilerParams(vmem_limit_bytes=limit << 20),
        cost_estimate=pl.CostEstimate(flops=flops, bytes_accessed=moved, transcendentals=0),
    )


def body(traces, observed, leaf_maps, level_maps, final_maps):
    total = traces.shape[0]
    boxes, points = traces.shape[1], traces.shape[4]
    rank = leaf_maps.shape[3]
    src_count, hi_count = lax.axis_size("src"), lax.axis_size("hi")
    src_bits = src_count.bit_length() - 1
    hi_bits = hi_count.bit_length() - 1
    device_bits = src_bits + hi_bits
    box_bits = boxes.bit_length() - 1
    vectors = total // CHUNKS
    lane_boxes = LANES // vectors
    groups, pairs = boxes // lane_boxes, boxes // 2

    leaf = leaf_maps.reshape(boxes, rank, points)
    final = final_maps.reshape(boxes, rank, points)
    levels = level_maps.reshape(level_maps.shape[0], boxes, rank, 2 * rank)
    samples = traces.reshape(total, boxes, points)
    wanted = observed.reshape(total, boxes, points)

    def shape(*dims, dtype=BF):
        return jax.ShapeDtypeStruct(dims, dtype)

    forward_shape = shape(groups, rank, LANES)
    pair_shape = shape(pairs, vectors, LANES)
    kept_shape = shape(pairs, vectors, LANES, dtype=F32)
    sample_shape = shape(vectors, boxes, points)
    full_shape = shape(total, boxes, points)
    wide = pltpu.VMEM((vectors * boxes, points), F32)
    held = pltpu.VMEM((vectors, boxes, points), BF)
    sems = pltpu.SemaphoreType.DMA((2,))
    flops = 2 * boxes * rank * 2 * rank * vectors
    moved = boxes * rank * 2 * rank * 2

    def exchange(array, level):
        if level < src_bits:
            axis, count, bit = "src", src_count, level
        else:
            axis, count, bit = "hi", hi_count, level - src_bits
        return lax.ppermute(array, axis, [(i, i ^ 1 << bit) for i in range(count)])

    def reversal(array):
        pairs_of = []
        for src in range(src_count):
            for hi in range(hi_count):
                there = reverse_bits(hi * src_count + src, device_bits)
                pairs_of.append(
                    (src * hi_count + hi, there % src_count * hi_count + there // src_count)
                )
        return lax.ppermute(array, ("src", "hi"), pairs_of)

    def leaf_call(*operands):
        scratch = [
            pltpu.VMEM((total, boxes, points), BF), pltpu.VMEM((boxes, rank, points), BF),
            pltpu.SemaphoreType.DMA((CHUNKS + 1,)), wide,
        ]
        return call(
            functools.partial(leaf_kernel, CHUNKS),
            (forward_shape,) * CHUNKS, [HBM] * 2, (VMEM,) * CHUNKS, scratch,
            CHUNKS * flops, 4 * moved, 8,
        )(*operands)

    whole = [
        pltpu.VMEM((total, boxes, points), BF), sems, pltpu.VMEM((total * boxes, points), F32)
    ]

    def order_call(*operands):
        return call(
            order_kernel, shape(boxes, total, points), [HBM, ANY], VMEM, whole, 0, 2 * moved, 8
        )(*operands)

    def target_call(chunk, *operands):
        kernel = functools.partial(target_kernel, chunk)
        return call(
            kernel, (shape(boxes, vectors, points), pair_shape), [VMEM] * 3 + [ANY],
            (VMEM, VMEM), [], 2 * flops, 4 * moved, 8,
        )(*operands)

    done_shape = shape(8, LANES, dtype=F32)

    def residual_call(chunk, *operands):
        return call(
            functools.partial(residual_kernel, chunk), (full_shape, done_shape),
            [VMEM, ANY] + [HBM] * (len(operands) - 2), (HBM, VMEM), [held, sems, wide],
            0, 2 * moved, 8, {2: 0} if len(operands) > 2 else None,
        )(*operands)

    def gradient_call(chunk, *operands):
        return call(
            functools.partial(gradient_kernel, chunk), (full_shape, done_shape),
            [VMEM] * 3 + [ANY] + [HBM] * (len(operands) - 4), (HBM, VMEM),
            [held, pltpu.SemaphoreType.DMA((PARTS,)), wide],
            flops, 2 * moved, 8, {4: 0} if len(operands) > 4 else None,
        )(*operands)

    def cross_call(level, *operands):
        kernel = functools.partial(cross_kernel, level, src_bits, lane_boxes)
        specs = [VMEM] * 3 + [ANY] * (len(operands) - 3)
        return call(kernel, forward_shape, specs, VMEM, [], flops, moved, 4)(*operands)

    def adjoint_call(level, *operands):
        kernel = functools.partial(adjoint_cross_kernel, level, src_bits)
        specs = [VMEM] * 3 + [ANY] * (len(operands) - 3)
        return call(
            kernel, (kept_shape, pair_shape), specs, (VMEM, VMEM), [], flops, moved, 4
        )(*operands)

    def local_forward_call(*operands):
        kernel = functools.partial(local_forward_kernel, top, src_bits, lane_boxes)
        scratch = [pltpu.VMEM((2, groups, rank, LANES), BF)]
        return call(
            kernel, forward_shape, [VMEM] * 3 + [ANY], VMEM, scratch, 7 * flops, 7 * moved, 8
        )(*operands)

    def local_adjoint_call(*operands):
        kernel = functools.partial(local_adjoint_kernel, top, src_bits)
        scratch = [pltpu.VMEM((2, pairs, vectors, LANES), BF)]
        return call(
            kernel, (kept_shape, pair_shape), [VMEM] * 2 + [ANY], (VMEM, VMEM), scratch,
            7 * flops, 7 * moved, 8,
        )(*operands)

    top = device_bits - 1
    every = range(CHUNKS)
    coeffs, kept, sent = [None] * CHUNKS, [None] * CHUNKS, [None] * CHUNKS
    coeffs = list(leaf_call(samples, leaf))
    token = coeffs[0]
    by_box = [None] * CHUNKS
    residual, gradient = (), ()
    first_back = top + 1 + 2 * GAP
    stages = first_back + top
    for step in range(stages + 1 + LAG * (CHUNKS - 1)):
        for c in reversed(every) if step == first_back else every:
            stage = step - LAG * c
            if 0 <= stage < top:
                level = stage
                maps = levels[level:level + 1] if level < EARLY else levels
                coeffs[c] = token = cross_call(
                    level, coeffs[c], exchange(coeffs[c], level), maps, token
                )
            elif stage == top:
                coeffs[c] = token = local_forward_call(
                    coeffs[c], exchange(coeffs[c], top), levels, token
                )
            elif stage == top + GAP:
                by_box[c], sent[c] = target_call(c, reversal(coeffs[c]), final, wanted, token)
                token = sent[c]
            elif stage == top + 2 * GAP:
                kept[c], sent[c] = local_adjoint_call(reversal(sent[c]), levels, token)
                token = sent[c]
            elif first_back <= stage < stages:
                level = top - 1 - (stage - first_back)
                kept[c], sent[c] = adjoint_call(
                    level, kept[c], exchange(sent[c], level + 1), levels, token
                )
                token = sent[c]
            elif stage == stages:
                *gradient, token = gradient_call(
                    c, kept[c], exchange(sent[c], 0), leaf, token, *gradient
                )
            if (stage, c) == (2, CHUNKS - 1):
                wanted = token = order_call(wanted, token)
            if (stage, c) in ((top + GAP, CHUNKS - 1), (top + 2 * GAP, 0)):
                part = 0 if c else 1
                *residual, token = residual_call(part, by_box[part], token, *residual)
    residual, gradient = residual[0], gradient[0]
    return (
        residual.reshape(total, 1, 1, boxes, points),
        gradient.reshape(total, boxes, 1, 1, points),
    )


def solution(mesh):
    placed = (
        P(None, None, "hi", "src", None),
        P(None, "hi", "src", None, None),
        P(None, "hi", "src", None, None),
        P(None, None, "hi", "src", None, None),
        P("hi", "src", None, None, None),
    )
    return jax.shard_map(
        body,
        mesh=mesh,
        in_specs=placed,
        out_specs=(P(None, "hi", "src", None, None), P(None, None, "hi", "src", None)),
        check_vma=False,
    )
```

```python
import functools

import jax
import jax.numpy as jnp
from jax import lax
from jax.experimental import pallas as pl
from jax.experimental.pallas import tpu as pltpu
from jax.sharding import PartitionSpec as P

CHUNKS = 2
PARTS = 4
EARLY = 3
LAG = 1
GAP = 2
LANES = 128
BF = jnp.bfloat16
F32 = jnp.float32


def reverse_bits(value, bits):
    return int(format(value, f"0{bits}b")[::-1], 2)


def lane_block(shape, width):
    return lax.broadcasted_iota(jnp.int32, shape, len(shape) - 1) // width


def pick_lanes(product, rows, count, width):
    block = lane_block((rows, LANES), width)
    out = product[:rows]
    for b in range(1, count):
        out = jnp.where(block == b, product[b * rows:(b + 1) * rows], out)
    return out


def split_rows(pair):
    left = lane_block(pair.shape, LANES // 2) == 0
    zero = jnp.zeros(pair.shape, pair.dtype)
    return jnp.concatenate([jnp.where(left, pair, zero), jnp.where(left, zero, pair)], axis=0)


def halves_of(product, rows):
    first, second = product[:rows], product[rows:]
    left = lane_block((rows, LANES), LANES // 2) == 0
    low = jnp.where(left, first, pltpu.roll(second, LANES // 2, 1))
    high = jnp.where(left, pltpu.roll(first, LANES // 2, 1), second)
    return low, high


def is_high(level, src_bits):
    if level < src_bits:
        return (lax.axis_index("src") >> level & 1) == 1
    return (lax.axis_index("hi") >> (level - src_bits) & 1) == 1


def dot(a, b):
    return jnp.dot(a, b, preferred_element_type=F32)


def dot_nt(a, b):
    return lax.dot_general(a, b, (((1,), (1,)), ((), ())), preferred_element_type=F32)


def leaf_kernel(chunks, traces, leaf, *refs):
    outs = refs[:chunks]
    held, mats, sems, wide = refs[chunks:]
    total, boxes, points = held.shape
    vectors = total // chunks
    lane_boxes = LANES // vectors
    rank = mats.shape[1]
    copies = [
        pltpu.make_async_copy(
            traces.at[pl.ds(c * vectors, vectors)], held.at[pl.ds(c * vectors, vectors)], sems.at[c]
        )
        for c in range(chunks)
    ]
    copies.append(pltpu.make_async_copy(leaf, mats, sems.at[chunks]))
    for copy in copies:
        copy.start()
    for c in range(chunks):
        copies[c].wait()
        rows = held[pl.ds(c * vectors, vectors)].astype(F32)
        wide[...] = rows.reshape(wide.shape)
        if c == 0:
            copies[chunks].wait()
        for g in range(boxes // lane_boxes):
            rows = [
                wide[pl.ds(g * lane_boxes + b, vectors, stride=boxes), :]
                for b in range(lane_boxes)
            ]
            stacked = jnp.concatenate(rows, axis=0).astype(BF)
            group = mats[pl.ds(g * lane_boxes, lane_boxes)].reshape(lane_boxes * rank, points)
            outs[c][g] = pick_lanes(dot_nt(group, stacked), rank, lane_boxes, vectors).astype(BF)


def forward_group(weights, stacked, lane_boxes, rank):
    mats = weights.reshape(lane_boxes * rank, LANES)
    return pick_lanes(dot(mats, stacked), rank, lane_boxes, LANES // lane_boxes).astype(BF)


def cross_step(own, other, mats, out, high, lane_boxes):
    groups, rank = own.shape[0], own.shape[1]
    for g in range(groups):
        mine, theirs = own[g], other[g]
        take = jnp.broadcast_to(high, mine.shape)
        lower = jnp.where(take, theirs, mine)
        upper = jnp.where(take, mine, theirs)
        stacked = jnp.concatenate([lower, upper], axis=0)
        weights = mats[pl.ds(g * lane_boxes, lane_boxes)]
        out[g] = forward_group(weights, stacked, lane_boxes, rank)


def cross_kernel(level, src_bits, lane_boxes, own, other, maps, *refs):
    mats = maps.at[level if maps.shape[0] > 1 else 0]
    cross_step(own, other, mats, refs[-1], is_high(level, src_bits), lane_boxes)


def local_forward(lane_boxes, maps, first, out, work):
    groups, rank = out.shape[0], out.shape[1]
    lane_bits = lane_boxes.bit_length() - 1
    box_bits = maps.shape[1].bit_length() - 1
    for bit in range(box_bits):
        mats = maps.at[first + bit]
        source = work.at[bit % 2]
        target = out if bit == box_bits - 1 else work.at[(bit + 1) % 2]
        if bit < lane_bits:
            shift = LANES // lane_boxes << bit
            for g in range(groups):
                value = source[g].astype(F32)
                is_set = (lane_block(value.shape, shift) & 1) == 1
                lower = jnp.where(is_set, pltpu.roll(value, shift, 1), value)
                upper = jnp.where(is_set, value, pltpu.roll(value, LANES - shift, 1))
                stacked = jnp.concatenate([lower, upper], axis=0).astype(BF)
                weights = mats[pl.ds(g * lane_boxes, lane_boxes)]
                target[g] = forward_group(weights, stacked, lane_boxes, rank)
        else:
            inner = 1 << bit - lane_bits
            for g0 in range(groups):
                if g0 & inner:
                    continue
                stacked = jnp.concatenate([source[g0], source[g0 + inner]], axis=0)
                for g in (g0, g0 + inner):
                    weights = mats[pl.ds(g * lane_boxes, lane_boxes)]
                    target[g] = forward_group(weights, stacked, lane_boxes, rank)


def order_kernel(observed, token, out, held, sems, wide):
    total, boxes, points = held.shape
    fetch = pltpu.make_async_copy(observed, held, sems.at[0])
    fetch.start()
    fetch.wait()
    wide[...] = held[...].astype(F32).reshape(wide.shape)
    for t in range(boxes):
        out[t] = wide[pl.ds(t, total, stride=boxes), :].astype(BF)


def target_kernel(chunk, coeffs, final, wanted, token, residual, adjoint):
    groups, rank = coeffs.shape[0], coeffs.shape[1]
    boxes, vectors = residual.shape[0], residual.shape[1]
    box_bits = boxes.bit_length() - 1
    lane_boxes = LANES // vectors
    for g in range(groups):
        turned = jnp.transpose(coeffs[g].astype(F32)).astype(BF)
        for pair in range(lane_boxes // 2):
            kept, mats = [], []
            for b in (2 * pair, 2 * pair + 1):
                t = reverse_bits(g * lane_boxes + b, box_bits)
                mat = final[t]
                value = dot(turned[b * vectors:(b + 1) * vectors], mat)
                target = wanted[t, pl.ds(chunk * vectors, vectors), :].astype(F32)
                value = (value - target).astype(BF)
                residual[t] = value
                kept.append(value)
                mats.append(mat)
            product = dot_nt(jnp.concatenate(kept, axis=0), jnp.concatenate(mats, axis=0))
            adjoint[g * lane_boxes // 2 + pair] = pick_lanes(product, vectors, 2, rank).astype(BF)


def residual_kernel(chunk, part, token, *refs):
    residual, done, held, sems, wide = refs[-5:]
    boxes, vectors = part.shape[0], part.shape[1]
    for t in range(boxes):
        wide[pl.ds(t, vectors, stride=boxes), :] = part[t].astype(F32)
    held[...] = wide[...].reshape(held.shape).astype(BF)
    done[...] = jnp.zeros(done.shape, done.dtype)
    store = pltpu.make_async_copy(
        held, residual.at[pl.ds(chunk * vectors, vectors)], sems.at[0]
    )
    store.start()
    store.wait()


def adjoint_cross_pair(value, mats, kept, sent, p, high):
    rows = value.shape[0]
    low, upper = halves_of(dot(split_rows(value), mats), rows)
    take = jnp.broadcast_to(high, low.shape)
    kept[p] = jnp.where(take, upper, low)
    sent[p] = jnp.where(take, low, upper).astype(BF)


def pair_rows(mats, p):
    rank = mats.shape[1]
    return mats[pl.ds(2 * p, 2)].reshape(2 * rank, LANES)


def local_forward_kernel(level, src_bits, lane_boxes, own, other, maps, token, coeffs, work):
    high = is_high(level, src_bits)
    cross_step(own, other, maps.at[level], work.at[0], high, lane_boxes)
    local_forward(lane_boxes, maps, level + 1, coeffs, work)


def local_adjoint_kernel(level, src_bits, adjoint, maps, token, kept, sent, work):
    pairs, vectors = work.shape[1], work.shape[2]
    box_bits = maps.shape[1].bit_length() - 1
    for step, bit in enumerate(reversed(range(box_bits))):
        mats = maps.at[level + 1 + bit]
        source = work.at[step % 2] if step else adjoint
        target = work.at[(step + 1) % 2]
        if bit == 0:
            for p in range(pairs):
                target[p] = dot(source[p], pair_rows(mats, p)).astype(BF)
        else:
            inner = 1 << bit - 1
            for p0 in range(pairs):
                if p0 & inner:
                    continue
                p1 = p0 + inner
                rows = jnp.concatenate([split_rows(source[p0]), split_rows(source[p1])], axis=1)
                stacked = jnp.concatenate([pair_rows(mats, p0), pair_rows(mats, p1)], axis=0)
                low, upper = halves_of(dot(rows, stacked), vectors)
                target[p0] = low.astype(BF)
                target[p1] = upper.astype(BF)
    source = work.at[box_bits % 2]
    high = is_high(level, src_bits)
    for p in range(pairs):
        adjoint_cross_pair(source[p], pair_rows(maps.at[level], p), kept, sent, p, high)


def adjoint_cross_kernel(level, src_bits, held_part, received, maps, *refs):
    kept, sent = refs[-2:]
    high = is_high(level, src_bits)
    for p in range(held_part.shape[0]):
        value = (held_part[p] + received[p].astype(F32)).astype(BF)
        adjoint_cross_pair(value, pair_rows(maps.at[level], p), kept, sent, p, high)


def gradient_kernel(chunk, held_part, received, leaf, token, *refs):
    gradient, done, held, sems, result = refs[-5:]
    done[...] = jnp.zeros(done.shape, done.dtype)
    pairs, vectors = held_part.shape[0], held_part.shape[1]
    boxes, points = held.shape[1], held.shape[2]
    stores = []
    for part in range(PARTS):
        for p in range(part * pairs // PARTS, (part + 1) * pairs // PARTS):
            value = (held_part[p] + received[p].astype(F32)).astype(BF)
            product = dot(split_rows(value), pair_rows(leaf, p))
            result[pl.ds(2 * p, vectors, stride=boxes), :] = product[:vectors]
            result[pl.ds(2 * p + 1, vectors, stride=boxes), :] = product[vectors:]
        own = pl.ds(part * boxes // PARTS, boxes // PARTS)
        for v in range(vectors):
            rows = result[pl.ds(v * boxes + part * boxes // PARTS, boxes // PARTS), :]
            held[v, own, :] = rows.astype(BF)
        store = pltpu.make_async_copy(
            held.at[:, own, :],
            gradient.at[pl.ds(chunk * vectors, vectors), own, :],
            sems.at[part],
        )
        store.start()
        stores.append(store)
    for store in stores:
        store.wait()


VMEM = pl.BlockSpec(memory_space=pltpu.VMEM)
ANY = pl.BlockSpec(memory_space=pl.ANY)
HBM = pl.BlockSpec(memory_space=pltpu.HBM)


def call(kernel, out_shape, in_specs, out_specs, scratch, flops, moved, limit, aliases=None):
    return pl.pallas_call(
        kernel,
        out_shape=out_shape,
        in_specs=in_specs,
        out_specs=out_specs,
        scratch_shapes=scratch,
        input_output_aliases=aliases or {},
        compiler_params=pltpu.CompilerParams(vmem_limit_bytes=limit << 20),
        cost_estimate=pl.CostEstimate(flops=flops, bytes_accessed=moved, transcendentals=0),
    )


def body(traces, observed, leaf_maps, level_maps, final_maps):
    total = traces.shape[0]
    boxes, points = traces.shape[1], traces.shape[4]
    rank = leaf_maps.shape[3]
    src_count, hi_count = lax.axis_size("src"), lax.axis_size("hi")
    src_bits = src_count.bit_length() - 1
    hi_bits = hi_count.bit_length() - 1
    device_bits = src_bits + hi_bits
    box_bits = boxes.bit_length() - 1
    vectors = total // CHUNKS
    lane_boxes = LANES // vectors
    groups, pairs = boxes // lane_boxes, boxes // 2

    leaf = leaf_maps.reshape(boxes, rank, points)
    final = final_maps.reshape(boxes, rank, points)
    levels = level_maps.reshape(level_maps.shape[0], boxes, rank, 2 * rank)
    samples = traces.reshape(total, boxes, points)
    wanted = observed.reshape(total, boxes, points)

    def shape(*dims, dtype=BF):
        return jax.ShapeDtypeStruct(dims, dtype)

    forward_shape = shape(groups, rank, LANES)
    pair_shape = shape(pairs, vectors, LANES)
    kept_shape = shape(pairs, vectors, LANES, dtype=F32)
    sample_shape = shape(vectors, boxes, points)
    full_shape = shape(total, boxes, points)
    wide = pltpu.VMEM((vectors * boxes, points), F32)
    held = pltpu.VMEM((vectors, boxes, points), BF)
    sems = pltpu.SemaphoreType.DMA((2,))
    flops = 2 * boxes * rank * 2 * rank * vectors
    moved = boxes * rank * 2 * rank * 2

    def exchange(array, level):
        if level < src_bits:
            axis, count, bit = "src", src_count, level
        else:
            axis, count, bit = "hi", hi_count, level - src_bits
        return lax.ppermute(array, axis, [(i, i ^ 1 << bit) for i in range(count)])

    def reversal(array):
        pairs_of = []
        for src in range(src_count):
            for hi in range(hi_count):
                there = reverse_bits(hi * src_count + src, device_bits)
                pairs_of.append(
                    (src * hi_count + hi, there % src_count * hi_count + there // src_count)
                )
        return lax.ppermute(array, ("src", "hi"), pairs_of)

    def leaf_call(*operands):
        scratch = [
            pltpu.VMEM((total, boxes, points), BF), pltpu.VMEM((boxes, rank, points), BF),
            pltpu.SemaphoreType.DMA((CHUNKS + 1,)), wide,
        ]
        return call(
            functools.partial(leaf_kernel, CHUNKS),
            (forward_shape,) * CHUNKS, [HBM] * 2, (VMEM,) * CHUNKS, scratch,
            CHUNKS * flops, 4 * moved, 8,
        )(*operands)

    whole = [
        pltpu.VMEM((total, boxes, points), BF), sems, pltpu.VMEM((total * boxes, points), F32)
    ]

    def order_call(*operands):
        return call(
            order_kernel, shape(boxes, total, points), [HBM, ANY], VMEM, whole, 0, 2 * moved, 8
        )(*operands)

    def target_call(chunk, *operands):
        kernel = functools.partial(target_kernel, chunk)
        return call(
            kernel, (shape(boxes, vectors, points), pair_shape), [VMEM] * 3 + [ANY],
            (VMEM, VMEM), [], 2 * flops, 4 * moved, 8,
        )(*operands)

    done_shape = shape(8, LANES, dtype=F32)

    def residual_call(chunk, *operands):
        return call(
            functools.partial(residual_kernel, chunk), (full_shape, done_shape),
            [VMEM, ANY] + [HBM] * (len(operands) - 2), (HBM, VMEM), [held, sems, wide],
            0, 2 * moved, 8, {2: 0} if len(operands) > 2 else None,
        )(*operands)

    def gradient_call(chunk, *operands):
        return call(
            functools.partial(gradient_kernel, chunk), (full_shape, done_shape),
            [VMEM] * 3 + [ANY] + [HBM] * (len(operands) - 4), (HBM, VMEM),
            [held, pltpu.SemaphoreType.DMA((PARTS,)), wide],
            flops, 2 * moved, 8, {4: 0} if len(operands) > 4 else None,
        )(*operands)

    def cross_call(level, *operands):
        kernel = functools.partial(cross_kernel, level, src_bits, lane_boxes)
        specs = [VMEM] * 3 + [ANY] * (len(operands) - 3)
        return call(kernel, forward_shape, specs, VMEM, [], flops, moved, 4)(*operands)

    def adjoint_call(level, *operands):
        kernel = functools.partial(adjoint_cross_kernel, level, src_bits)
        specs = [VMEM] * 3 + [ANY] * (len(operands) - 3)
        return call(
            kernel, (kept_shape, pair_shape), specs, (VMEM, VMEM), [], flops, moved, 4
        )(*operands)

    def local_forward_call(*operands):
        kernel = functools.partial(local_forward_kernel, top, src_bits, lane_boxes)
        scratch = [pltpu.VMEM((2, groups, rank, LANES), BF)]
        return call(
            kernel, forward_shape, [VMEM] * 3 + [ANY], VMEM, scratch, 7 * flops, 7 * moved, 8
        )(*operands)

    def local_adjoint_call(*operands):
        kernel = functools.partial(local_adjoint_kernel, top, src_bits)
        scratch = [pltpu.VMEM((2, pairs, vectors, LANES), BF)]
        return call(
            kernel, (kept_shape, pair_shape), [VMEM] * 2 + [ANY], (VMEM, VMEM), scratch,
            7 * flops, 7 * moved, 8,
        )(*operands)

    top = device_bits - 1
    every = range(CHUNKS)
    coeffs, kept, sent = [None] * CHUNKS, [None] * CHUNKS, [None] * CHUNKS
    coeffs = list(leaf_call(samples, leaf))
    token = coeffs[0]
    by_box = [None] * CHUNKS
    residual, gradient = (), ()
    first_back = top + 1 + 2 * GAP
    stages = first_back + top
    for step in range(stages + 1 + LAG * (CHUNKS - 1)):
        for c in reversed(every) if step in (first_back, first_back + 1) else every:
            stage = step - LAG * c
            if 0 <= stage < top:
                level = stage
                maps = levels[level:level + 1] if level < EARLY else levels
                coeffs[c] = token = cross_call(
                    level, coeffs[c], exchange(coeffs[c], level), maps, token
                )
            elif stage == top:
                coeffs[c] = token = local_forward_call(
                    coeffs[c], exchange(coeffs[c], top), levels, token
                )
            elif stage == top + GAP:
                by_box[c], sent[c] = target_call(c, reversal(coeffs[c]), final, wanted, token)
                token = sent[c]
            elif stage == top + 2 * GAP:
                kept[c], sent[c] = local_adjoint_call(reversal(sent[c]), levels, token)
                token = sent[c]
            elif first_back <= stage < stages:
                level = top - 1 - (stage - first_back)
                kept[c], sent[c] = adjoint_call(
                    level, kept[c], exchange(sent[c], level + 1), levels, token
                )
                token = sent[c]
            elif stage == stages:
                *gradient, token = gradient_call(
                    c, kept[c], exchange(sent[c], 0), leaf, token, *gradient
                )
            if (stage, c) == (2, CHUNKS - 1):
                wanted = token = order_call(wanted, token)
            if (stage, c) in ((top + GAP, CHUNKS - 1), (top + 2 * GAP, 0)):
                part = 0 if c else 1
                *residual, token = residual_call(part, by_box[part], token, *residual)
    residual, gradient = residual[0], gradient[0]
    return (
        residual.reshape(total, 1, 1, boxes, points),
        gradient.reshape(total, boxes, 1, 1, points),
    )


def solution(mesh):
    placed = (
        P(None, None, "hi", "src", None),
        P(None, "hi", "src", None, None),
        P(None, "hi", "src", None, None),
        P(None, None, "hi", "src", None, None),
        P("hi", "src", None, None, None),
    )
    return jax.shard_map(
        body,
        mesh=mesh,
        in_specs=placed,
        out_specs=(P(None, "hi", "src", None, None), P(None, None, "hi", "src", None)),
        check_vma=False,
    )
```
